512 devices in a mesh: row: 128 (over z, x, core), col: 4 (over y).
Axes of the slice: x: 4, y: 4, z: 16, core: 2. Of those that a mesh axis runs over, the one named last changes fastest.
Arguments:
- features: bfloat16 [256, 65536], P('col', 'row'), may hold values from -6 to 6
- send_pieces: int32 [128, 128], P('row'), may hold values from 0 to 7
- remote_target: int32 [128, 128], P('row'), may hold values from 0 to 3
- remote_count: int32 [128], P('row'), may hold values from 85 to 128, as said below
- local_values: bfloat16 [512, 128, 128], P('row'), may hold values from -0.29882812 to 0.29882812
- remote_values: bfloat16 [16384, 64, 128], P('row'), may hold values from -0.23925781 to 0.23925781
- hub_rows: int32 [128, 2], P('row'), may hold values from 0 to 511, as said below
- hub_adjacency: bfloat16 [256, 65536], P(None, 'row'), may hold values from -0.08984375 to 0.08984375
- weight: bfloat16 [256, 256], replicated, may hold values from -0.375 to 0.375
- cotangent: bfloat16 [256, 65536], P('col', 'row'), may hold values from -6 to 6
Outputs:
- output: bfloat16 [256, 65536], P('col', 'row')
- grad_input: bfloat16 [256, 65536], P('col', 'row')
- weight_grad: float32 [256, 256], P('col')
The draws below stay inside these ranges and needn't reach their ends.
Inputs may be any that keep to these rules, and one draw needn't show every extreme that they name: Peers from remote_count on contribute padding tiles; some device has all 128 peers live. `hub_rows`: A device's hubs are distinct local nodes.
All inputs are finite; a program needn't handle non-finite values.
Results may differ from the reference program's by a relative error of at most 0.0066.
Values may be sent and summed in bfloat16 or wider, within the bound.
No kernel may reach another device: no remote copies, remote signals or barrier semaphores. Data moves between devices by JAX's collectives and lax.ppermute only.
A program may use at most 64 MiB of HBM per device.

```python
import jax
import jax.numpy as jnp
from jax import lax

F = 256
B = 128
ROWS_DEV = 512
HUBS_DEV = 2
S = 64
NB = 4
H = 256
NODES = 65536
N_ROW = 128


def draw_remote_count(key, part):
    counts = jax.random.randint(jax.random.fold_in(key, 21), (N_ROW,), 2 * N_ROW // 3, N_ROW + 1)
    chosen = jax.random.randint(jax.random.fold_in(key, 22), (), 0, N_ROW)
    return jnp.where(jnp.arange(N_ROW) == chosen, N_ROW, counts).astype(jnp.int32)


def draw_hub_rows(key, part):
    stride = ROWS_DEV // HUBS_DEV
    offsets = jax.random.randint(jax.random.fold_in(key, 31), (N_ROW, HUBS_DEV), 0, stride)
    spread = jnp.arange(HUBS_DEV, dtype=jnp.int32)[None, :] * stride + offsets
    chosen = jax.random.randint(jax.random.fold_in(key, 32), (), 0, N_ROW)
    column = jnp.arange(HUBS_DEV, dtype=jnp.int32)[None, :]
    is_chosen = jnp.arange(N_ROW, dtype=jnp.int32)[:, None] == chosen
    spread = jnp.where(is_chosen & (column == HUBS_DEV - 1), ROWS_DEV - 1, spread)
    spread = jnp.where(is_chosen & (column == 0), 0, spread)
    return spread.astype(jnp.int32)


def set_ends(drawn, key, low, top_value):
    longest = drawn.shape.index(max(drawn.shape))
    spots = []
    for shift in (0, 1):
        where = [jax.random.randint(jax.random.fold_in(key, axis), (), 0, length) for axis, length in enumerate(drawn.shape)]
        where[longest] = (where[longest] + shift) % drawn.shape[longest]
        spots.append(tuple(where))
    return drawn.at[spots[0]].set(low).at[spots[1]].set(top_value)


def shard_levels(stream_key, extent, shards, least, high):
    level = 1.0
    for dim, shards_of in shards:
        steps = jax.random.uniform(jax.random.fold_in(jax.random.fold_in(stream_key, 6), dim), (shards_of,), jnp.float32, least / len(shards), high / len(shards))
        level = level * jnp.repeat(jnp.exp(steps), extent[dim] // shards_of).reshape((-1,) + (1,) * (len(extent) - 1 - dim))
    return level


def normal_values(stream_key, dims, deviation, bound, split=(), kind=jnp.bfloat16):
    result = jax.random.normal(stream_key, dims, jnp.float32) * deviation
    if len(split) > 0:
        result = shard_levels(stream_key, dims, split, -0.22, 0.18) * result
    return jnp.clip(result, min=-bound, max=bound).astype(kind)


def setup_inputs(seed: int = 0) -> dict:
    arg_keys = jax.random.split(jax.random.key(seed), 11)
    features = normal_values(arg_keys[0], (F, NODES), 1.0, 6.0, ((0, 4), (1, 128)))
    send_pieces = set_ends(jax.random.randint(arg_keys[1], (N_ROW, N_ROW), 0, 2 * NB), jax.random.fold_in(arg_keys[1], 1), 0, (2 * NB) - 1).astype(jnp.int32)
    remote_target = set_ends(jax.random.randint(arg_keys[2], (N_ROW, N_ROW), 0, NB), jax.random.fold_in(arg_keys[2], 1), 0, NB - 1).astype(jnp.int32)
    remote_count = draw_remote_count(jax.random.fold_in(arg_keys[10], 71), 0)
    local_values = normal_values(arg_keys[4], (NODES // B, B, B), 0.05, 0.29882812, ((0, 128),))
    remote_values = normal_values(arg_keys[5], (N_ROW * N_ROW, S, B), 0.04, 0.23925781, ((0, 128),))
    hub_rows = draw_hub_rows(jax.random.fold_in(arg_keys[10], 71), 0)
    hub_adjacency = normal_values(arg_keys[7], (H, NODES), 0.015, 0.08984375, ((1, 128),))
    weight = normal_values(arg_keys[8], (F, F), F ** -0.5, 0.375)
    cotangent = normal_values(arg_keys[9], (F, NODES), 1.0, 6.0, ((0, 4), (1, 128)))
    return dict(features=features, send_pieces=send_pieces, remote_target=remote_target, remote_count=remote_count, local_values=local_values, remote_values=remote_values, hub_rows=hub_rows, hub_adjacency=hub_adjacency, weight=weight, cotangent=cotangent)


def gelu_value(values):
    return jax.nn.gelu(values, approximate=True)

def product(left, right):
    return jnp.dot(left.astype(jnp.float32), right.astype(jnp.float32), precision=lax.Precision.HIGHEST)

def reference(features, send_pieces, remote_target, remote_count, local_values, remote_values, hub_rows, hub_adjacency, weight, cotangent):
    nodes = features.shape[1]
    block_count = ROWS_DEV // B
    piece_count = ROWS_DEV // S
    peer_ids = jnp.arange(N_ROW, dtype=jnp.int32)
    device_ids = peer_ids[:, None]
    live_mask = peer_ids[None, :] < remote_count[:, None]
    remote_live = remote_values.reshape(N_ROW, N_ROW, S, B) * live_mask[:, :, None, None].astype(remote_values.dtype)
    local_tiles = local_values.reshape(N_ROW, block_count, B, B)
    block_feats = features.reshape(F, N_ROW, block_count, B)
    piece_feats = features.reshape(F, N_ROW, piece_count, S)

    def forward_device(device):
        local_part = jnp.einsum('fbs,bsd->fbd', block_feats[:, device].astype(jnp.float32), local_tiles[device].astype(jnp.float32), precision=lax.Precision.HIGHEST)
        incoming = piece_feats[:, peer_ids, send_pieces[:, device]].astype(jnp.float32)
        products = jnp.einsum('fqs,qsd->fqd', incoming, remote_live[device].astype(jnp.float32), precision=lax.Precision.HIGHEST)
        onehot = (remote_target[device][:, None] == jnp.arange(block_count, dtype=jnp.int32)[None, :]).astype(jnp.float32)
        return local_part + jnp.einsum('fqd,qb->fbd', products, onehot, precision=lax.Precision.HIGHEST)
    per_device = lax.map(forward_device, peer_ids)
    tile_part = jnp.transpose(per_device, (1, 0, 2, 3)).reshape(F, nodes)
    hub_index = (device_ids * ROWS_DEV + hub_rows).reshape(-1).astype(jnp.int32)
    hub_feats = features[:, hub_index]
    hub_part = product(hub_feats, hub_adjacency)
    aggregate = (tile_part + hub_part).astype(jnp.bfloat16)
    pre_act = product(weight.T, aggregate)
    output = gelu_value(pre_act).astype(jnp.bfloat16)
    grad_pre = jax.vjp(gelu_value, pre_act)[1](cotangent.astype(jnp.float32))[0].astype(jnp.bfloat16)
    weight_grad = product(aggregate, grad_pre.T)
    grad_agg = product(weight, grad_pre).astype(jnp.bfloat16)
    grad_blocks = grad_agg.reshape(F, N_ROW, block_count, B)

    def local_device(device):
        return jnp.einsum('fbd,bsd->fbs', grad_blocks[:, device].astype(jnp.float32), local_tiles[device].astype(jnp.float32), precision=lax.Precision.HIGHEST)
    local_grad = jnp.transpose(lax.map(local_device, peer_ids), (1, 0, 2, 3)).reshape(F, N_ROW, piece_count, S)

    def backward_device(running, device):
        picked = grad_blocks[:, device, remote_target[device]].astype(jnp.float32)
        contrib = jnp.einsum('fqd,qsd->fqs', picked, remote_live[device].astype(jnp.float32), precision=lax.Precision.HIGHEST)
        return (running.at[:, peer_ids, send_pieces[:, device]].add(contrib), None)
    running = lax.scan(backward_device, local_grad, peer_ids)[0]
    hub_grad = product(grad_agg, hub_adjacency.T)
    grad_input = running.reshape(F, nodes).at[:, hub_index].add(hub_grad)
    return (output, grad_input.astype(jnp.bfloat16), weight_grad)
```

```python
import jax
import jax.numpy as jnp
from jax import lax
from jax.experimental import pallas as pl
from jax.experimental.pallas import tpu as pltpu
from jax.sharding import Mesh
from jax.sharding import PartitionSpec as P

BF = jnp.bfloat16
F32 = jnp.float32

FAR = 8
NEAR = 16
COLS = 4
PEERS = FAR * NEAR
FEAT = 64
HALF = FEAT // 2
ROWS = 512
BLK = 128
BLOCKS = ROWS // BLK
PIECE = 64
PIECES = ROWS // PIECE
DENSE = PIECES * HALF
OUT_ROWS = DENSE + 16
NEAR_ROWS = FAR * HALF + 16
BACK_ROWS = NEAR_ROWS + 16
VMEM_BYTES = 24 * 1024 * 1024

NT = (((1,), (1,)), ((), ()))
TN = (((0,), (0,)), ((), ()))
NN = (((1,), (0,)), ((), ()))


def dot(left, right, dims=NN):
    return lax.dot_general(left, right, dims, preferred_element_type=F32)


def vmem():
    return pl.BlockSpec(memory_space=pltpu.VMEM)


def smem():
    return pl.BlockSpec(memory_space=pltpu.SMEM)


def call(body, ins, outs, scratch=(), flops=1_000_000, size=1_000_000):
    return pl.pallas_call(
        body,
        in_specs=ins,
        out_specs=[vmem() for _ in outs],
        out_shape=[jax.ShapeDtypeStruct(s, t) for s, t in outs],
        scratch_shapes=list(scratch),
        compiler_params=pltpu.CompilerParams(vmem_limit_bytes=VMEM_BYTES),
        cost_estimate=pl.CostEstimate(flops=flops, bytes_accessed=size, transcendentals=0),
    )


def pack_body(hubs, feats, wanted, out):
    for k in range(PIECES):
        low = feats[:HALF, k * PIECE : (k + 1) * PIECE]
        high = feats[HALF:, k * PIECE : (k + 1) * PIECE]
        out[k * HALF : (k + 1) * HALF, :] = jnp.concatenate([low, high], axis=1)
    node = lax.broadcasted_iota(jnp.int32, (8, ROWS), 1)
    which = lax.broadcasted_iota(jnp.int32, (8, ROWS), 0)
    hub = jnp.where(which == 0, hubs[0, 0], hubs[0, 1])
    pick = ((node == hub) & (which < 2)).astype(BF)
    rows = dot(pick, feats[...], NT)
    hub_row = jnp.concatenate([rows[0:1], rows[1:2]], axis=1)
    place = lax.broadcasted_iota(jnp.int32, (16, 128), 0)
    extra = jnp.where(
        place == 0,
        jnp.broadcast_to(wanted[...].astype(F32), (16, 128)),
        jnp.where(place == 1, jnp.broadcast_to(hub_row, (16, 128)), 0.0),
    )
    out[DENSE:, :] = extra.astype(BF)


def pick_body(piece, gathered, out):
    place = lax.broadcasted_iota(jnp.int32, (16, 128), 0)
    extra = jnp.zeros((16, 128), F32)
    for s in range(FAR):
        tail = gathered[s, DENSE:, :].astype(F32)
        extra = jnp.where(place == s, jnp.broadcast_to(tail[1:2], (16, 128)), extra)
    extra = extra.astype(BF)

    def step(n, carry):
        for s in range(FAR):
            start = pl.multiple_of(piece[s, n] * HALF, HALF)
            out[n, s * HALF : (s + 1) * HALF, :] = gathered[s, pl.ds(start, HALF), :]
        out[n, FAR * HALF :, :] = extra
        return carry

    lax.fori_loop(0, NEAR, step, 0)


def twice(tile):
    zero = jnp.zeros_like(tile)
    return jnp.concatenate(
        [jnp.concatenate([tile, zero], axis=1), jnp.concatenate([zero, tile], axis=1)], axis=0
    )


def forward_body(target, came, remote, feats, local, adj, cot, out, total):
    total[...] = jnp.zeros_like(total)

    def step(s, carry):
        start = pl.multiple_of(s * HALF, HALF)
        for first in range(0, NEAR, 8):
            parts = []
            for n in range(first, first + 8):
                parts.append(dot(came[n, pl.ds(start, HALF), :], twice(remote[s * NEAR + n])))
            for n in range(first, first + 8):
                total[target[s * NEAR + n]] += parts[n - first]
        return carry

    lax.fori_loop(0, FAR, step, 0)
    hub_rows = jnp.concatenate([came[n, FAR * HALF :, :][:8] for n in range(NEAR)], axis=0)
    hub = (
        dot(hub_rows, adj[: PEERS, :], TN)[:FEAT] + dot(hub_rows, adj[PEERS:, :], TN)[FEAT:]
    )
    for b in range(BLOCKS):
        cols = slice(b * BLK, (b + 1) * BLK)
        own = dot(feats[:, cols], local[b])
        tiles = jnp.concatenate([total[b, :, :BLK], total[b, :, BLK:]], axis=0)
        value = (own + tiles + hub[:, cols]).astype(BF)
        for c in range(COLS):
            out[c, :FEAT, cols] = value
    for c in range(COLS):
        out[c, FEAT:, :] = cot[...]


def middle_body(
    col, target, came, weight, remote, local, adj, output, back, own_grad, agg, grad, pick
):
    for c in range(COLS):
        agg[c * FEAT : (c + 1) * FEAT, :] = came[c, :FEAT, :]
    scale = 0.7978845608028654
    mine = pl.multiple_of(col[0] * FEAT, FEAT)
    for c in range(COLS):
        pre = dot(weight[:, c * FEAT : (c + 1) * FEAT], agg[...], TN)
        square = pre * pre
        bend = jnp.tanh(scale * (pre + 0.044715 * (square * pre)))
        half = 0.5 * (1.0 + bend)
        slope = half + 0.5 * pre * (1.0 - bend * bend) * (
            scale * (1.0 + 3.0 * 0.044715 * square)
        )
        grad[c * FEAT : (c + 1) * FEAT, :] = (came[c, FEAT:, :].astype(F32) * slope).astype(BF)

        @pl.when(col[0] == c)
        def _():
            output[...] = (pre * half).astype(BF)

    grad_agg = dot(weight[pl.ds(mine, FEAT), :], grad[...]).astype(BF)
    weight_grad = dot(agg[pl.ds(mine, FEAT), :], grad[...], NT)
    for b in range(BLOCKS):
        cols = slice(b * BLK, (b + 1) * BLK)
        pick[b] = jnp.concatenate([grad_agg[:HALF, cols], grad_agg[HALF:, cols]], axis=1)
        own_grad[:, cols] = dot(grad_agg[:, cols], local[b], NT)
    pick[BLOCKS] = jnp.zeros((HALF, 2 * BLK), BF)
    hub = dot(adj[...], grad_agg, NT)
    hub = jnp.concatenate([hub[:PEERS], hub[PEERS:]], axis=1)
    zero = jnp.zeros((8, 128), F32)
    for n in range(NEAR):
        back[n, FAR * HALF : NEAR_ROWS, :] = jnp.concatenate(
            [hub[n * 8 : (n + 1) * 8], zero], axis=0
        ).astype(BF)
        i, j = n // 2, n % 2
        tile = weight_grad[i * 8 : (i + 1) * 8, j * 128 : (j + 1) * 128]
        high = tile.astype(BF).astype(F32)
        back[n, NEAR_ROWS:, :] = jnp.concatenate([high, tile - high], axis=0).astype(BF)

    def step(s, carry):
        start = pl.multiple_of(s * HALF, HALF)
        for n in range(NEAR):
            q = s * NEAR + n
            part = dot(pick[target[q]], twice(remote[q]), NT)
            back[n, pl.ds(start, HALF), :] = part.astype(BF)
        return carry

    lax.fori_loop(0, FAR, step, 0)


def gather_body(piece, came, out, total):
    extra = jnp.zeros((16, 128), F32)
    grads = jnp.zeros((16, 128), F32)
    for n in range(NEAR):
        extra += came[n, FAR * HALF : NEAR_ROWS, :].astype(F32)
        grads += came[n, NEAR_ROWS:, :].astype(F32)
    chunk = grads[:8] + grads[8:]
    high = chunk.astype(BF).astype(F32)
    chunk = jnp.concatenate([high, chunk - high], axis=0).astype(BF)
    total[...] = jnp.zeros_like(total)

    def step(s, carry):
        start = pl.multiple_of(s * HALF, HALF)
        for n in range(NEAR):
            at = pl.multiple_of(piece[s, n] * HALF, HALF)
            total[s, pl.ds(at, HALF), :] += came[n, pl.ds(start, HALF), :].astype(F32)
        out[s, :DENSE, :] = total[s].astype(BF)
        return carry

    lax.fori_loop(0, FAR, step, 0)
    for s in range(FAR):
        out[s, DENSE:NEAR_ROWS, :] = jnp.broadcast_to(extra[s : s + 1], (16, 128)).astype(BF)
        out[s, NEAR_ROWS:, :] = chunk


def final_body(hubs, came, own_grad, out, chunk):
    total = came[0].astype(F32)
    for s in range(1, FAR):
        total += came[s].astype(F32)
    node = lax.broadcasted_iota(jnp.int32, (8, ROWS), 1)
    which = lax.broadcasted_iota(jnp.int32, (8, ROWS), 0)
    hub = jnp.where(which == 0, hubs[0, 0], hubs[0, 1])
    pick = ((node == hub) & (which < 2)).astype(F32)
    row = total[DENSE : DENSE + 8]
    place = lax.broadcasted_iota(jnp.int32, (8, FEAT), 0)
    values = jnp.where(place == 0, row[:, :FEAT], row[:, FEAT:])
    hub_grad = lax.dot_general(
        values, pick, TN, preferred_element_type=F32, precision=lax.Precision.HIGHEST
    )
    for k in range(0, PIECES, 2):
        cols = slice(k * PIECE, (k + 2) * PIECE)
        a, b = total[k * HALF : (k + 1) * HALF], total[(k + 1) * HALF : (k + 2) * HALF]
        low = jnp.concatenate([a[:, :PIECE], b[:, :PIECE]], axis=1)
        high = jnp.concatenate([a[:, PIECE:], b[:, PIECE:]], axis=1)
        tiles = jnp.concatenate([low, high], axis=0)
        out[:, cols] = (own_grad[:, cols] + tiles + hub_grad[:, cols]).astype(BF)
    grads = total[NEAR_ROWS : NEAR_ROWS + 8] + total[NEAR_ROWS + 8 :]
    for n in range(NEAR):
        chunk[n] = grads


def exchange(values, axis):
    return lax.all_to_all(values, axis, split_axis=0, concat_axis=0, tiled=True)


def shards(
    features,
    send_pieces,
    remote_target,
    remote_count,
    local_values,
    remote_values,
    hub_rows,
    hub_adjacency,
    weight,
    cotangent,
):
    far = lax.axis_index("far")
    col = lax.axis_index("col").astype(jnp.int32).reshape(1)
    target = jnp.where(
        jnp.arange(PEERS, dtype=jnp.int32) < remote_count[0], remote_target[0], BLOCKS
    )
    adj = (
        hub_adjacency.reshape(FAR, NEAR, 2, ROWS).transpose(2, 1, 0, 3).reshape(2 * PEERS, ROWS)
    )

    (packed,) = call(pack_body, [smem(), vmem(), vmem()], [((OUT_ROWS, 128), BF)])(
        hub_rows, features, send_pieces
    )
    gathered = lax.all_gather(packed, "far", axis=0, tiled=False)
    piece = lax.dynamic_slice(
        gathered[:, DENSE, :], (jnp.int32(0), far * NEAR), (FAR, NEAR)
    ).astype(jnp.int32)
    (picked,) = call(pick_body, [smem(), vmem()], [((NEAR, NEAR_ROWS, 128), BF)])(piece, gathered)
    came = exchange(picked, "near")
    (agg_cot,) = call(
        forward_body,
        [smem()] + [vmem()] * 6,
        [((COLS, 2 * FEAT, ROWS), BF)],
        [pltpu.VMEM((BLOCKS + 1, HALF, 2 * BLK), F32)],
    )(target, came, remote_values, features, local_values, adj, cotangent)
    full = exchange(agg_cot, "col")
    output, back, own_grad = call(
        middle_body,
        [smem(), smem()] + [vmem()] * 5,
        [((FEAT, ROWS), BF), ((NEAR, BACK_ROWS, 128), BF), ((FEAT, ROWS), F32)],
        [
            pltpu.VMEM((COLS * FEAT, ROWS), BF),
            pltpu.VMEM((COLS * FEAT, ROWS), BF),
            pltpu.VMEM((BLOCKS + 1, HALF, 2 * BLK), BF),
        ],
    )(col, target, full, weight, remote_values, local_values, adj)
    back = exchange(back, "near")
    (sums,) = call(
        gather_body,
        [smem(), vmem()],
        [((FAR, BACK_ROWS, 128), BF)],
        [pltpu.VMEM((FAR, DENSE, 128), F32)],
    )(piece, back)
    sums = exchange(sums, "far")
    grad_input, chunk = call(
        final_body,
        [smem(), vmem(), vmem()],
        [((FEAT, ROWS), BF), ((NEAR, 8, 128), F32)],
    )(hub_rows, sums, own_grad)
    tiles = exchange(chunk, "near")
    weight_grad = tiles.reshape(8, 2, 8, 128).transpose(0, 2, 1, 3).reshape(FEAT, 256)
    return (output, grad_input, weight_grad)


def solution(mesh):
    fine = Mesh(mesh.devices.reshape(FAR, NEAR, COLS), ("far", "near", "col"))
    row = ("far", "near")
    placed = (
        P("col", row),
        P(row, None),
        P(row, None),
        P(row),
        P(row, None, None),
        P(row, None, None),
        P(row, None),
        P(None, row),
        P(),
        P("col", row),
    )
    return jax.shard_map(
        shards,
        mesh=fine,
        in_specs=placed,
        out_specs=(P("col", row), P("col", row), P("col", None)),
        check_vma=False,
    )
```

```python
import jax
import jax.numpy as jnp
from jax import lax
from jax.experimental import pallas as pl
from jax.experimental.pallas import tpu as pltpu
from jax.sharding import Mesh
from jax.sharding import PartitionSpec as P

BF = jnp.bfloat16
F32 = jnp.float32

FAR = 8
NEAR = 16
COLS = 4
PEERS = FAR * NEAR
FEAT = 64
HALF = FEAT // 2
ROWS = 512
BLK = 128
BLOCKS = ROWS // BLK
PIECE = 64
PIECES = ROWS // PIECE
DENSE = PIECES * HALF
OUT_ROWS = DENSE + 16
NEAR_ROWS = FAR * HALF + 16
BACK_ROWS = NEAR_ROWS
VMEM_BYTES = 30 * 1024 * 1024
ORDER = (7, 0, 12, 3, 9, 14, 5, 10, 1, 15, 6, 2, 13, 8, 4, 11)
SLOT = tuple(ORDER.index(n) for n in range(NEAR))

NT = (((1,), (1,)), ((), ()))
TN = (((0,), (0,)), ((), ()))
NN = (((1,), (0,)), ((), ()))


def dot(left, right, dims=NN):
    return lax.dot_general(left, right, dims, preferred_element_type=F32)


def vmem():
    return pl.BlockSpec(memory_space=pltpu.VMEM)


def smem():
    return pl.BlockSpec(memory_space=pltpu.SMEM)


def away():
    return pl.BlockSpec(memory_space=pl.ANY)


def call(body, ins, outs, scratch=(), flops=1_000_000, size=1_000_000):
    return pl.pallas_call(
        body,
        in_specs=ins,
        out_specs=[spec for _, _, spec in outs],
        out_shape=[
            pltpu.HBM(shape, kind)
            if spec.memory_space is pl.ANY
            else jax.ShapeDtypeStruct(shape, kind)
            for shape, kind, spec in outs
        ],
        scratch_shapes=list(scratch),
        compiler_params=pltpu.CompilerParams(vmem_limit_bytes=VMEM_BYTES),
        cost_estimate=pl.CostEstimate(flops=flops, bytes_accessed=size, transcendentals=0),
    )


def start_all(pairs, sems):
    copies = [pltpu.make_async_copy(src, dst, sems.at[i]) for i, (src, dst) in enumerate(pairs)]
    for copy in copies:
        copy.start()
    return copies


def stay(value):
    return pltpu.with_memory_space_constraint(value, pltpu.HBM)


def part(ref, s):
    return ref.at[:, pl.ds(pl.multiple_of(s * HALF, HALF), HALF), :]


def tiles_of(ref, s):
    return ref.at[pl.ds(s * NEAR, NEAR)]


def pack_body(hubs, feats, wanted, out):
    for k in range(PIECES):
        low = feats[:HALF, k * PIECE : (k + 1) * PIECE]
        high = feats[HALF:, k * PIECE : (k + 1) * PIECE]
        out[k * HALF : (k + 1) * HALF, :] = jnp.concatenate([low, high], axis=1)
    node = lax.broadcasted_iota(jnp.int32, (8, ROWS), 1)
    which = lax.broadcasted_iota(jnp.int32, (8, ROWS), 0)
    hub = jnp.where(which == 0, hubs[0, 0], hubs[0, 1])
    pick = ((node == hub) & (which < 2)).astype(BF)
    rows = dot(pick, feats[...], NT)
    hub_row = jnp.concatenate([rows[0:1], rows[1:2]], axis=1)
    place = lax.broadcasted_iota(jnp.int32, (16, 128), 0)
    extra = jnp.where(
        place == 0,
        jnp.broadcast_to(wanted[...].astype(F32), (16, 128)),
        jnp.where(place == 1, jnp.broadcast_to(hub_row, (16, 128)), 0.0),
    )
    out[DENSE:, :] = extra.astype(BF)


def pick_body(piece, gathered, out, held, sems):
    place = lax.broadcasted_iota(jnp.int32, (16, 128), 0)
    extra = jnp.zeros((16, 128), F32)
    for s in range(FAR):
        tail = gathered[s, DENSE:, :].astype(F32)
        extra = jnp.where(place == s, jnp.broadcast_to(tail[1:2], (16, 128)), extra)
    extra = extra.astype(BF)
    copies = []
    for n in range(NEAR):
        for s in range(FAR):
            start = pl.multiple_of(piece[s, ORDER[n]] * HALF, HALF)
            held[n, s * HALF : (s + 1) * HALF, :] = gathered[s, pl.ds(start, HALF), :]
        held[n, FAR * HALF :, :] = extra
        copies.append(pltpu.make_async_copy(held.at[n], out.at[n], sems.at[n]))
        copies[-1].start()
    for copy in copies:
        copy.wait()


def twice(tile):
    zero = jnp.zeros_like(tile)
    return jnp.concatenate(
        [jnp.concatenate([tile, zero], axis=1), jnp.concatenate([zero, tile], axis=1)], axis=0
    )


def forward_body(
    target,
    came,
    remote_far,
    feats_far,
    local_far,
    adj_far,
    out,
    remote,
    feats,
    local,
    adj,
    own,
    value,
    total,
    sems,
    remote_sems,
    out_sems,
):
    pairs = [(feats_far, feats), (local_far, local)]
    first = start_all(pairs, sems)
    start_all([(tiles_of(remote_far, s), tiles_of(remote, s)) for s in range(FAR)], remote_sems)
    last = pltpu.make_async_copy(adj_far, adj, sems.at[2])
    last.start()
    total[...] = jnp.zeros_like(total)
    for copy in first:
        copy.wait()
    for b in range(BLOCKS):
        cols = slice(b * BLK, (b + 1) * BLK)
        own[:, cols] = dot(feats[:, cols], local[b])

    def step(s, carry):
        start = pl.multiple_of(s * HALF, HALF)
        pltpu.make_async_copy(
            tiles_of(remote_far, s), tiles_of(remote, s), remote_sems.at[s]
        ).wait()
        for first in range(0, NEAR, 8):
            parts = []
            for n in range(first, first + 8):
                parts.append(
                    dot(came[n, pl.ds(start, HALF), :], twice(remote[s * NEAR + ORDER[n]]))
                )
            for n in range(first, first + 8):
                total[target[s * NEAR + ORDER[n]]] += parts[n - first]
        return carry

    lax.fori_loop(0, FAR, step, 0)
    last.wait()
    hub_rows = jnp.concatenate([came[SLOT[n], FAR * HALF :, :][:8] for n in range(NEAR)], axis=0)
    hub = (
        dot(hub_rows, adj[: PEERS, :], TN)[:FEAT] + dot(hub_rows, adj[PEERS:, :], TN)[FEAT:]
    )
    for b in range(BLOCKS):
        cols = slice(b * BLK, (b + 1) * BLK)
        tiles = jnp.concatenate([total[b, :, :BLK], total[b, :, BLK:]], axis=0)
        value[:, cols] = (own[:, cols] + tiles + hub[:, cols]).astype(BF)
    for copy in start_all([(value, out.at[c]) for c in range(COLS)], out_sems):
        copy.wait()


def middle_body(
    col,
    target,
    agg,
    cot_far,
    weight_far,
    remote_far,
    local_far,
    adj_far,
    output,
    back,
    own_grad,
    cot,
    weight,
    remote,
    local,
    adj,
    grad,
    pick,
    held,
    sems,
    remote_sems,
    back_sems,
):
    pairs = [
        (weight_far, weight),
        (cot_far, cot),
        (local_far, local),
        (adj_far, adj),
    ]
    copies = start_all(pairs, sems)
    start_all([(tiles_of(remote_far, s), tiles_of(remote, s)) for s in range(FAR)], remote_sems)
    for copy in copies[:2]:
        copy.wait()
    scale = 0.7978845608028654
    mine = pl.multiple_of(col[0] * FEAT, FEAT)
    for c in range(COLS):
        pre = dot(weight[:, c * FEAT : (c + 1) * FEAT], agg[...], TN)
        square = pre * pre
        bend = jnp.tanh(scale * (pre + 0.044715 * (square * pre)))
        half = 0.5 * (1.0 + bend)
        slope = half + 0.5 * pre * (1.0 - bend * bend) * (
            scale * (1.0 + 3.0 * 0.044715 * square)
        )
        grad[c * FEAT : (c + 1) * FEAT, :] = (
            cot[c * FEAT : (c + 1) * FEAT, :].astype(F32) * slope
        ).astype(BF)

        @pl.when(col[0] == c)
        def _():
            output[...] = (pre * half).astype(BF)

    grad_agg = dot(weight[pl.ds(mine, FEAT), :], grad[...]).astype(BF)
    weight_grad = dot(agg[pl.ds(mine, FEAT), :], grad[...], NT)
    for copy in copies[2:]:
        copy.wait()
    for b in range(BLOCKS):
        cols = slice(b * BLK, (b + 1) * BLK)
        pick[b] = jnp.concatenate([grad_agg[:HALF, cols], grad_agg[HALF:, cols]], axis=1)
        own_grad[:, cols] = dot(grad_agg[:, cols], local[b], NT)
    pick[BLOCKS] = jnp.zeros((HALF, 2 * BLK), BF)
    hub = dot(adj[...], grad_agg, NT)
    hub = jnp.concatenate([hub[:PEERS], hub[PEERS:]], axis=1)
    for n in range(NEAR):
        m = ORDER[n]
        i, j = m // 2, m % 2
        tile = weight_grad[i * 8 : (i + 1) * 8, j * 128 : (j + 1) * 128]
        held[n, FAR * HALF :, :] = jnp.concatenate([hub[m * 8 : (m + 1) * 8], tile], axis=0).astype(BF)
    ends = slice(FAR * HALF, NEAR_ROWS)
    last = pltpu.make_async_copy(held.at[:, ends, :], back.at[:, ends, :], sems.at[4])
    last.start()

    def step(s, carry):
        start = pl.multiple_of(s * HALF, HALF)
        pltpu.make_async_copy(
            tiles_of(remote_far, s), tiles_of(remote, s), remote_sems.at[s]
        ).wait()
        for n in range(NEAR):
            q = s * NEAR + ORDER[n]
            tile = dot(pick[target[q]], twice(remote[q]), NT)
            held[n, pl.ds(start, HALF), :] = tile.astype(BF)
        pltpu.make_async_copy(part(held, s), part(back, s), back_sems.at[s]).start()
        return carry

    lax.fori_loop(0, FAR, step, 0)
    last.wait()
    for s in range(FAR):
        pltpu.make_async_copy(part(held, s), part(back, s), back_sems.at[s]).wait()


def gather_body(piece, came, out, held, total, out_sems):
    total[...] = jnp.zeros_like(total)
    extra = jnp.zeros((16, 128), F32)
    for n in range(NEAR):
        extra += came[n, FAR * HALF :, :].astype(F32)
    for s in range(FAR):
        hub = jnp.broadcast_to(extra[s : s + 1], (8, 128))
        held[s, DENSE:, :] = jnp.concatenate([hub, extra[8:]], axis=0).astype(BF)

    def step(s, carry):
        start = pl.multiple_of(s * HALF, HALF)
        for n in range(NEAR):
            at = pl.multiple_of(piece[s, ORDER[n]] * HALF, HALF)
            total[s, pl.ds(at, HALF), :] += came[n, pl.ds(start, HALF), :].astype(F32)
        held[s, :DENSE, :] = total[s].astype(BF)
        pltpu.make_async_copy(held.at[s], out.at[s], out_sems.at[s]).start()
        return carry

    lax.fori_loop(0, FAR, step, 0)
    for s in range(FAR):
        pltpu.make_async_copy(held.at[s], out.at[s], out_sems.at[s]).wait()


def chunk_body(came, chunk):
    tail = came[0, DENSE:, :].astype(F32)
    for s in range(1, FAR):
        tail += came[s, DENSE:, :].astype(F32)
    for n in range(NEAR):
        chunk[n] = tail[8:]


def final_body(hubs, came, own_grad, out):
    total = came[0].astype(F32)
    for s in range(1, FAR):
        total += came[s].astype(F32)
    node = lax.broadcasted_iota(jnp.int32, (8, ROWS), 1)
    which = lax.broadcasted_iota(jnp.int32, (8, ROWS), 0)
    hub = jnp.where(which == 0, hubs[0, 0], hubs[0, 1])
    pick = ((node == hub) & (which < 2)).astype(F32)
    row = total[DENSE : DENSE + 8]
    place = lax.broadcasted_iota(jnp.int32, (8, FEAT), 0)
    values = jnp.where(place == 0, row[:, :FEAT], row[:, FEAT:])
    hub_grad = lax.dot_general(
        values, pick, TN, preferred_element_type=F32, precision=lax.Precision.HIGHEST
    )
    for k in range(0, PIECES, 2):
        cols = slice(k * PIECE, (k + 2) * PIECE)
        a, b = total[k * HALF : (k + 1) * HALF], total[(k + 1) * HALF : (k + 2) * HALF]
        low = jnp.concatenate([a[:, :PIECE], b[:, :PIECE]], axis=1)
        high = jnp.concatenate([a[:, PIECE:], b[:, PIECE:]], axis=1)
        tiles = jnp.concatenate([low, high], axis=0)
        out[:, cols] = (own_grad[:, cols] + tiles + hub_grad[:, cols]).astype(BF)


def exchange(values, axis, order=None):
    return lax.all_to_all(
        values,
        axis,
        split_axis=0,
        concat_axis=0,
        tiled=True,
        axis_index_groups=None if order is None else [list(order)],
    )


def shards(
    features,
    send_pieces,
    remote_target,
    remote_count,
    local_values,
    remote_values,
    hub_rows,
    hub_adjacency,
    weight,
    cotangent,
):
    far = lax.axis_index("far")
    col = lax.axis_index("col").astype(jnp.int32).reshape(1)
    target = jnp.where(
        jnp.arange(PEERS, dtype=jnp.int32) < remote_count[0], remote_target[0], BLOCKS
    )
    adj = (
        hub_adjacency.reshape(FAR, NEAR, 2, ROWS).transpose(2, 1, 0, 3).reshape(2 * PEERS, ROWS)
    )
    (packed,) = call(pack_body, [smem(), vmem(), vmem()], [((OUT_ROWS, 128), BF, vmem())])(
        stay(hub_rows), stay(features), stay(send_pieces)
    )
    gathered = lax.all_gather(packed, "far", axis=0, tiled=False)
    piece = lax.dynamic_slice(
        gathered[:, DENSE, :], (jnp.int32(0), far * NEAR), (FAR, NEAR)
    ).astype(jnp.int32)
    near_all = (NEAR, NEAR_ROWS, 128)
    (picked,) = call(
        pick_body,
        [smem(), vmem()],
        [(near_all, BF, away())],
        [pltpu.VMEM(near_all, BF), pltpu.SemaphoreType.DMA((NEAR,))],
    )(piece, gathered)
    picked, cotangent = lax.optimization_barrier((picked, cotangent))
    came = exchange(picked, "near", ORDER)
    cot = lax.all_gather(cotangent, "col", axis=0, tiled=True)
    came, cot = lax.optimization_barrier((came, cot))
    (agg,) = call(
        forward_body,
        [smem(), vmem()] + [away()] * 4,
        [((COLS, FEAT, ROWS), BF, away())],
        [
            pltpu.VMEM((PEERS, PIECE, BLK), BF),
            pltpu.VMEM((FEAT, ROWS), BF),
            pltpu.VMEM((BLOCKS, BLK, BLK), BF),
            pltpu.VMEM((2 * PEERS, ROWS), BF),
            pltpu.VMEM((FEAT, ROWS), F32),
            pltpu.VMEM((FEAT, ROWS), BF),
            pltpu.VMEM((BLOCKS + 1, HALF, 2 * BLK), F32),
            pltpu.SemaphoreType.DMA((3,)),
            pltpu.SemaphoreType.DMA((FAR,)),
            pltpu.SemaphoreType.DMA((COLS,)),
        ],
    )(target, came, *map(stay, (remote_values, features, local_values, adj)))
    agg = exchange(agg, "col").reshape(COLS * FEAT, ROWS)
    wide = (COLS * FEAT, ROWS)
    output, back, own_grad = call(
        middle_body,
        [smem(), smem(), vmem()] + [away()] * 5,
        [((FEAT, ROWS), BF, vmem()), (near_all, BF, away()), ((FEAT, ROWS), F32, vmem())],
        [
            pltpu.VMEM(wide, BF),
            pltpu.VMEM((COLS * FEAT, COLS * FEAT), BF),
            pltpu.VMEM((PEERS, PIECE, BLK), BF),
            pltpu.VMEM((BLOCKS, BLK, BLK), BF),
            pltpu.VMEM((2 * PEERS, ROWS), BF),
            pltpu.VMEM(wide, BF),
            pltpu.VMEM((BLOCKS + 1, HALF, 2 * BLK), BF),
            pltpu.VMEM(near_all, BF),
            pltpu.SemaphoreType.DMA((5,)),
            pltpu.SemaphoreType.DMA((FAR,)),
            pltpu.SemaphoreType.DMA((FAR,)),
        ],
    )(col, target, agg, *map(stay, (cot, weight, remote_values, local_values, adj)))
    back = exchange(back, "near", ORDER)
    far_all = (FAR, BACK_ROWS, 128)
    (sums,) = call(
        gather_body,
        [smem(), vmem()],
        [(far_all, BF, away())],
        [
            pltpu.VMEM(far_all, BF),
            pltpu.VMEM((FAR, DENSE, 128), F32),
            pltpu.SemaphoreType.DMA((FAR,)),
        ],
    )(piece, back)
    sums = exchange(sums, "far")
    (chunk,) = call(chunk_body, [vmem()], [((NEAR, 8, 128), F32, vmem())])(sums)
    tiles = exchange(chunk, "near")
    (grad_input,) = call(
        final_body, [smem(), vmem(), vmem()], [((FEAT, ROWS), BF, vmem())]
    )(stay(hub_rows), sums, own_grad)
    weight_grad = tiles.reshape(8, 2, 8, 128).transpose(0, 2, 1, 3).reshape(FEAT, 256)
    return (output, grad_input, weight_grad)


def solution(mesh):
    fine = Mesh(mesh.devices.reshape(FAR, NEAR, COLS), ("far", "near", "col"))
    row = ("far", "near")
    placed = (
        P("col", row),
        P(row, None),
        P(row, None),
        P(row),
        P(row, None, None),
        P(row, None, None),
        P(row, None),
        P(None, row),
        P(),
        P("col", row),
    )
    return jax.shard_map(
        shards,
        mesh=fine,
        in_specs=placed,
        out_specs=(P("col", row), P("col", row), P("col", None)),
        check_vma=False,
    )
```

```python
import jax
import jax.numpy as jnp
from jax import lax
from jax.experimental import pallas as pl
from jax.experimental.pallas import tpu as pltpu
from jax.sharding import Mesh
from jax.sharding import PartitionSpec as P

BF = jnp.bfloat16
F32 = jnp.float32

FAR = 8
NEAR = 16
COLS = 4
PEERS = FAR * NEAR
FEAT = 64
HALF = FEAT // 2
ROWS = 512
BLK = 128
BLOCKS = ROWS // BLK
PIECE = 64
PIECES = ROWS // PIECE
DENSE = PIECES * HALF
OUT_ROWS = DENSE + 16
NEAR_ROWS = FAR * HALF + 16
BACK_ROWS = NEAR_ROWS
VMEM_BYTES = 30 * 1024 * 1024
ORDER = (7, 0, 12, 3, 9, 14, 5, 10, 1, 15, 6, 2, 13, 8, 4, 11)
SLOT = tuple(ORDER.index(n) for n in range(NEAR))

NT = (((1,), (1,)), ((), ()))
TN = (((0,), (0,)), ((), ()))
NN = (((1,), (0,)), ((), ()))


def dot(left, right, dims=NN):
    return lax.dot_general(left, right, dims, preferred_element_type=F32)


def vmem():
    return pl.BlockSpec(memory_space=pltpu.VMEM)


def smem():
    return pl.BlockSpec(memory_space=pltpu.SMEM)


def away():
    return pl.BlockSpec(memory_space=pl.ANY)


def call(body, ins, outs, scratch=(), flops=1_000_000, size=1_000_000):
    return pl.pallas_call(
        body,
        in_specs=ins,
        out_specs=[spec for _, _, spec in outs],
        out_shape=[
            pltpu.HBM(shape, kind)
            if spec.memory_space is pl.ANY
            else jax.ShapeDtypeStruct(shape, kind)
            for shape, kind, spec in outs
        ],
        scratch_shapes=list(scratch),
        compiler_params=pltpu.CompilerParams(vmem_limit_bytes=VMEM_BYTES),
        cost_estimate=pl.CostEstimate(flops=flops, bytes_accessed=size, transcendentals=0),
    )


def start_all(pairs, sems):
    copies = [pltpu.make_async_copy(src, dst, sems.at[i]) for i, (src, dst) in enumerate(pairs)]
    for copy in copies:
        copy.start()
    return copies


def stay(value):
    return pltpu.with_memory_space_constraint(value, pltpu.HBM)


def pack_body(hubs, feats, wanted, out):
    for k in range(PIECES):
        low = feats[:HALF, k * PIECE : (k + 1) * PIECE]
        high = feats[HALF:, k * PIECE : (k + 1) * PIECE]
        out[k * HALF : (k + 1) * HALF, :] = jnp.concatenate([low, high], axis=1)
    node = lax.broadcasted_iota(jnp.int32, (8, ROWS), 1)
    which = lax.broadcasted_iota(jnp.int32, (8, ROWS), 0)
    hub = jnp.where(which == 0, hubs[0, 0], hubs[0, 1])
    pick = ((node == hub) & (which < 2)).astype(BF)
    rows = dot(pick, feats[...], NT)
    hub_row = jnp.concatenate([rows[0:1], rows[1:2]], axis=1)
    place = lax.broadcasted_iota(jnp.int32, (16, 128), 0)
    extra = jnp.where(
        place == 0,
        jnp.broadcast_to(wanted[...].astype(F32), (16, 128)),
        jnp.where(place == 1, jnp.broadcast_to(hub_row, (16, 128)), 0.0),
    )
    out[DENSE:, :] = extra.astype(BF)


def pick_body(piece, gathered, out, held, sems):
    place = lax.broadcasted_iota(jnp.int32, (16, 128), 0)
    extra = jnp.zeros((16, 128), F32)
    for s in range(FAR):
        tail = gathered[s, DENSE:, :].astype(F32)
        extra = jnp.where(place == s, jnp.broadcast_to(tail[1:2], (16, 128)), extra)
    extra = extra.astype(BF)
    copies = []
    for n in range(NEAR):
        for s in range(FAR):
            start = pl.multiple_of(piece[s, ORDER[n]] * HALF, HALF)
            held[n, s * HALF : (s + 1) * HALF, :] = gathered[s, pl.ds(start, HALF), :]
        held[n, FAR * HALF :, :] = extra
        copies.append(pltpu.make_async_copy(held.at[n], out.at[n], sems.at[n]))
        copies[-1].start()
    for copy in copies:
        copy.wait()


def twice(tile):
    zero = jnp.zeros_like(tile)
    return jnp.concatenate(
        [jnp.concatenate([tile, zero], axis=1), jnp.concatenate([zero, tile], axis=1)], axis=0
    )


def forward_body(
    target,
    came,
    remote,
    feats_far,
    local_far,
    adj_far,
    out,
    feats,
    local,
    adj,
    value,
    total,
    sems,
    out_sems,
):
    copies = start_all([(feats_far, feats), (local_far, local), (adj_far, adj)], sems)
    total[...] = jnp.zeros_like(total)

    def step(s, carry):
        start = pl.multiple_of(s * HALF, HALF)
        for first in range(0, NEAR, 8):
            parts = []
            for n in range(first, first + 8):
                parts.append(
                    dot(came[n, pl.ds(start, HALF), :], twice(remote[s * NEAR + ORDER[n]]))
                )
            for n in range(first, first + 8):
                total[target[s * NEAR + ORDER[n]]] += parts[n - first]
        return carry

    lax.fori_loop(0, FAR, step, 0)
    for copy in copies:
        copy.wait()
    hub_rows = jnp.concatenate([came[SLOT[n], FAR * HALF :, :][:8] for n in range(NEAR)], axis=0)
    hub = (
        dot(hub_rows, adj[: PEERS, :], TN)[:FEAT] + dot(hub_rows, adj[PEERS:, :], TN)[FEAT:]
    )
    for b in range(BLOCKS):
        cols = slice(b * BLK, (b + 1) * BLK)
        tiles = jnp.concatenate([total[b, :, :BLK], total[b, :, BLK:]], axis=0)
        own = dot(feats[:, cols], local[b])
        value[:, cols] = (own + tiles + hub[:, cols]).astype(BF)
    for copy in start_all([(value, out.at[c]) for c in range(COLS)], out_sems):
        copy.wait()


def middle_body(
    col,
    target,
    agg,
    remote,
    weight_far,
    cot_far,
    local_far,
    adj_far,
    output,
    back,
    own_grad,
    weight,
    cot,
    local,
    adj,
    grad,
    pick,
    sems,
):
    pairs = [(weight_far, weight), (cot_far, cot), (local_far, local), (adj_far, adj)]
    copies = start_all(pairs, sems)
    copies[0].wait()
    scale = 0.7978845608028654
    mine = pl.multiple_of(col[0] * FEAT, FEAT)
    for c in range(COLS):
        pre = dot(weight[:, c * FEAT : (c + 1) * FEAT], agg[...], TN)
        square = pre * pre
        bend = jnp.tanh(scale * (pre + 0.044715 * (square * pre)))
        half = 0.5 * (1.0 + bend)
        slope = half + 0.5 * pre * (1.0 - bend * bend) * (
            scale * (1.0 + 3.0 * 0.044715 * square)
        )
        if c == 0:
            copies[1].wait()
        grad[c * FEAT : (c + 1) * FEAT, :] = (
            cot[c * FEAT : (c + 1) * FEAT, :].astype(F32) * slope
        ).astype(BF)

        @pl.when(col[0] == c)
        def _():
            output[...] = (pre * half).astype(BF)

    grad_agg = dot(weight[pl.ds(mine, FEAT), :], grad[...]).astype(BF)
    weight_grad = dot(agg[pl.ds(mine, FEAT), :], grad[...], NT)
    copies[2].wait()
    for b in range(BLOCKS):
        cols = slice(b * BLK, (b + 1) * BLK)
        pick[b] = grad_agg[:, cols]
        own_grad[:, cols] = dot(grad_agg[:, cols], local[b], NT)
    copies[3].wait()
    pick[BLOCKS] = jnp.zeros((FEAT, BLK), BF)
    hub = dot(adj[...], grad_agg, NT)
    hub = jnp.concatenate([hub[:PEERS], hub[PEERS:]], axis=1)
    for n in range(NEAR):
        m = ORDER[n]
        i, j = m // 2, m % 2
        tile = weight_grad[i * 8 : (i + 1) * 8, j * 128 : (j + 1) * 128]
        back[n, FAR * HALF :, :] = jnp.concatenate([hub[m * 8 : (m + 1) * 8], tile], axis=0).astype(BF)

    def step(s, carry):
        start = pl.multiple_of(s * HALF, HALF)
        for n in range(NEAR):
            q = s * NEAR + ORDER[n]
            tile = dot(pick[target[q]], remote[q], NT)
            tile = jnp.concatenate([tile[:HALF], tile[HALF:]], axis=1)
            back[n, pl.ds(start, HALF), :] = tile.astype(BF)
        return carry

    lax.fori_loop(0, FAR, step, 0)


def gather_body(piece, came, out, total):
    total[...] = jnp.zeros_like(total)
    extra = jnp.zeros((16, 128), F32)
    for n in range(NEAR):
        extra += came[n, FAR * HALF :, :].astype(F32)
    for s in range(FAR):
        hub = jnp.broadcast_to(extra[s : s + 1], (8, 128))
        out[s, DENSE:, :] = jnp.concatenate([hub, extra[8:]], axis=0).astype(BF)

    def step(s, carry):
        start = pl.multiple_of(s * HALF, HALF)
        for n in range(NEAR):
            at = pl.multiple_of(piece[s, ORDER[n]] * HALF, HALF)
            total[s, pl.ds(at, HALF), :] += came[n, pl.ds(start, HALF), :].astype(F32)
        out[s, :DENSE, :] = total[s].astype(BF)
        return carry

    lax.fori_loop(0, FAR, step, 0)


def chunk_body(came, chunk):
    tail = came[0, DENSE:, :].astype(F32)
    for s in range(1, FAR):
        tail += came[s, DENSE:, :].astype(F32)
    for n in range(NEAR):
        chunk[n] = tail[8:]


def final_body(hubs, came, own_grad, out):
    total = came[0].astype(F32)
    for s in range(1, FAR):
        total += came[s].astype(F32)
    node = lax.broadcasted_iota(jnp.int32, (8, ROWS), 1)
    which = lax.broadcasted_iota(jnp.int32, (8, ROWS), 0)
    hub = jnp.where(which == 0, hubs[0, 0], hubs[0, 1])
    pick = ((node == hub) & (which < 2)).astype(F32)
    row = total[DENSE : DENSE + 8]
    place = lax.broadcasted_iota(jnp.int32, (8, FEAT), 0)
    values = jnp.where(place == 0, row[:, :FEAT], row[:, FEAT:])
    hub_grad = lax.dot_general(
        values, pick, TN, preferred_element_type=F32, precision=lax.Precision.HIGHEST
    )
    for k in range(0, PIECES, 2):
        cols = slice(k * PIECE, (k + 2) * PIECE)
        a, b = total[k * HALF : (k + 1) * HALF], total[(k + 1) * HALF : (k + 2) * HALF]
        low = jnp.concatenate([a[:, :PIECE], b[:, :PIECE]], axis=1)
        high = jnp.concatenate([a[:, PIECE:], b[:, PIECE:]], axis=1)
        tiles = jnp.concatenate([low, high], axis=0)
        out[:, cols] = (own_grad[:, cols] + tiles + hub_grad[:, cols]).astype(BF)


def exchange(values, axis, order=None):
    return lax.all_to_all(
        values,
        axis,
        split_axis=0,
        concat_axis=0,
        tiled=True,
        axis_index_groups=None if order is None else [list(order)],
    )


def shards(
    features,
    send_pieces,
    remote_target,
    remote_count,
    local_values,
    remote_values,
    hub_rows,
    hub_adjacency,
    weight,
    cotangent,
):
    far = lax.axis_index("far")
    col = lax.axis_index("col").astype(jnp.int32).reshape(1)
    target = jnp.where(
        jnp.arange(PEERS, dtype=jnp.int32) < remote_count[0], remote_target[0], BLOCKS
    )
    adj = (
        hub_adjacency.reshape(FAR, NEAR, 2, ROWS).transpose(2, 1, 0, 3).reshape(2 * PEERS, ROWS)
    )
    (packed,) = call(pack_body, [smem(), vmem(), vmem()], [((OUT_ROWS, 128), BF, vmem())])(
        stay(hub_rows), stay(features), stay(send_pieces)
    )
    gathered = lax.all_gather(packed, "far", axis=0, tiled=False)
    piece = lax.dynamic_slice(
        gathered[:, DENSE, :], (jnp.int32(0), far * NEAR), (FAR, NEAR)
    ).astype(jnp.int32)
    near_all = (NEAR, NEAR_ROWS, 128)
    (picked,) = call(
        pick_body,
        [smem(), vmem()],
        [(near_all, BF, away())],
        [pltpu.VMEM(near_all, BF), pltpu.SemaphoreType.DMA((NEAR,))],
    )(piece, gathered)
    picked, cotangent = lax.optimization_barrier((picked, cotangent))
    came = exchange(picked, "near", ORDER)
    cot = lax.all_gather(cotangent, "col", axis=0, tiled=True)
    came, cot = lax.optimization_barrier((came, cot))
    small = [pltpu.VMEM((BLOCKS, BLK, BLK), BF), pltpu.VMEM((2 * PEERS, ROWS), BF)]
    (agg,) = call(
        forward_body,
        [smem(), vmem(), vmem()] + [away()] * 3,
        [((COLS, FEAT, ROWS), BF, away())],
        [pltpu.VMEM((FEAT, ROWS), BF)]
        + small
        + [
            pltpu.VMEM((FEAT, ROWS), BF),
            pltpu.VMEM((BLOCKS + 1, HALF, 2 * BLK), F32),
            pltpu.SemaphoreType.DMA((3,)),
            pltpu.SemaphoreType.DMA((COLS,)),
        ],
    )(target, came, remote_values, *map(stay, (features, local_values, adj)))
    wide = (COLS * FEAT, ROWS)
    agg = exchange(agg, "col").reshape(wide)
    output, back, own_grad = call(
        middle_body,
        [smem(), smem(), vmem(), vmem()] + [away()] * 4,
        [((FEAT, ROWS), BF, vmem()), (near_all, BF, vmem()), ((FEAT, ROWS), F32, vmem())],
        [pltpu.VMEM((COLS * FEAT, COLS * FEAT), BF), pltpu.VMEM(wide, BF)]
        + small
        + [
            pltpu.VMEM(wide, BF),
            pltpu.VMEM((BLOCKS + 1, FEAT, BLK), BF),
            pltpu.SemaphoreType.DMA((4,)),
        ],
    )(col, target, agg, remote_values, *map(stay, (weight, cot, local_values, adj)))
    back = exchange(back, "near", ORDER)
    far_all = (FAR, BACK_ROWS, 128)
    (sums,) = call(
        gather_body,
        [smem(), vmem()],
        [(far_all, BF, vmem())],
        [pltpu.VMEM((FAR, DENSE, 128), F32)],
    )(piece, back)
    sums = exchange(sums, "far")
    (chunk,) = call(chunk_body, [vmem()], [((NEAR, 8, 128), F32, vmem())])(sums)
    tiles = exchange(chunk, "near")
    (grad_input,) = call(
        final_body, [smem(), vmem(), vmem()], [((FEAT, ROWS), BF, vmem())]
    )(stay(hub_rows), sums, own_grad)
    weight_grad = tiles.reshape(8, 2, 8, 128).transpose(0, 2, 1, 3).reshape(FEAT, 256)
    return (output, grad_input, weight_grad)


def solution(mesh):
    fine = Mesh(mesh.devices.reshape(FAR, NEAR, COLS), ("far", "near", "col"))
    row = ("far", "near")
    placed = (
        P("col", row),
        P(row, None),
        P(row, None),
        P(row),
        P(row, None, None),
        P(row, None, None),
        P(row, None),
        P(None, row),
        P(),
        P("col", row),
    )
    return jax.shard_map(
        shards,
        mesh=fine,
        in_specs=placed,
        out_specs=(P("col", row), P("col", row), P("col", None)),
        check_vma=False,
    )
```

```python
import jax
import jax.numpy as jnp
from jax import lax
from jax.experimental import pallas as pl
from jax.experimental.pallas import tpu as pltpu
from jax.sharding import Mesh
from jax.sharding import PartitionSpec as P

BF = jnp.bfloat16
F32 = jnp.float32

FAR = 8
NEAR = 16
COLS = 4
PEERS = FAR * NEAR
FEAT = 64
HALF = FEAT // 2
ROWS = 512
BLK = 128
BLOCKS = ROWS // BLK
PIECE = 64
PIECES = ROWS // PIECE
DENSE = PIECES * HALF
OUT_ROWS = DENSE + 16
NEAR_ROWS = FAR * HALF + 16
BACK_ROWS = NEAR_ROWS
VMEM_BYTES = 30 * 1024 * 1024
ORDER = (7, 0, 12, 3, 9, 14, 5, 10, 1, 15, 6, 2, 13, 8, 4, 11)
SLOT = tuple(ORDER.index(n) for n in range(NEAR))

NT = (((1,), (1,)), ((), ()))
TN = (((0,), (0,)), ((), ()))
NN = (((1,), (0,)), ((), ()))


def dot(left, right, dims=NN):
    return lax.dot_general(left, right, dims, preferred_element_type=F32)


def vmem():
    return pl.BlockSpec(memory_space=pltpu.VMEM)


def smem():
    return pl.BlockSpec(memory_space=pltpu.SMEM)


def away():
    return pl.BlockSpec(memory_space=pl.ANY)


def call(body, ins, outs, scratch=(), flops=1_000_000, size=1_000_000):
    return pl.pallas_call(
        body,
        in_specs=ins,
        out_specs=[spec for _, _, spec in outs],
        out_shape=[
            pltpu.HBM(shape, kind)
            if spec.memory_space is pl.ANY
            else jax.ShapeDtypeStruct(shape, kind)
            for shape, kind, spec in outs
        ],
        scratch_shapes=list(scratch),
        compiler_params=pltpu.CompilerParams(vmem_limit_bytes=VMEM_BYTES),
        cost_estimate=pl.CostEstimate(flops=flops, bytes_accessed=size, transcendentals=0),
    )


def start_all(pairs, sems):
    copies = [pltpu.make_async_copy(src, dst, sems.at[i]) for i, (src, dst) in enumerate(pairs)]
    for copy in copies:
        copy.start()
    return copies


def stay(value):
    return pltpu.with_memory_space_constraint(value, pltpu.HBM)


def pack_body(hubs, feats, wanted, out):
    for k in range(PIECES):
        low = feats[:HALF, k * PIECE : (k + 1) * PIECE]
        high = feats[HALF:, k * PIECE : (k + 1) * PIECE]
        out[k * HALF : (k + 1) * HALF, :] = jnp.concatenate([low, high], axis=1)
    node = lax.broadcasted_iota(jnp.int32, (8, ROWS), 1)
    which = lax.broadcasted_iota(jnp.int32, (8, ROWS), 0)
    hub = jnp.where(which == 0, hubs[0, 0], hubs[0, 1])
    pick = ((node == hub) & (which < 2)).astype(BF)
    rows = dot(pick, feats[...], NT)
    hub_row = jnp.concatenate([rows[0:1], rows[1:2]], axis=1)
    place = lax.broadcasted_iota(jnp.int32, (16, 128), 0)
    extra = jnp.where(
        place == 0,
        jnp.broadcast_to(wanted[...].astype(F32), (16, 128)),
        jnp.where(place == 1, jnp.broadcast_to(hub_row, (16, 128)), 0.0),
    )
    out[DENSE:, :] = extra.astype(BF)


def pick_body(piece, gathered, out, held, sems):
    place = lax.broadcasted_iota(jnp.int32, (16, 128), 0)
    extra = jnp.zeros((16, 128), F32)
    for s in range(FAR):
        tail = gathered[s, DENSE:, :].astype(F32)
        extra = jnp.where(place == s, jnp.broadcast_to(tail[1:2], (16, 128)), extra)
    extra = extra.astype(BF)
    copies = []
    for n in range(NEAR):
        for s in range(FAR):
            start = pl.multiple_of(piece[s, ORDER[n]] * HALF, HALF)
            held[n, s * HALF : (s + 1) * HALF, :] = gathered[s, pl.ds(start, HALF), :]
        held[n, FAR * HALF :, :] = extra
        copies.append(pltpu.make_async_copy(held.at[n], out.at[n], sems.at[n]))
        copies[-1].start()
    for copy in copies:
        copy.wait()


def hub_places():
    hub = lax.broadcasted_iota(jnp.int32, (2 * PEERS, 2 * PEERS), 0)
    place = lax.broadcasted_iota(jnp.int32, (2 * PEERS, 2 * PEERS), 1)
    owner = ((place & 7) << 5) + (((place >> 3) & 15) << 1) + (place >> 7)
    return (hub == owner).astype(BF)


def twice(tile):
    zero = jnp.zeros_like(tile)
    return jnp.concatenate(
        [jnp.concatenate([tile, zero], axis=1), jnp.concatenate([zero, tile], axis=1)], axis=0
    )


def forward_body(
    target,
    came,
    remote,
    feats_far,
    local_far,
    adj_far,
    out,
    feats,
    local,
    adj,
    value,
    total,
    sems,
    out_sems,
):
    copies = start_all([(feats_far, feats), (local_far, local), (adj_far, adj)], sems)
    total[...] = jnp.zeros_like(total)

    def step(s, carry):
        start = pl.multiple_of(s * HALF, HALF)
        for first in range(0, NEAR, 8):
            parts = []
            for n in range(first, first + 8):
                parts.append(
                    dot(came[n, pl.ds(start, HALF), :], twice(remote[s * NEAR + ORDER[n]]))
                )
            for n in range(first, first + 8):
                total[target[s * NEAR + ORDER[n]]] += parts[n - first]
        return carry

    lax.fori_loop(0, FAR, step, 0)
    for copy in copies:
        copy.wait()
    rows = jnp.concatenate([came[SLOT[n], FAR * HALF :, :][:8] for n in range(NEAR)], axis=0)
    rows = jnp.concatenate([rows[:, :FEAT], rows[:, FEAT:]], axis=0)
    hubs = dot(hub_places(), rows).astype(BF)
    hub = dot(hubs, adj[...], TN)
    for b in range(BLOCKS):
        cols = slice(b * BLK, (b + 1) * BLK)
        tiles = jnp.concatenate([total[b, :, :BLK], total[b, :, BLK:]], axis=0)
        own = dot(feats[:, cols], local[b])
        value[:, cols] = (own + tiles + hub[:, cols]).astype(BF)
    for copy in start_all([(value, out.at[c]) for c in range(COLS)], out_sems):
        copy.wait()


def middle_body(
    col,
    target,
    agg,
    remote,
    weight_far,
    cot_far,
    local_far,
    adj_far,
    output,
    back,
    own_grad,
    weight,
    cot,
    local,
    adj,
    grad,
    pick,
    sems,
):
    pairs = [(weight_far, weight), (cot_far, cot), (local_far, local), (adj_far, adj)]
    copies = start_all(pairs, sems)
    copies[0].wait()
    scale = 0.7978845608028654
    mine = pl.multiple_of(col[0] * FEAT, FEAT)
    for c in range(COLS):
        pre = dot(weight[:, c * FEAT : (c + 1) * FEAT], agg[...], TN)
        square = pre * pre
        bend = jnp.tanh(scale * (pre + 0.044715 * (square * pre)))
        half = 0.5 * (1.0 + bend)
        slope = half + 0.5 * pre * (1.0 - bend * bend) * (
            scale * (1.0 + 3.0 * 0.044715 * square)
        )
        if c == 0:
            copies[1].wait()
        grad[c * FEAT : (c + 1) * FEAT, :] = (
            cot[c * FEAT : (c + 1) * FEAT, :].astype(F32) * slope
        ).astype(BF)

        @pl.when(col[0] == c)
        def _():
            output[...] = (pre * half).astype(BF)

    grad_agg = dot(weight[pl.ds(mine, FEAT), :], grad[...]).astype(BF)
    weight_grad = dot(agg[pl.ds(mine, FEAT), :], grad[...], NT)
    copies[2].wait()
    for b in range(BLOCKS):
        cols = slice(b * BLK, (b + 1) * BLK)
        pick[b] = grad_agg[:, cols]
        own_grad[:, cols] = dot(grad_agg[:, cols], local[b], NT)
    copies[3].wait()
    pick[BLOCKS] = jnp.zeros((FEAT, BLK), BF)
    hub = dot(adj[...], grad_agg, NT).astype(BF)
    hub = dot(hub_places(), hub, TN)
    hub = jnp.concatenate([hub[:PEERS], hub[PEERS:]], axis=1)
    for n in range(NEAR):
        m = ORDER[n]
        i, j = m // 2, m % 2
        tile = weight_grad[i * 8 : (i + 1) * 8, j * 128 : (j + 1) * 128]
        back[n, FAR * HALF :, :] = jnp.concatenate([hub[m * 8 : (m + 1) * 8], tile], axis=0).astype(BF)

    def step(s, carry):
        start = pl.multiple_of(s * HALF, HALF)
        for n in range(NEAR):
            q = s * NEAR + ORDER[n]
            tile = dot(pick[target[q]], remote[q], NT)
            tile = jnp.concatenate([tile[:HALF], tile[HALF:]], axis=1)
            back[n, pl.ds(start, HALF), :] = tile.astype(BF)
        return carry

    lax.fori_loop(0, FAR, step, 0)


def gather_body(piece, came, out, chunk, held, total, sems):
    total[...] = jnp.zeros_like(total)
    extra = jnp.zeros((16, 128), F32)
    for n in range(NEAR):
        extra += came[n, FAR * HALF :, :].astype(F32)
    chunk[...] = extra[8:]

    def step(s, carry):
        start = pl.multiple_of(s * HALF, HALF)
        for n in range(NEAR):
            at = pl.multiple_of(piece[s, ORDER[n]] * HALF, HALF)
            total[s, pl.ds(at, HALF), :] += came[n, pl.ds(start, HALF), :].astype(F32)
        return carry

    lax.fori_loop(0, FAR, step, 0)
    copies = []
    for s in range(FAR):
        held[s, :DENSE, :] = total[s].astype(BF)
        held[s, DENSE:, :] = jnp.broadcast_to(extra[s : s + 1], (16, 128)).astype(BF)
        copies.append(pltpu.make_async_copy(held.at[s], out.at[s], sems.at[s]))
        copies[-1].start()
    for copy in copies:
        copy.wait()


def add_body(parts, out):
    total = parts[0]
    for s in range(1, FAR):
        total += parts[s]
    out[...] = total


def final_body(hubs, came, own_grad, out):
    total = came[0].astype(F32)
    for s in range(1, FAR):
        total += came[s].astype(F32)
    node = lax.broadcasted_iota(jnp.int32, (8, ROWS), 1)
    which = lax.broadcasted_iota(jnp.int32, (8, ROWS), 0)
    hub = jnp.where(which == 0, hubs[0, 0], hubs[0, 1])
    pick = ((node == hub) & (which < 2)).astype(F32)
    row = total[DENSE : DENSE + 8]
    place = lax.broadcasted_iota(jnp.int32, (8, FEAT), 0)
    values = jnp.where(place == 0, row[:, :FEAT], row[:, FEAT:])
    hub_grad = lax.dot_general(
        values, pick, TN, preferred_element_type=F32, precision=lax.Precision.HIGHEST
    )
    for k in range(0, PIECES, 2):
        cols = slice(k * PIECE, (k + 2) * PIECE)
        a, b = total[k * HALF : (k + 1) * HALF], total[(k + 1) * HALF : (k + 2) * HALF]
        low = jnp.concatenate([a[:, :PIECE], b[:, :PIECE]], axis=1)
        high = jnp.concatenate([a[:, PIECE:], b[:, PIECE:]], axis=1)
        tiles = jnp.concatenate([low, high], axis=0)
        out[:, cols] = (own_grad[:, cols] + tiles + hub_grad[:, cols]).astype(BF)


def exchange(values, axis, order=None):
    return lax.all_to_all(
        values,
        axis,
        split_axis=0,
        concat_axis=0,
        tiled=True,
        axis_index_groups=None if order is None else [list(order)],
    )


def shards(
    features,
    send_pieces,
    remote_target,
    remote_count,
    local_values,
    remote_values,
    hub_rows,
    hub_adjacency,
    weight,
    cotangent,
):
    far = lax.axis_index("far")
    col = lax.axis_index("col").astype(jnp.int32).reshape(1)
    target = jnp.where(
        jnp.arange(PEERS, dtype=jnp.int32) < remote_count[0], remote_target[0], BLOCKS
    )
    (packed,) = call(pack_body, [smem(), vmem(), vmem()], [((OUT_ROWS, 128), BF, vmem())])(
        stay(hub_rows), stay(features), stay(send_pieces)
    )
    gathered = lax.all_gather(packed, "far", axis=0, tiled=False)
    piece = lax.dynamic_slice(
        gathered[:, DENSE, :], (jnp.int32(0), far * NEAR), (FAR, NEAR)
    ).astype(jnp.int32)
    near_all = (NEAR, NEAR_ROWS, 128)
    (picked,) = call(
        pick_body,
        [smem(), vmem()],
        [(near_all, BF, away())],
        [pltpu.VMEM(near_all, BF), pltpu.SemaphoreType.DMA((NEAR,))],
    )(piece, gathered)
    picked, cotangent = lax.optimization_barrier((picked, cotangent))
    came = exchange(picked, "near", ORDER)
    cot = lax.all_gather(cotangent, "col", axis=0, tiled=True)
    came, cot = lax.optimization_barrier((came, cot))
    small = [pltpu.VMEM((BLOCKS, BLK, BLK), BF), pltpu.VMEM((2 * PEERS, ROWS), BF)]
    (agg,) = call(
        forward_body,
        [smem(), vmem(), vmem()] + [away()] * 3,
        [((COLS, FEAT, ROWS), BF, away())],
        [pltpu.VMEM((FEAT, ROWS), BF)]
        + small
        + [
            pltpu.VMEM((FEAT, ROWS), BF),
            pltpu.VMEM((BLOCKS + 1, HALF, 2 * BLK), F32),
            pltpu.SemaphoreType.DMA((3,)),
            pltpu.SemaphoreType.DMA((COLS,)),
        ],
    )(target, came, remote_values, *map(stay, (features, local_values, hub_adjacency)))
    wide = (COLS * FEAT, ROWS)
    agg = exchange(agg, "col").reshape(wide)
    output, back, own_grad = call(
        middle_body,
        [smem(), smem(), vmem(), vmem()] + [away()] * 4,
        [((FEAT, ROWS), BF, vmem()), (near_all, BF, vmem()), ((FEAT, ROWS), F32, vmem())],
        [pltpu.VMEM((COLS * FEAT, COLS * FEAT), BF), pltpu.VMEM(wide, BF)]
        + small
        + [
            pltpu.VMEM(wide, BF),
            pltpu.VMEM((BLOCKS + 1, FEAT, BLK), BF),
            pltpu.SemaphoreType.DMA((4,)),
        ],
    )(col, target, agg, remote_values, *map(stay, (weight, cot, local_values, hub_adjacency)))
    back = exchange(back, "near", ORDER)
    far_all = (FAR, BACK_ROWS, 128)
    sums, chunk = call(
        gather_body,
        [smem(), vmem()],
        [(far_all, BF, away()), ((8, 128), F32, vmem())],
        [
            pltpu.VMEM(far_all, BF),
            pltpu.VMEM((FAR, DENSE, 128), F32),
            pltpu.SemaphoreType.DMA((FAR,)),
        ],
    )(piece, back)
    sums = exchange(sums, "far")
    parts = lax.all_gather(chunk, "far", axis=0, tiled=False)
    (chunk,) = call(add_body, [vmem()], [((8, 128), F32, vmem())])(parts)
    tiles = lax.all_gather(chunk, "near", axis=0, tiled=False)
    sums, tiles = lax.optimization_barrier((sums, tiles))
    (grad_input,) = call(
        final_body, [smem(), vmem(), vmem()], [((FEAT, ROWS), BF, vmem())]
    )(stay(hub_rows), sums, own_grad)
    weight_grad = tiles.reshape(8, 2, 8, 128).transpose(0, 2, 1, 3).reshape(FEAT, 256)
    return (output, grad_input, weight_grad)


def solution(mesh):
    fine = Mesh(mesh.devices.reshape(FAR, NEAR, COLS), ("far", "near", "col"))
    row = ("far", "near")
    placed = (
        P("col", row),
        P(row, None),
        P(row, None),
        P(row),
        P(row, None, None),
        P(row, None, None),
        P(row, None),
        P(None, row),
        P(),
        P("col", row),
    )
    return jax.shard_map(
        shards,
        mesh=fine,
        in_specs=placed,
        out_specs=(P("col", row), P("col", row), P("col", None)),
        check_vma=False,
    )
```

```python
import jax
import jax.numpy as jnp
from jax import lax
from jax.experimental import pallas as pl
from jax.experimental.pallas import tpu as pltpu
from jax.sharding import PartitionSpec as P

BF = jnp.bfloat16
F32 = jnp.float32

FAR = 8
NEAR = 16
COLS = 4
PEERS = FAR * NEAR
FEAT = 64
HALF = FEAT // 2
ROWS = 512
BLK = 128
BLOCKS = ROWS // BLK
PIECE = 64
PIECES = ROWS // PIECE
DENSE = PIECES * HALF
OUT_ROWS = DENSE + 16
NEAR_ROWS = FAR * HALF + 16
BACK_ROWS = NEAR_ROWS
VMEM_BYTES = 30 * 1024 * 1024
ORDER = (7, 0, 12, 3, 9, 14, 5, 10, 1, 15, 6, 2, 13, 8, 4, 11)
FAR_ORDERS = (
    (6, 2, 7, 0, 5, 3, 1, 4),
    (6, 1, 3, 0, 5, 4, 2, 7),
    (0, 7, 6, 2, 1, 5, 3, 4),
    (5, 6, 3, 2, 0, 7, 4, 1),
)
FAR_SLOTS = tuple(tuple(order.index(s) for s in range(FAR)) for order in FAR_ORDERS)
NEAR_IDS = tuple(tuple(f * NEAR + n for n in range(NEAR)) for f in range(FAR))
FAR_IDS = tuple(tuple(f * NEAR + n for f in range(FAR)) for n in range(NEAR))
NEAR_GROUPS = tuple(tuple(ids[n] for n in ORDER) for ids in NEAR_IDS)


def place_of(near):
    return 2 * (near // 8) + near % 2


FAR_GROUPS = tuple(
    tuple(FAR_IDS[n][f] for f in FAR_ORDERS[place_of(n)]) for n in range(NEAR)
)
SLOT = tuple(ORDER.index(n) for n in range(NEAR))

NT = (((1,), (1,)), ((), ()))
TN = (((0,), (0,)), ((), ()))
NN = (((1,), (0,)), ((), ()))


def dot(left, right, dims=NN):
    return lax.dot_general(left, right, dims, preferred_element_type=F32)


def vmem():
    return pl.BlockSpec(memory_space=pltpu.VMEM)


def smem():
    return pl.BlockSpec(memory_space=pltpu.SMEM)


def away():
    return pl.BlockSpec(memory_space=pl.ANY)


def call(body, ins, outs, scratch=(), flops=1_000_000, size=1_000_000):
    return pl.pallas_call(
        body,
        in_specs=ins,
        out_specs=[spec for _, _, spec in outs],
        out_shape=[
            pltpu.HBM(shape, kind)
            if spec.memory_space is pl.ANY
            else jax.ShapeDtypeStruct(shape, kind)
            for shape, kind, spec in outs
        ],
        scratch_shapes=list(scratch),
        compiler_params=pltpu.CompilerParams(vmem_limit_bytes=VMEM_BYTES),
        cost_estimate=pl.CostEstimate(flops=flops, bytes_accessed=size, transcendentals=0),
    )


def start_all(pairs, sems):
    copies = [pltpu.make_async_copy(src, dst, sems.at[i]) for i, (src, dst) in enumerate(pairs)]
    for copy in copies:
        copy.start()
    return copies


def stay(value):
    return pltpu.with_memory_space_constraint(value, pltpu.HBM)


def pack_body(hubs, feats, wanted, out):
    for k in range(PIECES):
        low = feats[:HALF, k * PIECE : (k + 1) * PIECE]
        high = feats[HALF:, k * PIECE : (k + 1) * PIECE]
        out[k * HALF : (k + 1) * HALF, :] = jnp.concatenate([low, high], axis=1)
    node = lax.broadcasted_iota(jnp.int32, (8, ROWS), 1)
    which = lax.broadcasted_iota(jnp.int32, (8, ROWS), 0)
    hub = jnp.where(which == 0, hubs[0, 0], hubs[0, 1])
    pick = ((node == hub) & (which < 2)).astype(BF)
    rows = dot(pick, feats[...], NT)
    hub_row = jnp.concatenate([rows[0:1], rows[1:2]], axis=1)
    place = lax.broadcasted_iota(jnp.int32, (16, 128), 0)
    extra = jnp.where(
        place == 0,
        jnp.broadcast_to(wanted[...].astype(F32), (16, 128)),
        jnp.where(place == 1, jnp.broadcast_to(hub_row, (16, 128)), 0.0),
    )
    out[DENSE:, :] = extra.astype(BF)


def pick_body(piece, gathered, out, held, sems):
    place = lax.broadcasted_iota(jnp.int32, (16, 128), 0)
    extra = jnp.zeros((16, 128), F32)
    for s in range(FAR):
        tail = gathered[s, DENSE:, :].astype(F32)
        extra = jnp.where(place == s, jnp.broadcast_to(tail[1:2], (16, 128)), extra)
    extra = extra.astype(BF)
    copies = []
    for n in range(NEAR):
        for s in range(FAR):
            start = pl.multiple_of(piece[s, ORDER[n]] * HALF, HALF)
            held[n, s * HALF : (s + 1) * HALF, :] = gathered[s, pl.ds(start, HALF), :]
        held[n, FAR * HALF :, :] = extra
        copies.append(pltpu.make_async_copy(held.at[n], out.at[n], sems.at[n]))
        copies[-1].start()
    for copy in copies:
        copy.wait()


def twice(tile):
    zero = jnp.zeros_like(tile)
    return jnp.concatenate(
        [jnp.concatenate([tile, zero], axis=1), jnp.concatenate([zero, tile], axis=1)], axis=0
    )


def forward_body(
    target,
    came,
    remote,
    feats_far,
    local_far,
    adj_far,
    out,
    feats,
    local,
    adj,
    total,
    sems,
):
    copies = start_all([(feats_far, feats), (local_far, local), (adj_far, adj)], sems)
    total[...] = jnp.zeros_like(total)

    def step(s, carry):
        start = pl.multiple_of(s * HALF, HALF)
        for first in range(0, NEAR, 8):
            parts = []
            for n in range(first, first + 8):
                parts.append(
                    dot(came[n, pl.ds(start, HALF), :], twice(remote[s * NEAR + ORDER[n]]))
                )
            for n in range(first, first + 8):
                total[target[s * NEAR + ORDER[n]]] += parts[n - first]
        return carry

    lax.fori_loop(0, FAR, step, 0)
    for copy in copies:
        copy.wait()
    hub_rows = jnp.concatenate([came[SLOT[n], FAR * HALF :, :][:8] for n in range(NEAR)], axis=0)
    hub = (
        dot(hub_rows, adj[: PEERS, :], TN)[:FEAT] + dot(hub_rows, adj[PEERS:, :], TN)[FEAT:]
    )
    for b in range(BLOCKS):
        cols = slice(b * BLK, (b + 1) * BLK)
        tiles = jnp.concatenate([total[b, :, :BLK], total[b, :, BLK:]], axis=0)
        own = dot(feats[:, cols], local[b])
        value = (own + tiles + hub[:, cols]).astype(BF)
        for c in range(COLS):
            out[c, :, cols] = value


def middle_body(
    col,
    target,
    agg,
    remote,
    weight_far,
    cot_far,
    local_far,
    adj_far,
    output,
    back,
    own_grad,
    weight,
    cot,
    local,
    adj,
    grad,
    pick,
    sems,
):
    pairs = [(weight_far, weight), (cot_far, cot), (local_far, local), (adj_far, adj)]
    copies = start_all(pairs, sems)
    copies[0].wait()
    scale = 0.7978845608028654
    mine = pl.multiple_of(col[0] * FEAT, FEAT)
    for c in range(COLS):
        pre = dot(weight[:, c * FEAT : (c + 1) * FEAT], agg[...], TN)
        square = pre * pre
        bend = jnp.tanh(scale * (pre + 0.044715 * (square * pre)))
        half = 0.5 * (1.0 + bend)
        slope = half + 0.5 * pre * (1.0 - bend * bend) * (
            scale * (1.0 + 3.0 * 0.044715 * square)
        )
        if c == 0:
            copies[1].wait()
        grad[c * FEAT : (c + 1) * FEAT, :] = (
            cot[c * FEAT : (c + 1) * FEAT, :].astype(F32) * slope
        ).astype(BF)

        @pl.when(col[0] == c)
        def _():
            output[...] = (pre * half).astype(BF)

    grad_agg = dot(weight[pl.ds(mine, FEAT), :], grad[...]).astype(BF)
    weight_grad = dot(agg[pl.ds(mine, FEAT), :], grad[...], NT)
    copies[2].wait()
    for b in range(BLOCKS):
        cols = slice(b * BLK, (b + 1) * BLK)
        pick[b] = grad_agg[:, cols]
        own_grad[:, cols] = dot(grad_agg[:, cols], local[b], NT)
    copies[3].wait()
    pick[BLOCKS] = jnp.zeros((FEAT, BLK), BF)
    hub = dot(adj[...], grad_agg, NT)
    hub = jnp.concatenate([hub[:PEERS], hub[PEERS:]], axis=1)
    for n in range(NEAR):
        m = ORDER[n]
        i, j = m // 2, m % 2
        tile = weight_grad[i * 8 : (i + 1) * 8, j * 128 : (j + 1) * 128]
        back[n, FAR * HALF :, :] = jnp.concatenate([hub[m * 8 : (m + 1) * 8], tile], axis=0).astype(BF)

    def step(s, carry):
        start = pl.multiple_of(s * HALF, HALF)
        for n in range(NEAR):
            q = s * NEAR + ORDER[n]
            tile = dot(pick[target[q]], remote[q], NT)
            tile = jnp.concatenate([tile[:HALF], tile[HALF:]], axis=1)
            back[n, pl.ds(start, HALF), :] = tile.astype(BF)
        return carry

    lax.fori_loop(0, FAR, step, 0)


def gather_body(slot, piece, came, out, total):
    total[...] = jnp.zeros_like(total)
    extra = jnp.zeros((16, 128), F32)
    for n in range(NEAR):
        extra += came[n, FAR * HALF :, :].astype(F32)
    for s in range(FAR):
        hub = jnp.broadcast_to(extra[s : s + 1], (8, 128))
        out[slot[s], DENSE:, :] = jnp.concatenate([hub, extra[8:]], axis=0).astype(BF)

    def step(s, carry):
        start = pl.multiple_of(s * HALF, HALF)
        for n in range(NEAR):
            at = pl.multiple_of(piece[s, ORDER[n]] * HALF, HALF)
            total[s, pl.ds(at, HALF), :] += came[n, pl.ds(start, HALF), :].astype(F32)
        out[slot[s], :DENSE, :] = total[s].astype(BF)
        return carry

    lax.fori_loop(0, FAR, step, 0)


def chunk_body(came, chunk):
    tail = came[0, DENSE:, :].astype(F32)
    for s in range(1, FAR):
        tail += came[s, DENSE:, :].astype(F32)
    for n in range(NEAR):
        chunk[n] = tail[8:]


def final_body(hubs, came, own_grad, out):
    total = came[0].astype(F32)
    for s in range(1, FAR):
        total += came[s].astype(F32)
    node = lax.broadcasted_iota(jnp.int32, (8, ROWS), 1)
    which = lax.broadcasted_iota(jnp.int32, (8, ROWS), 0)
    hub = jnp.where(which == 0, hubs[0, 0], hubs[0, 1])
    pick = ((node == hub) & (which < 2)).astype(F32)
    row = total[DENSE : DENSE + 8]
    place = lax.broadcasted_iota(jnp.int32, (8, FEAT), 0)
    values = jnp.where(place == 0, row[:, :FEAT], row[:, FEAT:])
    hub_grad = lax.dot_general(
        values, pick, TN, preferred_element_type=F32, precision=lax.Precision.HIGHEST
    )
    for k in range(0, PIECES, 2):
        cols = slice(k * PIECE, (k + 2) * PIECE)
        a, b = total[k * HALF : (k + 1) * HALF], total[(k + 1) * HALF : (k + 2) * HALF]
        low = jnp.concatenate([a[:, :PIECE], b[:, :PIECE]], axis=1)
        high = jnp.concatenate([a[:, PIECE:], b[:, PIECE:]], axis=1)
        tiles = jnp.concatenate([low, high], axis=0)
        out[:, cols] = (own_grad[:, cols] + tiles + hub_grad[:, cols]).astype(BF)


def exchange(values, axis, groups=None):
    return lax.all_to_all(
        values,
        axis,
        split_axis=0,
        concat_axis=0,
        tiled=True,
        axis_index_groups=groups,
    )


def shards(
    features,
    send_pieces,
    remote_target,
    remote_count,
    local_values,
    remote_values,
    hub_rows,
    hub_adjacency,
    weight,
    cotangent,
):
    row = lax.axis_index("row").astype(jnp.int32)
    far, near = row // NEAR, row % NEAR
    slot = jnp.array(FAR_SLOTS, jnp.int32)[place_of(near)]
    col = lax.axis_index("col").astype(jnp.int32).reshape(1)
    target = jnp.where(
        jnp.arange(PEERS, dtype=jnp.int32) < remote_count[0], remote_target[0], BLOCKS
    )
    adj = (
        hub_adjacency.reshape(FAR, NEAR, 2, ROWS).transpose(2, 1, 0, 3).reshape(2 * PEERS, ROWS)
    )
    (packed,) = call(pack_body, [smem(), vmem(), vmem()], [((OUT_ROWS, 128), BF, vmem())])(
        stay(hub_rows), stay(features), stay(send_pieces)
    )
    gathered = lax.all_gather(packed, "row", axis=0, axis_index_groups=FAR_IDS)
    piece = lax.dynamic_slice(
        gathered[:, DENSE, :], (jnp.int32(0), far * NEAR), (FAR, NEAR)
    ).astype(jnp.int32)
    near_all = (NEAR, NEAR_ROWS, 128)
    (picked,) = call(
        pick_body,
        [smem(), vmem()],
        [(near_all, BF, away())],
        [pltpu.VMEM(near_all, BF), pltpu.SemaphoreType.DMA((NEAR,))],
    )(piece, gathered)
    picked, cotangent = lax.optimization_barrier((picked, cotangent))
    came = exchange(picked, "row", NEAR_GROUPS)
    cot = lax.all_gather(cotangent, "col", axis=0, tiled=True)
    came, cot, col, slot = lax.optimization_barrier((came, cot, col, slot))
    small = [pltpu.VMEM((BLOCKS, BLK, BLK), BF), pltpu.VMEM((2 * PEERS, ROWS), BF)]
    (agg,) = call(
        forward_body,
        [smem(), vmem(), vmem()] + [away()] * 3,
        [((COLS, FEAT, ROWS), BF, vmem())],
        [pltpu.VMEM((FEAT, ROWS), BF)]
        + small
        + [
            pltpu.VMEM((BLOCKS + 1, HALF, 2 * BLK), F32),
            pltpu.SemaphoreType.DMA((3,)),
        ],
    )(target, came, remote_values, *map(stay, (features, local_values, adj)))
    wide = (COLS * FEAT, ROWS)
    agg = exchange(agg, "col").reshape(wide)
    output, back, own_grad = call(
        middle_body,
        [smem(), smem(), vmem(), vmem()] + [away()] * 4,
        [((FEAT, ROWS), BF, vmem()), (near_all, BF, vmem()), ((FEAT, ROWS), F32, vmem())],
        [pltpu.VMEM((COLS * FEAT, COLS * FEAT), BF), pltpu.VMEM(wide, BF)]
        + small
        + [
            pltpu.VMEM(wide, BF),
            pltpu.VMEM((BLOCKS + 1, FEAT, BLK), BF),
            pltpu.SemaphoreType.DMA((4,)),
        ],
    )(col, target, agg, remote_values, *map(stay, (weight, cot, local_values, adj)))
    back = exchange(back, "row", NEAR_GROUPS)
    far_all = (FAR, BACK_ROWS, 128)
    (sums,) = call(
        gather_body,
        [smem(), smem(), vmem()],
        [(far_all, BF, vmem())],
        [pltpu.VMEM((FAR, DENSE, 128), F32)],
    )(slot, piece, back)
    sums = exchange(sums, "row", FAR_GROUPS)
    (chunk,) = call(chunk_body, [vmem()], [((NEAR, 8, 128), F32, vmem())])(sums)
    tiles = exchange(chunk, "row", NEAR_IDS)
    (grad_input,) = call(
        final_body, [smem(), vmem(), vmem()], [((FEAT, ROWS), BF, vmem())]
    )(stay(hub_rows), sums, own_grad)
    weight_grad = tiles.reshape(8, 2, 8, 128).transpose(0, 2, 1, 3).reshape(FEAT, 256)
    return (output, grad_input, weight_grad)


def solution(mesh):
    row = "row"
    placed = (
        P("col", row),
        P(row, None),
        P(row, None),
        P(row),
        P(row, None, None),
        P(row, None, None),
        P(row, None),
        P(None, row),
        P(),
        P("col", row),
    )
    return jax.shard_map(
        shards,
        mesh=mesh,
        in_specs=placed,
        out_specs=(P("col", row), P("col", row), P("col", None)),
        check_vma=False,
    )
```

```python
import jax
import jax.numpy as jnp
from jax import lax
from jax.experimental import pallas as pl
from jax.experimental.pallas import tpu as pltpu
from jax.sharding import PartitionSpec as P

BF = jnp.bfloat16
F32 = jnp.float32

FAR = 8
NEAR = 16
COLS = 4
PEERS = FAR * NEAR
FEAT = 64
HALF = FEAT // 2
ROWS = 512
BLK = 128
BLOCKS = ROWS // BLK
PIECE = 64
PIECES = ROWS // PIECE
DENSE = PIECES * HALF
OUT_ROWS = DENSE + 16
NEAR_ROWS = FAR * HALF + 16
BACK_ROWS = NEAR_ROWS
VMEM_BYTES = 30 * 1024 * 1024
ORDER = (7, 0, 12, 3, 9, 14, 5, 10, 1, 15, 6, 2, 13, 8, 4, 11)
FAR_ORDERS = (
    (6, 2, 7, 0, 5, 3, 1, 4),
    (6, 1, 3, 0, 5, 4, 2, 7),
    (0, 7, 6, 2, 1, 5, 3, 4),
    (5, 6, 3, 2, 0, 7, 4, 1),
)
FAR_SLOTS = tuple(tuple(order.index(s) for s in range(FAR)) for order in FAR_ORDERS)
NEAR_IDS = tuple(tuple(f * NEAR + n for n in range(NEAR)) for f in range(FAR))
FAR_IDS = tuple(tuple(f * NEAR + n for f in range(FAR)) for n in range(NEAR))
NEAR_GROUPS = tuple(tuple(ids[n] for n in ORDER) for ids in NEAR_IDS)


def place_of(near):
    return 2 * (near // 8) + near % 2


FAR_GROUPS = tuple(
    tuple(FAR_IDS[n][f] for f in FAR_ORDERS[place_of(n)]) for n in range(NEAR)
)
SLOT = tuple(ORDER.index(n) for n in range(NEAR))

NT = (((1,), (1,)), ((), ()))
TN = (((0,), (0,)), ((), ()))
NN = (((1,), (0,)), ((), ()))


def dot(left, right, dims=NN):
    return lax.dot_general(left, right, dims, preferred_element_type=F32)


def vmem():
    return pl.BlockSpec(memory_space=pltpu.VMEM)


def smem():
    return pl.BlockSpec(memory_space=pltpu.SMEM)


def away():
    return pl.BlockSpec(memory_space=pl.ANY)


def call(body, ins, outs, scratch=(), flops=1_000_000, size=1_000_000):
    return pl.pallas_call(
        body,
        in_specs=ins,
        out_specs=[spec for _, _, spec in outs],
        out_shape=[
            pltpu.HBM(shape, kind)
            if spec.memory_space is pl.ANY
            else jax.ShapeDtypeStruct(shape, kind)
            for shape, kind, spec in outs
        ],
        scratch_shapes=list(scratch),
        compiler_params=pltpu.CompilerParams(vmem_limit_bytes=VMEM_BYTES),
        cost_estimate=pl.CostEstimate(flops=flops, bytes_accessed=size, transcendentals=0),
    )


def start_all(pairs, sems):
    copies = [pltpu.make_async_copy(src, dst, sems.at[i]) for i, (src, dst) in enumerate(pairs)]
    for copy in copies:
        copy.start()
    return copies


def stay(value):
    return pltpu.with_memory_space_constraint(value, pltpu.HBM)


def pack_body(hubs, feats, wanted, out):
    for k in range(PIECES):
        low = feats[:HALF, k * PIECE : (k + 1) * PIECE]
        high = feats[HALF:, k * PIECE : (k + 1) * PIECE]
        out[k * HALF : (k + 1) * HALF, :] = jnp.concatenate([low, high], axis=1)
    node = lax.broadcasted_iota(jnp.int32, (8, ROWS), 1)
    which = lax.broadcasted_iota(jnp.int32, (8, ROWS), 0)
    hub = jnp.where(which == 0, hubs[0, 0], hubs[0, 1])
    pick = ((node == hub) & (which < 2)).astype(BF)
    rows = dot(pick, feats[...], NT)
    hub_row = jnp.concatenate([rows[0:1], rows[1:2]], axis=1)
    place = lax.broadcasted_iota(jnp.int32, (16, 128), 0)
    extra = jnp.where(
        place == 0,
        jnp.broadcast_to(wanted[...].astype(F32), (16, 128)),
        jnp.where(place == 1, jnp.broadcast_to(hub_row, (16, 128)), 0.0),
    )
    out[DENSE:, :] = extra.astype(BF)


def pick_body(piece, gathered, out, held, sems):
    place = lax.broadcasted_iota(jnp.int32, (16, 128), 0)
    extra = jnp.zeros((16, 128), F32)
    for s in range(FAR):
        tail = gathered[s, DENSE:, :].astype(F32)
        extra = jnp.where(place == s, jnp.broadcast_to(tail[1:2], (16, 128)), extra)
    extra = extra.astype(BF)
    copies = []
    for n in range(NEAR):
        for s in range(FAR):
            start = pl.multiple_of(piece[s, ORDER[n]] * HALF, HALF)
            held[n, s * HALF : (s + 1) * HALF, :] = gathered[s, pl.ds(start, HALF), :]
        held[n, FAR * HALF :, :] = extra
        copies.append(pltpu.make_async_copy(held.at[n], out.at[n], sems.at[n]))
        copies[-1].start()
    for copy in copies:
        copy.wait()


def twice(tile):
    zero = jnp.zeros_like(tile)
    return jnp.concatenate(
        [jnp.concatenate([tile, zero], axis=1), jnp.concatenate([zero, tile], axis=1)], axis=0
    )


def forward_body(
    target,
    came,
    remote,
    feats_far,
    local_far,
    adj_far,
    out,
    feats,
    local,
    adj,
    total,
    sems,
):
    copies = start_all([(feats_far, feats), (local_far, local), (adj_far, adj)], sems)
    total[...] = jnp.zeros_like(total)

    for s in range(FAR):
        for first in range(0, NEAR, 8):
            parts = []
            for n in range(first, first + 8):
                q = s * NEAR + ORDER[n]
                parts.append(dot(came[n, s * HALF : (s + 1) * HALF, :], twice(remote[q])))
            for n in range(first, first + 8):
                total[target[s * NEAR + ORDER[n]]] += parts[n - first]
    for copy in copies:
        copy.wait()
    hub_rows = jnp.concatenate([came[SLOT[n], FAR * HALF :, :][:8] for n in range(NEAR)], axis=0)
    hub = (
        dot(hub_rows, adj[: PEERS, :], TN)[:FEAT] + dot(hub_rows, adj[PEERS:, :], TN)[FEAT:]
    )
    for b in range(BLOCKS):
        cols = slice(b * BLK, (b + 1) * BLK)
        tiles = jnp.concatenate([total[b, :, :BLK], total[b, :, BLK:]], axis=0)
        own = dot(feats[:, cols], local[b])
        value = (own + tiles + hub[:, cols]).astype(BF)
        for c in range(COLS):
            out[c, :, cols] = value


def middle_body(
    col,
    target,
    agg,
    remote,
    weight_far,
    cot_far,
    local_far,
    adj_far,
    output,
    back,
    own_grad,
    weight,
    cot,
    local,
    adj,
    grad,
    pick,
    sems,
):
    pairs = [(weight_far, weight), (cot_far, cot), (local_far, local), (adj_far, adj)]
    copies = start_all(pairs, sems)
    copies[0].wait()
    scale = 0.7978845608028654
    mine = pl.multiple_of(col[0] * FEAT, FEAT)
    for c in range(COLS):
        pre = dot(weight[:, c * FEAT : (c + 1) * FEAT], agg[...], TN)
        square = pre * pre
        bend = jnp.tanh(scale * (pre + 0.044715 * (square * pre)))
        half = 0.5 * (1.0 + bend)
        slope = half + 0.5 * pre * (1.0 - bend * bend) * (
            scale * (1.0 + 3.0 * 0.044715 * square)
        )
        if c == 0:
            copies[1].wait()
        grad[c * FEAT : (c + 1) * FEAT, :] = (
            cot[c * FEAT : (c + 1) * FEAT, :].astype(F32) * slope
        ).astype(BF)

        @pl.when(col[0] == c)
        def _():
            output[...] = (pre * half).astype(BF)

    grad_agg = dot(weight[pl.ds(mine, FEAT), :], grad[...]).astype(BF)
    weight_grad = dot(agg[pl.ds(mine, FEAT), :], grad[...], NT)
    copies[2].wait()
    for b in range(BLOCKS):
        cols = slice(b * BLK, (b + 1) * BLK)
        pick[b] = grad_agg[:, cols]
        own_grad[:, cols] = dot(grad_agg[:, cols], local[b], NT)
    copies[3].wait()
    pick[BLOCKS] = jnp.zeros((FEAT, BLK), BF)
    hub = dot(adj[...], grad_agg, NT)
    hub = jnp.concatenate([hub[:PEERS], hub[PEERS:]], axis=1)
    for n in range(NEAR):
        m = ORDER[n]
        i, j = m // 2, m % 2
        tile = weight_grad[i * 8 : (i + 1) * 8, j * 128 : (j + 1) * 128]
        back[n, FAR * HALF :, :] = jnp.concatenate([hub[m * 8 : (m + 1) * 8], tile], axis=0).astype(BF)

    for s in range(FAR):
        for n in range(NEAR):
            q = s * NEAR + ORDER[n]
            tile = dot(pick[target[q]], remote[q], NT)
            tile = jnp.concatenate([tile[:HALF], tile[HALF:]], axis=1)
            back[n, s * HALF : (s + 1) * HALF, :] = tile.astype(BF)


def gather_body(slot, piece, came, out, total):
    total[...] = jnp.zeros_like(total)
    extra = jnp.zeros((16, 128), F32)
    for n in range(NEAR):
        extra += came[n, FAR * HALF :, :].astype(F32)
    for s in range(FAR):
        hub = jnp.broadcast_to(extra[s : s + 1], (8, 128))
        out[slot[s], DENSE:, :] = jnp.concatenate([hub, extra[8:]], axis=0).astype(BF)

    for s in range(FAR):
        for n in range(NEAR):
            at = pl.multiple_of(piece[s, ORDER[n]] * HALF, HALF)
            total[s, pl.ds(at, HALF), :] += came[n, s * HALF : (s + 1) * HALF, :].astype(F32)
        out[slot[s], :DENSE, :] = total[s].astype(BF)


def chunk_body(came, chunk):
    tail = came[0, DENSE:, :].astype(F32)
    for s in range(1, FAR):
        tail += came[s, DENSE:, :].astype(F32)
    for n in range(NEAR):
        chunk[n] = tail[8:]


def final_body(hubs, came, own_grad, out):
    total = came[0].astype(F32)
    for s in range(1, FAR):
        total += came[s].astype(F32)
    node = lax.broadcasted_iota(jnp.int32, (8, ROWS), 1)
    which = lax.broadcasted_iota(jnp.int32, (8, ROWS), 0)
    hub = jnp.where(which == 0, hubs[0, 0], hubs[0, 1])
    pick = ((node == hub) & (which < 2)).astype(F32)
    row = total[DENSE : DENSE + 8]
    place = lax.broadcasted_iota(jnp.int32, (8, FEAT), 0)
    values = jnp.where(place == 0, row[:, :FEAT], row[:, FEAT:])
    hub_grad = lax.dot_general(
        values, pick, TN, preferred_element_type=F32, precision=lax.Precision.HIGHEST
    )
    for k in range(0, PIECES, 2):
        cols = slice(k * PIECE, (k + 2) * PIECE)
        a, b = total[k * HALF : (k + 1) * HALF], total[(k + 1) * HALF : (k + 2) * HALF]
        low = jnp.concatenate([a[:, :PIECE], b[:, :PIECE]], axis=1)
        high = jnp.concatenate([a[:, PIECE:], b[:, PIECE:]], axis=1)
        tiles = jnp.concatenate([low, high], axis=0)
        out[:, cols] = (own_grad[:, cols] + tiles + hub_grad[:, cols]).astype(BF)


def exchange(values, axis, groups=None):
    return lax.all_to_all(
        values,
        axis,
        split_axis=0,
        concat_axis=0,
        tiled=True,
        axis_index_groups=groups,
    )


def shards(
    features,
    send_pieces,
    remote_target,
    remote_count,
    local_values,
    remote_values,
    hub_rows,
    hub_adjacency,
    weight,
    cotangent,
):
    row = lax.axis_index("row").astype(jnp.int32)
    far, near = row // NEAR, row % NEAR
    slot = jnp.array(FAR_SLOTS, jnp.int32)[place_of(near)]
    col = lax.axis_index("col").astype(jnp.int32).reshape(1)
    target = jnp.where(
        jnp.arange(PEERS, dtype=jnp.int32) < remote_count[0], remote_target[0], BLOCKS
    )
    adj = (
        hub_adjacency.reshape(FAR, NEAR, 2, ROWS).transpose(2, 1, 0, 3).reshape(2 * PEERS, ROWS)
    )
    (packed,) = call(pack_body, [smem(), vmem(), vmem()], [((OUT_ROWS, 128), BF, vmem())])(
        stay(hub_rows), stay(features), stay(send_pieces)
    )
    gathered = lax.all_gather(packed, "row", axis=0, axis_index_groups=FAR_IDS)
    piece = lax.dynamic_slice(
        gathered[:, DENSE, :], (jnp.int32(0), far * NEAR), (FAR, NEAR)
    ).astype(jnp.int32)
    near_all = (NEAR, NEAR_ROWS, 128)
    (picked,) = call(
        pick_body,
        [smem(), vmem()],
        [(near_all, BF, away())],
        [pltpu.VMEM(near_all, BF), pltpu.SemaphoreType.DMA((NEAR,))],
    )(piece, gathered)
    picked, cotangent = lax.optimization_barrier((picked, cotangent))
    came = exchange(picked, "row", NEAR_GROUPS)
    cot = lax.all_gather(cotangent, "col", axis=0, tiled=True)
    came, cot, col, slot = lax.optimization_barrier((came, cot, col, slot))
    small = [pltpu.VMEM((BLOCKS, BLK, BLK), BF), pltpu.VMEM((2 * PEERS, ROWS), BF)]
    (agg,) = call(
        forward_body,
        [smem(), vmem(), vmem()] + [away()] * 3,
        [((COLS, FEAT, ROWS), BF, vmem())],
        [pltpu.VMEM((FEAT, ROWS), BF)]
        + small
        + [
            pltpu.VMEM((BLOCKS + 1, HALF, 2 * BLK), F32),
            pltpu.SemaphoreType.DMA((3,)),
        ],
    )(target, came, remote_values, *map(stay, (features, local_values, adj)))
    wide = (COLS * FEAT, ROWS)
    agg = exchange(agg, "col").reshape(wide)
    output, back, own_grad = call(
        middle_body,
        [smem(), smem(), vmem(), vmem()] + [away()] * 4,
        [((FEAT, ROWS), BF, vmem()), (near_all, BF, vmem()), ((FEAT, ROWS), F32, vmem())],
        [pltpu.VMEM((COLS * FEAT, COLS * FEAT), BF), pltpu.VMEM(wide, BF)]
        + small
        + [
            pltpu.VMEM(wide, BF),
            pltpu.VMEM((BLOCKS + 1, FEAT, BLK), BF),
            pltpu.SemaphoreType.DMA((4,)),
        ],
    )(col, target, agg, remote_values, *map(stay, (weight, cot, local_values, adj)))
    back = exchange(back, "row", NEAR_GROUPS)
    far_all = (FAR, BACK_ROWS, 128)
    (sums,) = call(
        gather_body,
        [smem(), smem(), vmem()],
        [(far_all, BF, vmem())],
        [pltpu.VMEM((FAR, DENSE, 128), F32)],
    )(slot, piece, back)
    sums = exchange(sums, "row", FAR_GROUPS)
    (chunk,) = call(chunk_body, [vmem()], [((NEAR, 8, 128), F32, vmem())])(sums)
    tiles = exchange(chunk, "row", NEAR_IDS)
    (grad_input,) = call(
        final_body, [smem(), vmem(), vmem()], [((FEAT, ROWS), BF, vmem())]
    )(stay(hub_rows), sums, own_grad)
    weight_grad = tiles.reshape(8, 2, 8, 128).transpose(0, 2, 1, 3).reshape(FEAT, 256)
    return (output, grad_input, weight_grad)


def solution(mesh):
    row = "row"
    placed = (
        P("col", row),
        P(row, None),
        P(row, None),
        P(row),
        P(row, None, None),
        P(row, None, None),
        P(row, None),
        P(None, row),
        P(),
        P("col", row),
    )
    return jax.shard_map(
        shards,
        mesh=mesh,
        in_specs=placed,
        out_specs=(P("col", row), P("col", row), P("col", None)),
        check_vma=False,
    )
```

```python
import jax
import jax.numpy as jnp
from jax import lax
from jax.experimental import pallas as pl
from jax.experimental.pallas import tpu as pltpu
from jax.sharding import PartitionSpec as P

BF = jnp.bfloat16
F32 = jnp.float32

FAR = 8
NEAR = 16
COLS = 4
PEERS = FAR * NEAR
FEAT = 64
HALF = FEAT // 2
ROWS = 512
BLK = 128
BLOCKS = ROWS // BLK
PIECE = 64
PIECES = ROWS // PIECE
DENSE = PIECES * HALF
OUT_ROWS = DENSE + 16
NEAR_ROWS = FAR * HALF + 16
BACK_ROWS = NEAR_ROWS
VMEM_BYTES = 30 * 1024 * 1024
ORDER = (7, 0, 12, 3, 9, 14, 5, 10, 1, 15, 6, 2, 13, 8, 4, 11)
FAR_ORDERS = (
    (6, 2, 7, 0, 5, 3, 1, 4),
    (6, 1, 3, 0, 5, 4, 2, 7),
    (0, 7, 6, 2, 1, 5, 3, 4),
    (5, 6, 3, 2, 0, 7, 4, 1),
)
FAR_SLOTS = tuple(tuple(order.index(s) for s in range(FAR)) for order in FAR_ORDERS)
NEAR_IDS = tuple(tuple(f * NEAR + n for n in range(NEAR)) for f in range(FAR))
FAR_IDS = tuple(tuple(f * NEAR + n for f in range(FAR)) for n in range(NEAR))
NEAR_GROUPS = tuple(tuple(ids[n] for n in ORDER) for ids in NEAR_IDS)


def place_of(near):
    return 2 * (near // 8) + near % 2


def slot_of(place, s):
    chosen = jnp.int32(FAR_SLOTS[0][s])
    for other in range(1, len(FAR_SLOTS)):
        chosen = jnp.where(place == other, FAR_SLOTS[other][s], chosen)
    return chosen


FAR_GROUPS = tuple(
    tuple(FAR_IDS[n][f] for f in FAR_ORDERS[place_of(n)]) for n in range(NEAR)
)
SLOT = tuple(ORDER.index(n) for n in range(NEAR))

NT = (((1,), (1,)), ((), ()))
TN = (((0,), (0,)), ((), ()))
NN = (((1,), (0,)), ((), ()))


def dot(left, right, dims=NN):
    return lax.dot_general(left, right, dims, preferred_element_type=F32)


def vmem():
    return pl.BlockSpec(memory_space=pltpu.VMEM)


def smem():
    return pl.BlockSpec(memory_space=pltpu.SMEM)


def away():
    return pl.BlockSpec(memory_space=pl.ANY)


def call(body, ins, outs, scratch=(), flops=1_000_000, size=1_000_000):
    return pl.pallas_call(
        body,
        in_specs=ins,
        out_specs=[spec for _, _, spec in outs],
        out_shape=[
            pltpu.HBM(shape, kind)
            if spec.memory_space is pl.ANY
            else jax.ShapeDtypeStruct(shape, kind)
            for shape, kind, spec in outs
        ],
        scratch_shapes=list(scratch),
        compiler_params=pltpu.CompilerParams(vmem_limit_bytes=VMEM_BYTES),
        cost_estimate=pl.CostEstimate(flops=flops, bytes_accessed=size, transcendentals=0),
    )


def start_all(pairs, sems):
    copies = [pltpu.make_async_copy(src, dst, sems.at[i]) for i, (src, dst) in enumerate(pairs)]
    for copy in copies:
        copy.start()
    return copies


def stay(value):
    return pltpu.with_memory_space_constraint(value, pltpu.HBM)


def pack_body(hubs, feats, wanted, out):
    for k in range(PIECES):
        low = feats[:HALF, k * PIECE : (k + 1) * PIECE]
        high = feats[HALF:, k * PIECE : (k + 1) * PIECE]
        out[k * HALF : (k + 1) * HALF, :] = jnp.concatenate([low, high], axis=1)
    node = lax.broadcasted_iota(jnp.int32, (8, ROWS), 1)
    which = lax.broadcasted_iota(jnp.int32, (8, ROWS), 0)
    hub = jnp.where(which == 0, hubs[0, 0], hubs[0, 1])
    pick = ((node == hub) & (which < 2)).astype(BF)
    rows = dot(pick, feats[...], NT)
    hub_row = jnp.concatenate([rows[0:1], rows[1:2]], axis=1)
    place = lax.broadcasted_iota(jnp.int32, (16, 128), 0)
    extra = jnp.where(
        place == 0,
        jnp.broadcast_to(wanted[...].astype(F32), (16, 128)),
        jnp.where(place == 1, jnp.broadcast_to(hub_row, (16, 128)), 0.0),
    )
    out[DENSE:, :] = extra.astype(BF)


def pick_body(piece, gathered, out, held, sems):
    place = lax.broadcasted_iota(jnp.int32, (16, 128), 0)
    extra = jnp.zeros((16, 128), F32)
    for s in range(FAR):
        tail = gathered[s, DENSE:, :].astype(F32)
        extra = jnp.where(place == s, jnp.broadcast_to(tail[1:2], (16, 128)), extra)
    extra = extra.astype(BF)
    copies = []
    for n in range(NEAR):
        for s in range(FAR):
            start = pl.multiple_of(piece[s, ORDER[n]] * HALF, HALF)
            held[n, s * HALF : (s + 1) * HALF, :] = gathered[s, pl.ds(start, HALF), :]
        held[n, FAR * HALF :, :] = extra
        copies.append(pltpu.make_async_copy(held.at[n], out.at[n], sems.at[n]))
        copies[-1].start()
    for copy in copies:
        copy.wait()


def twice(tile):
    zero = jnp.zeros_like(tile)
    return jnp.concatenate(
        [jnp.concatenate([tile, zero], axis=1), jnp.concatenate([zero, tile], axis=1)], axis=0
    )


def forward_body(
    target,
    came,
    remote,
    feats_far,
    local_far,
    adj_far,
    out,
    feats,
    local,
    adj,
    total,
    sems,
):
    copies = start_all([(feats_far, feats), (local_far, local), (adj_far, adj)], sems)
    total[...] = jnp.zeros_like(total)

    for s in range(FAR):
        for first in range(0, NEAR, 8):
            parts = []
            for n in range(first, first + 8):
                q = s * NEAR + ORDER[n]
                parts.append(dot(came[n, s * HALF : (s + 1) * HALF, :], twice(remote[q])))
            for n in range(first, first + 8):
                total[target[s * NEAR + ORDER[n]]] += parts[n - first]
    for copy in copies:
        copy.wait()
    hub_rows = jnp.concatenate([came[SLOT[n], FAR * HALF :, :][:8] for n in range(NEAR)], axis=0)
    hub_rows = jnp.concatenate([hub_rows[:, :FEAT], hub_rows[:, FEAT:]], axis=0)
    hub = dot(hub_rows, adj[...], TN)
    for b in range(BLOCKS):
        cols = slice(b * BLK, (b + 1) * BLK)
        tiles = jnp.concatenate([total[b, :, :BLK], total[b, :, BLK:]], axis=0)
        own = dot(feats[:, cols], local[b])
        value = (own + tiles + hub[:, cols]).astype(BF)
        for c in range(COLS):
            out[c, :, cols] = value


def middle_body(
    col,
    target,
    agg,
    remote,
    weight,
    cot,
    local,
    adj,
    output,
    back,
    own_grad,
    grad,
    pick,
):
    scale = 0.7978845608028654
    mine = pl.multiple_of(col[0] * FEAT, FEAT)
    for c in range(COLS):
        pre = dot(weight[:, c * FEAT : (c + 1) * FEAT], agg[...], TN)
        square = pre * pre
        bend = jnp.tanh(scale * (pre + 0.044715 * (square * pre)))
        half = 0.5 * (1.0 + bend)
        slope = half + 0.5 * pre * (1.0 - bend * bend) * (
            scale * (1.0 + 3.0 * 0.044715 * square)
        )
        grad[c * FEAT : (c + 1) * FEAT, :] = (
            cot[c * FEAT : (c + 1) * FEAT, :].astype(F32) * slope
        ).astype(BF)

        @pl.when(col[0] == c)
        def _():
            output[...] = (pre * half).astype(BF)

    grad_agg = dot(weight[pl.ds(mine, FEAT), :], grad[...]).astype(BF)
    weight_grad = dot(agg[pl.ds(mine, FEAT), :], grad[...], NT)
    for b in range(BLOCKS):
        cols = slice(b * BLK, (b + 1) * BLK)
        pick[b] = grad_agg[:, cols]
        own_grad[:, cols] = dot(grad_agg[:, cols], local[b], NT)
    pick[BLOCKS] = jnp.zeros((FEAT, BLK), BF)
    hub = dot(adj[...], grad_agg, NT)
    hub = jnp.concatenate([hub[:PEERS], hub[PEERS:]], axis=1)
    for n in range(NEAR):
        m = ORDER[n]
        i, j = m // 2, m % 2
        tile = weight_grad[i * 8 : (i + 1) * 8, j * 128 : (j + 1) * 128]
        back[n, FAR * HALF :, :] = jnp.concatenate([hub[m * 8 : (m + 1) * 8], tile], axis=0).astype(BF)

    for s in range(FAR):
        for n in range(NEAR):
            q = s * NEAR + ORDER[n]
            tile = dot(pick[target[q]], remote[q], NT)
            tile = jnp.concatenate([tile[:HALF], tile[HALF:]], axis=1)
            back[n, s * HALF : (s + 1) * HALF, :] = tile.astype(BF)


def gather_body(place, piece, came, out, total):
    slot = [slot_of(place[0], s) for s in range(FAR)]
    total[...] = jnp.zeros_like(total)
    extra = jnp.zeros((16, 128), F32)
    for n in range(NEAR):
        extra += came[n, FAR * HALF :, :].astype(F32)
    for s in range(FAR):
        hub = jnp.broadcast_to(extra[s : s + 1], (8, 128))
        out[slot[s], DENSE:, :] = jnp.concatenate([hub, extra[8:]], axis=0).astype(BF)

    for s in range(FAR):
        for n in range(NEAR):
            at = pl.multiple_of(piece[s, ORDER[n]] * HALF, HALF)
            total[s, pl.ds(at, HALF), :] += came[n, s * HALF : (s + 1) * HALF, :].astype(F32)
        out[slot[s], :DENSE, :] = total[s].astype(BF)


def chunk_body(came, chunk):
    tail = came[0, DENSE:, :].astype(F32)
    for s in range(1, FAR):
        tail += came[s, DENSE:, :].astype(F32)
    for n in range(NEAR):
        chunk[n] = tail[8:]


def final_body(hubs, came, own_grad, out):
    total = came[0].astype(F32)
    for s in range(1, FAR):
        total += came[s].astype(F32)
    node = lax.broadcasted_iota(jnp.int32, (8, ROWS), 1)
    which = lax.broadcasted_iota(jnp.int32, (8, ROWS), 0)
    hub = jnp.where(which == 0, hubs[0, 0], hubs[0, 1])
    pick = ((node == hub) & (which < 2)).astype(F32)
    row = total[DENSE : DENSE + 8]
    place = lax.broadcasted_iota(jnp.int32, (8, FEAT), 0)
    values = jnp.where(place == 0, row[:, :FEAT], row[:, FEAT:])
    hub_grad = lax.dot_general(
        values, pick, TN, preferred_element_type=F32, precision=lax.Precision.HIGHEST
    )
    for k in range(0, PIECES, 2):
        cols = slice(k * PIECE, (k + 2) * PIECE)
        a, b = total[k * HALF : (k + 1) * HALF], total[(k + 1) * HALF : (k + 2) * HALF]
        low = jnp.concatenate([a[:, :PIECE], b[:, :PIECE]], axis=1)
        high = jnp.concatenate([a[:, PIECE:], b[:, PIECE:]], axis=1)
        tiles = jnp.concatenate([low, high], axis=0)
        out[:, cols] = (own_grad[:, cols] + tiles + hub_grad[:, cols]).astype(BF)


def exchange(values, axis, groups=None):
    return lax.all_to_all(
        values,
        axis,
        split_axis=0,
        concat_axis=0,
        tiled=True,
        axis_index_groups=groups,
    )


def shards(
    features,
    send_pieces,
    remote_target,
    remote_count,
    local_values,
    remote_values,
    hub_rows,
    hub_adjacency,
    weight,
    cotangent,
):
    row = lax.axis_index("row").astype(jnp.int32)
    far, near = row // NEAR, row % NEAR
    place = place_of(near).reshape(1)
    col = lax.axis_index("col").astype(jnp.int32).reshape(1)
    target = jnp.where(
        jnp.arange(PEERS, dtype=jnp.int32) < remote_count[0], remote_target[0], BLOCKS
    )
    adj = (
        hub_adjacency.reshape(FAR, NEAR, 2, ROWS).transpose(2, 1, 0, 3).reshape(2 * PEERS, ROWS)
    )
    (packed,) = call(pack_body, [smem(), vmem(), vmem()], [((OUT_ROWS, 128), BF, vmem())])(
        stay(hub_rows), stay(features), stay(send_pieces)
    )
    gathered = lax.all_gather(packed, "row", axis=0, axis_index_groups=FAR_IDS)
    piece = lax.dynamic_slice(
        gathered[:, DENSE, :], (jnp.int32(0), far * NEAR), (FAR, NEAR)
    ).astype(jnp.int32)
    near_all = (NEAR, NEAR_ROWS, 128)
    (picked,) = call(
        pick_body,
        [smem(), vmem()],
        [(near_all, BF, away())],
        [pltpu.VMEM(near_all, BF), pltpu.SemaphoreType.DMA((NEAR,))],
    )(piece, gathered)
    picked, cotangent = lax.optimization_barrier((picked, cotangent))
    came = exchange(picked, "row", NEAR_GROUPS)
    cot = lax.all_gather(cotangent, "col", axis=0, tiled=True)
    came, cot, col, place = lax.optimization_barrier((came, cot, col, place))
    small = [pltpu.VMEM((BLOCKS, BLK, BLK), BF), pltpu.VMEM((2 * PEERS, ROWS), BF)]
    (agg,) = call(
        forward_body,
        [smem(), vmem(), vmem()] + [away()] * 3,
        [((COLS, FEAT, ROWS), BF, vmem())],
        [pltpu.VMEM((FEAT, ROWS), BF)]
        + small
        + [
            pltpu.VMEM((BLOCKS + 1, HALF, 2 * BLK), F32),
            pltpu.SemaphoreType.DMA((3,)),
        ],
    )(target, came, remote_values, *map(stay, (features, local_values, adj)))
    wide = (COLS * FEAT, ROWS)
    agg = exchange(agg, "col").reshape(wide)
    output, back, own_grad = call(
        middle_body,
        [smem(), smem()] + [vmem()] * 6,
        [((FEAT, ROWS), BF, vmem()), (near_all, BF, vmem()), ((FEAT, ROWS), F32, vmem())],
        [pltpu.VMEM(wide, BF), pltpu.VMEM((BLOCKS + 1, FEAT, BLK), BF)],
    )(col, target, agg, remote_values, weight, cot, local_values, adj)
    back = exchange(back, "row", NEAR_GROUPS)
    far_all = (FAR, BACK_ROWS, 128)
    (sums,) = call(
        gather_body,
        [smem(), smem(), vmem()],
        [(far_all, BF, vmem())],
        [pltpu.VMEM((FAR, DENSE, 128), F32)],
    )(place, piece, back)
    sums = exchange(sums, "row", FAR_GROUPS)
    (chunk,) = call(chunk_body, [vmem()], [((NEAR, 8, 128), F32, vmem())])(sums)
    tiles = exchange(chunk, "row", NEAR_IDS)
    (grad_input,) = call(
        final_body, [smem(), vmem(), vmem()], [((FEAT, ROWS), BF, vmem())]
    )(stay(hub_rows), sums, own_grad)
    weight_grad = tiles.reshape(8, 2, 8, 128).transpose(0, 2, 1, 3).reshape(FEAT, 256)
    return (output, grad_input, weight_grad)


def solution(mesh):
    row = "row"
    placed = (
        P("col", row),
        P(row, None),
        P(row, None),
        P(row),
        P(row, None, None),
        P(row, None, None),
        P(row, None),
        P(None, row),
        P(),
        P("col", row),
    )
    return jax.shard_map(
        shards,
        mesh=mesh,
        in_specs=placed,
        out_specs=(P("col", row), P("col", row), P("col", None)),
        check_vma=False,
    )
```

```python
import jax
import jax.numpy as jnp
from jax import lax
from jax.experimental import pallas as pl
from jax.experimental.pallas import tpu as pltpu
from jax.sharding import PartitionSpec as P

BF = jnp.bfloat16
F32 = jnp.float32

FAR = 8
NEAR = 16
COLS = 4
PEERS = FAR * NEAR
FEAT = 64
HALF = FEAT // 2
ROWS = 512
BLK = 128
BLOCKS = ROWS // BLK
PIECE = 64
PIECES = ROWS // PIECE
DENSE = PIECES * HALF
OUT_ROWS = DENSE + 16
NEAR_ROWS = FAR * HALF + 16
BACK_ROWS = NEAR_ROWS
VMEM_BYTES = 30 * 1024 * 1024
ORDER = (7, 0, 12, 3, 9, 14, 5, 10, 1, 15, 6, 2, 13, 8, 4, 11)
FAR_ORDERS = (
    (6, 2, 7, 0, 5, 3, 1, 4),
    (6, 1, 3, 0, 5, 4, 2, 7),
    (0, 7, 6, 2, 1, 5, 3, 4),
    (5, 6, 3, 2, 0, 7, 4, 1),
)
FAR_SLOTS = tuple(tuple(order.index(s) for s in range(FAR)) for order in FAR_ORDERS)
NEAR_IDS = tuple(tuple(f * NEAR + n for n in range(NEAR)) for f in range(FAR))
FAR_IDS = tuple(tuple(f * NEAR + n for f in range(FAR)) for n in range(NEAR))
NEAR_GROUPS = tuple(tuple(ids[n] for n in ORDER) for ids in NEAR_IDS)


def place_of(near):
    return 2 * (near // 8) + near % 2


def slot_of(place, s):
    chosen = jnp.int32(FAR_SLOTS[0][s])
    for other in range(1, len(FAR_SLOTS)):
        chosen = jnp.where(place == other, FAR_SLOTS[other][s], chosen)
    return chosen


FAR_GROUPS = tuple(
    tuple(FAR_IDS[n][f] for f in FAR_ORDERS[place_of(n)]) for n in range(NEAR)
)
SLOT = tuple(ORDER.index(n) for n in range(NEAR))

NT = (((1,), (1,)), ((), ()))
TN = (((0,), (0,)), ((), ()))
NN = (((1,), (0,)), ((), ()))


def dot(left, right, dims=NN):
    return lax.dot_general(left, right, dims, preferred_element_type=F32)


def vmem():
    return pl.BlockSpec(memory_space=pltpu.VMEM)


def smem():
    return pl.BlockSpec(memory_space=pltpu.SMEM)


def away():
    return pl.BlockSpec(memory_space=pl.ANY)


def call(body, ins, outs, scratch=(), flops=1_000_000, size=1_000_000):
    return pl.pallas_call(
        body,
        in_specs=ins,
        out_specs=[spec for _, _, spec in outs],
        out_shape=[
            pltpu.HBM(shape, kind)
            if spec.memory_space is pl.ANY
            else jax.ShapeDtypeStruct(shape, kind)
            for shape, kind, spec in outs
        ],
        scratch_shapes=list(scratch),
        compiler_params=pltpu.CompilerParams(vmem_limit_bytes=VMEM_BYTES),
        cost_estimate=pl.CostEstimate(flops=flops, bytes_accessed=size, transcendentals=0),
    )


def start_all(pairs, sems):
    copies = [pltpu.make_async_copy(src, dst, sems.at[i]) for i, (src, dst) in enumerate(pairs)]
    for copy in copies:
        copy.start()
    return copies


def stay(value):
    return pltpu.with_memory_space_constraint(value, pltpu.HBM)


def pack_body(hubs, feats, wanted, out):
    for k in range(PIECES):
        low = feats[:HALF, k * PIECE : (k + 1) * PIECE]
        high = feats[HALF:, k * PIECE : (k + 1) * PIECE]
        out[k * HALF : (k + 1) * HALF, :] = jnp.concatenate([low, high], axis=1)
    node = lax.broadcasted_iota(jnp.int32, (8, ROWS), 1)
    which = lax.broadcasted_iota(jnp.int32, (8, ROWS), 0)
    hub = jnp.where(which == 0, hubs[0, 0], hubs[0, 1])
    pick = ((node == hub) & (which < 2)).astype(BF)
    rows = dot(pick, feats[...], NT)
    hub_row = jnp.concatenate([rows[0:1], rows[1:2]], axis=1)
    place = lax.broadcasted_iota(jnp.int32, (16, 128), 0)
    extra = jnp.where(
        place == 0,
        jnp.broadcast_to(wanted[...].astype(F32), (16, 128)),
        jnp.where(place == 1, jnp.broadcast_to(hub_row, (16, 128)), 0.0),
    )
    out[DENSE:, :] = extra.astype(BF)


def pick_body(piece, gathered, out, held, sems):
    place = lax.broadcasted_iota(jnp.int32, (16, 128), 0)
    extra = jnp.zeros((16, 128), F32)
    for s in range(FAR):
        tail = gathered[s, DENSE:, :].astype(F32)
        extra = jnp.where(place == s, jnp.broadcast_to(tail[1:2], (16, 128)), extra)
    extra = extra.astype(BF)
    copies = []
    for n in range(NEAR):
        for s in range(FAR):
            start = pl.multiple_of(piece[s, ORDER[n]] * HALF, HALF)
            held[n, s * HALF : (s + 1) * HALF, :] = gathered[s, pl.ds(start, HALF), :]
        held[n, FAR * HALF :, :] = extra
        copies.append(pltpu.make_async_copy(held.at[n], out.at[n], sems.at[n]))
        copies[-1].start()
    for copy in copies:
        copy.wait()


def twice(tile):
    zero = jnp.zeros_like(tile)
    return jnp.concatenate(
        [jnp.concatenate([tile, zero], axis=1), jnp.concatenate([zero, tile], axis=1)], axis=0
    )


def forward_body(target, came, remote, feats, adj, local_far, out, local, total, sem):
    fetch = pltpu.make_async_copy(local_far, local, sem)
    fetch.start()
    total[...] = jnp.zeros_like(total)

    for s in range(FAR):
        for first in range(0, NEAR, 8):
            parts = []
            for n in range(first, first + 8):
                q = s * NEAR + ORDER[n]
                parts.append(dot(came[n, s * HALF : (s + 1) * HALF, :], twice(remote[q])))
            for n in range(first, first + 8):
                total[target[s * NEAR + ORDER[n]]] += parts[n - first]
    fetch.wait()
    hub_rows = jnp.concatenate([came[SLOT[n], FAR * HALF :, :][:8] for n in range(NEAR)], axis=0)
    hub_rows = jnp.concatenate([hub_rows[:, :FEAT], hub_rows[:, FEAT:]], axis=0)
    hub = dot(hub_rows, adj[...], TN)
    for b in range(BLOCKS):
        cols = slice(b * BLK, (b + 1) * BLK)
        tiles = jnp.concatenate([total[b, :, :BLK], total[b, :, BLK:]], axis=0)
        own = dot(feats[:, cols], local[b])
        value = (own + tiles + hub[:, cols]).astype(BF)
        for c in range(COLS):
            out[c, :, cols] = value


def middle_body(
    col,
    target,
    agg,
    remote,
    weight,
    cot,
    local,
    adj,
    output,
    back,
    own_grad,
    grad,
    pick,
):
    scale = 0.7978845608028654
    mine = pl.multiple_of(col[0] * FEAT, FEAT)
    for c in range(COLS):
        pre = dot(weight[:, c * FEAT : (c + 1) * FEAT], agg[...], TN)
        square = pre * pre
        bend = jnp.tanh(scale * (pre + 0.044715 * (square * pre)))
        half = 0.5 * (1.0 + bend)
        slope = half + 0.5 * pre * (1.0 - bend * bend) * (
            scale * (1.0 + 3.0 * 0.044715 * square)
        )
        grad[c * FEAT : (c + 1) * FEAT, :] = (
            cot[c * FEAT : (c + 1) * FEAT, :].astype(F32) * slope
        ).astype(BF)

        @pl.when(col[0] == c)
        def _():
            output[...] = (pre * half).astype(BF)

    grad_agg = dot(weight[pl.ds(mine, FEAT), :], grad[...]).astype(BF)
    weight_grad = dot(agg[pl.ds(mine, FEAT), :], grad[...], NT)
    for b in range(BLOCKS):
        cols = slice(b * BLK, (b + 1) * BLK)
        pick[b] = grad_agg[:, cols]
        own_grad[:, cols] = dot(grad_agg[:, cols], local[b], NT)
    pick[BLOCKS] = jnp.zeros((FEAT, BLK), BF)
    hub = dot(adj[...], grad_agg, NT)
    hub = jnp.concatenate([hub[:PEERS], hub[PEERS:]], axis=1)
    for n in range(NEAR):
        m = ORDER[n]
        i, j = n // 2, n % 2
        tile = weight_grad[i * 8 : (i + 1) * 8, j * 128 : (j + 1) * 128]
        back[n, FAR * HALF :, :] = jnp.concatenate([hub[m * 8 : (m + 1) * 8], tile], axis=0).astype(BF)

    for s in range(FAR):
        for n in range(NEAR):
            q = s * NEAR + ORDER[n]
            tile = dot(pick[target[q]], remote[q], NT)
            tile = jnp.concatenate([tile[:HALF], tile[HALF:]], axis=1)
            back[n, s * HALF : (s + 1) * HALF, :] = tile.astype(BF)


def gather_body(place, piece, came, out, total):
    slot = [slot_of(place[0], s) for s in range(FAR)]
    total[...] = jnp.zeros_like(total)
    extra = jnp.zeros((16, 128), F32)
    for n in range(NEAR):
        extra += came[n, FAR * HALF :, :].astype(F32)
    for s in range(FAR):
        hub = jnp.broadcast_to(extra[s : s + 1], (8, 128))
        out[slot[s], DENSE:, :] = jnp.concatenate([hub, extra[8:]], axis=0).astype(BF)

    for s in range(FAR):
        for n in range(NEAR):
            at = pl.multiple_of(piece[s, ORDER[n]] * HALF, HALF)
            total[s, pl.ds(at, HALF), :] += came[n, s * HALF : (s + 1) * HALF, :].astype(F32)
        out[slot[s], :DENSE, :] = total[s].astype(BF)


def chunk_body(came, chunk):
    tail = came[0, DENSE:, :].astype(F32)
    for s in range(1, FAR):
        tail += came[s, DENSE:, :].astype(F32)
    for n in range(NEAR):
        chunk[n] = tail[8:]


def final_body(hubs, came, own_grad, out):
    total = came[0].astype(F32)
    for s in range(1, FAR):
        total += came[s].astype(F32)
    node = lax.broadcasted_iota(jnp.int32, (8, ROWS), 1)
    which = lax.broadcasted_iota(jnp.int32, (8, ROWS), 0)
    hub = jnp.where(which == 0, hubs[0, 0], hubs[0, 1])
    pick = ((node == hub) & (which < 2)).astype(F32)
    row = total[DENSE : DENSE + 8]
    place = lax.broadcasted_iota(jnp.int32, (8, FEAT), 0)
    values = jnp.where(place == 0, row[:, :FEAT], row[:, FEAT:])
    hub_grad = lax.dot_general(
        values, pick, TN, preferred_element_type=F32, precision=lax.Precision.HIGHEST
    )
    for k in range(0, PIECES, 2):
        cols = slice(k * PIECE, (k + 2) * PIECE)
        a, b = total[k * HALF : (k + 1) * HALF], total[(k + 1) * HALF : (k + 2) * HALF]
        low = jnp.concatenate([a[:, :PIECE], b[:, :PIECE]], axis=1)
        high = jnp.concatenate([a[:, PIECE:], b[:, PIECE:]], axis=1)
        tiles = jnp.concatenate([low, high], axis=0)
        out[:, cols] = (own_grad[:, cols] + tiles + hub_grad[:, cols]).astype(BF)


def exchange(values, axis, groups=None):
    return lax.all_to_all(
        values,
        axis,
        split_axis=0,
        concat_axis=0,
        tiled=True,
        axis_index_groups=groups,
    )


def shards(
    features,
    send_pieces,
    remote_target,
    remote_count,
    local_values,
    remote_values,
    hub_rows,
    hub_adjacency,
    weight,
    cotangent,
):
    row = lax.axis_index("row").astype(jnp.int32)
    far, near = row // NEAR, row % NEAR
    place = place_of(near).reshape(1)
    col = lax.axis_index("col").astype(jnp.int32).reshape(1)
    target = jnp.where(
        jnp.arange(PEERS, dtype=jnp.int32) < remote_count[0], remote_target[0], BLOCKS
    )
    adj = (
        hub_adjacency.reshape(FAR, NEAR, 2, ROWS).transpose(2, 1, 0, 3).reshape(2 * PEERS, ROWS)
    )
    (packed,) = call(pack_body, [smem(), vmem(), vmem()], [((OUT_ROWS, 128), BF, vmem())])(
        stay(hub_rows), stay(features), stay(send_pieces)
    )
    gathered = lax.all_gather(packed, "row", axis=0, axis_index_groups=FAR_IDS)
    piece = lax.dynamic_slice(
        gathered[:, DENSE, :], (jnp.int32(0), far * NEAR), (FAR, NEAR)
    ).astype(jnp.int32)
    near_all = (NEAR, NEAR_ROWS, 128)
    (picked,) = call(
        pick_body,
        [smem(), vmem()],
        [(near_all, BF, away())],
        [pltpu.VMEM(near_all, BF), pltpu.SemaphoreType.DMA((NEAR,))],
    )(piece, gathered)
    picked, cotangent = lax.optimization_barrier((picked, cotangent))
    came = exchange(picked, "row", NEAR_GROUPS)
    cot = lax.all_gather(cotangent, "col", axis=0, tiled=True)
    came, cot, col, place = lax.optimization_barrier((came, cot, col, place))
    (agg,) = call(
        forward_body,
        [smem()] + [vmem()] * 4 + [away()],
        [((COLS, FEAT, ROWS), BF, vmem())],
        [
            pltpu.VMEM((BLOCKS, BLK, BLK), BF),
            pltpu.VMEM((BLOCKS + 1, HALF, 2 * BLK), F32),
            pltpu.SemaphoreType.DMA,
        ],
    )(target, came, remote_values, features, adj, stay(local_values))
    wide = (COLS * FEAT, ROWS)
    agg = exchange(agg, "col").reshape(wide)
    output, back, own_grad = call(
        middle_body,
        [smem(), smem()] + [vmem()] * 6,
        [((FEAT, ROWS), BF, vmem()), (near_all, BF, vmem()), ((FEAT, ROWS), F32, vmem())],
        [pltpu.VMEM(wide, BF), pltpu.VMEM((BLOCKS + 1, FEAT, BLK), BF)],
    )(col, target, agg, remote_values, weight, cot, local_values, adj)
    back = exchange(back, "row", NEAR_GROUPS)
    far_all = (FAR, BACK_ROWS, 128)
    (sums,) = call(
        gather_body,
        [smem(), smem(), vmem()],
        [(far_all, BF, vmem())],
        [pltpu.VMEM((FAR, DENSE, 128), F32)],
    )(place, piece, back)
    sums = exchange(sums, "row", FAR_GROUPS)
    (chunk,) = call(chunk_body, [vmem()], [((NEAR, 8, 128), F32, vmem())])(sums)
    tiles = exchange(chunk, "row", NEAR_GROUPS)
    (grad_input,) = call(
        final_body, [smem(), vmem(), vmem()], [((FEAT, ROWS), BF, vmem())]
    )(stay(hub_rows), sums, own_grad)
    weight_grad = tiles.reshape(8, 2, 8, 128).transpose(0, 2, 1, 3).reshape(FEAT, 256)
    return (output, grad_input, weight_grad)


def solution(mesh):
    row = "row"
    placed = (
        P("col", row),
        P(row, None),
        P(row, None),
        P(row),
        P(row, None, None),
        P(row, None, None),
        P(row, None),
        P(None, row),
        P(),
        P("col", row),
    )
    return jax.shard_map(
        shards,
        mesh=mesh,
        in_specs=placed,
        out_specs=(P("col", row), P("col", row), P("col", None)),
        check_vma=False,
    )
```

```python
import jax
import jax.numpy as jnp
from jax import lax
from jax.experimental import pallas as pl
from jax.experimental.pallas import tpu as pltpu
from jax.sharding import PartitionSpec as P

BF = jnp.bfloat16
F32 = jnp.float32

FAR = 8
NEAR = 16
COLS = 4
PEERS = FAR * NEAR
FEAT = 64
HALF = FEAT // 2
ROWS = 512
BLK = 128
BLOCKS = ROWS // BLK
PIECE = 64
PIECES = ROWS // PIECE
DENSE = PIECES * HALF
OUT_ROWS = DENSE + 16
NEAR_ROWS = FAR * HALF + 16
BACK_ROWS = NEAR_ROWS
VMEM_BYTES = 30 * 1024 * 1024
ORDER = (7, 0, 12, 3, 9, 14, 5, 10, 1, 15, 6, 2, 13, 8, 4, 11)
FAR_ORDERS = (
    (6, 2, 7, 0, 5, 3, 1, 4),
    (6, 1, 3, 0, 5, 4, 2, 7),
    (0, 7, 6, 2, 1, 5, 3, 4),
    (5, 6, 3, 2, 0, 7, 4, 1),
)
FAR_SLOTS = tuple(tuple(order.index(s) for s in range(FAR)) for order in FAR_ORDERS)
NEAR_IDS = tuple(tuple(f * NEAR + n for n in range(NEAR)) for f in range(FAR))
FAR_IDS = tuple(tuple(f * NEAR + n for f in range(FAR)) for n in range(NEAR))
NEAR_GROUPS = tuple(tuple(ids[n] for n in ORDER) for ids in NEAR_IDS)


def place_of(near):
    return 2 * (near // 8) + near % 2


def slot_of(place, s):
    chosen = jnp.int32(FAR_SLOTS[0][s])
    for other in range(1, len(FAR_SLOTS)):
        chosen = jnp.where(place == other, FAR_SLOTS[other][s], chosen)
    return chosen


FAR_GROUPS = tuple(
    tuple(FAR_IDS[n][f] for f in FAR_ORDERS[place_of(n)]) for n in range(NEAR)
)
SLOT = tuple(ORDER.index(n) for n in range(NEAR))

NT = (((1,), (1,)), ((), ()))
TN = (((0,), (0,)), ((), ()))
NN = (((1,), (0,)), ((), ()))


def dot(left, right, dims=NN):
    return lax.dot_general(left, right, dims, preferred_element_type=F32)


def vmem():
    return pl.BlockSpec(memory_space=pltpu.VMEM)


def smem():
    return pl.BlockSpec(memory_space=pltpu.SMEM)


def away():
    return pl.BlockSpec(memory_space=pl.ANY)


def call(body, ins, outs, scratch=(), flops=1_000_000, size=1_000_000):
    return pl.pallas_call(
        body,
        in_specs=ins,
        out_specs=[spec for _, _, spec in outs],
        out_shape=[
            pltpu.HBM(shape, kind)
            if spec.memory_space is pl.ANY
            else jax.ShapeDtypeStruct(shape, kind)
            for shape, kind, spec in outs
        ],
        scratch_shapes=list(scratch),
        compiler_params=pltpu.CompilerParams(vmem_limit_bytes=VMEM_BYTES),
        cost_estimate=pl.CostEstimate(flops=flops, bytes_accessed=size, transcendentals=0),
    )


def start_all(pairs, sems):
    copies = [pltpu.make_async_copy(src, dst, sems.at[i]) for i, (src, dst) in enumerate(pairs)]
    for copy in copies:
        copy.start()
    return copies


def stay(value):
    return pltpu.with_memory_space_constraint(value, pltpu.HBM)


def pack_body(hubs, feats, wanted, out):
    for k in range(PIECES):
        low = feats[:HALF, k * PIECE : (k + 1) * PIECE]
        high = feats[HALF:, k * PIECE : (k + 1) * PIECE]
        out[k * HALF : (k + 1) * HALF, :] = jnp.concatenate([low, high], axis=1)
    node = lax.broadcasted_iota(jnp.int32, (8, ROWS), 1)
    which = lax.broadcasted_iota(jnp.int32, (8, ROWS), 0)
    hub = jnp.where(which == 0, hubs[0, 0], hubs[0, 1])
    pick = ((node == hub) & (which < 2)).astype(BF)
    rows = dot(pick, feats[...], NT)
    hub_row = jnp.concatenate([rows[0:1], rows[1:2]], axis=1)
    place = lax.broadcasted_iota(jnp.int32, (16, 128), 0)
    extra = jnp.where(
        place == 0,
        jnp.broadcast_to(wanted[...].astype(F32), (16, 128)),
        jnp.where(place == 1, jnp.broadcast_to(hub_row, (16, 128)), 0.0),
    )
    out[DENSE:, :] = extra.astype(BF)


def pick_body(piece, gathered, out, held, sems):
    place = lax.broadcasted_iota(jnp.int32, (16, 128), 0)
    extra = jnp.zeros((16, 128), F32)
    for s in range(FAR):
        tail = gathered[s, DENSE:, :].astype(F32)
        extra = jnp.where(place == s, jnp.broadcast_to(tail[1:2], (16, 128)), extra)
    extra = extra.astype(BF)
    copies = []
    for n in range(NEAR):
        for s in range(FAR):
            start = pl.multiple_of(piece[s, ORDER[n]] * HALF, HALF)
            held[n, s * HALF : (s + 1) * HALF, :] = gathered[s, pl.ds(start, HALF), :]
        held[n, FAR * HALF :, :] = extra
        copies.append(pltpu.make_async_copy(held.at[n], out.at[n], sems.at[n]))
        copies[-1].start()
    for copy in copies:
        copy.wait()


def twice(tile):
    zero = jnp.zeros_like(tile)
    return jnp.concatenate(
        [jnp.concatenate([tile, zero], axis=1), jnp.concatenate([zero, tile], axis=1)], axis=0
    )


def forward_body(
    col,
    target,
    came,
    remote,
    feats,
    adj,
    local_far,
    cot_0,
    cot_1,
    cot_2,
    cot_3,
    out,
    cot,
    local,
    total,
    sems,
):
    pairs = [(local_far, local)]
    for hop, value in enumerate((cot_0, cot_1, cot_2, cot_3)):
        source = lax.rem(col[0] + COLS - hop, COLS)
        pairs.append((value, cot.at[pl.ds(pl.multiple_of(source * FEAT, FEAT), FEAT)]))
    copies = start_all(pairs, sems)
    total[...] = jnp.zeros_like(total)

    for s in range(FAR):
        for first in range(0, NEAR, 8):
            parts = []
            for n in range(first, first + 8):
                q = s * NEAR + ORDER[n]
                parts.append(dot(came[n, s * HALF : (s + 1) * HALF, :], twice(remote[q])))
            for n in range(first, first + 8):
                total[target[s * NEAR + ORDER[n]]] += parts[n - first]
    for copy in copies:
        copy.wait()
    hub_rows = jnp.concatenate([came[SLOT[n], FAR * HALF :, :][:8] for n in range(NEAR)], axis=0)
    hub_rows = jnp.concatenate([hub_rows[:, :FEAT], hub_rows[:, FEAT:]], axis=0)
    hub = dot(hub_rows, adj[...], TN)
    for b in range(BLOCKS):
        cols = slice(b * BLK, (b + 1) * BLK)
        tiles = jnp.concatenate([total[b, :, :BLK], total[b, :, BLK:]], axis=0)
        own = dot(feats[:, cols], local[b])
        value = (own + tiles + hub[:, cols]).astype(BF)
        for c in range(COLS):
            out[c, :, cols] = value


def middle_body(
    col,
    target,
    agg,
    remote,
    weight,
    local,
    adj,
    cot,
    output,
    back,
    own_grad,
    grad,
    pick,
):
    scale = 0.7978845608028654
    mine = pl.multiple_of(col[0] * FEAT, FEAT)
    for c in range(COLS):
        pre = dot(weight[:, c * FEAT : (c + 1) * FEAT], agg[...], TN)
        square = pre * pre
        bend = jnp.tanh(scale * (pre + 0.044715 * (square * pre)))
        half = 0.5 * (1.0 + bend)
        slope = half + 0.5 * pre * (1.0 - bend * bend) * (
            scale * (1.0 + 3.0 * 0.044715 * square)
        )
        grad[c * FEAT : (c + 1) * FEAT, :] = (
            cot[c * FEAT : (c + 1) * FEAT, :].astype(F32) * slope
        ).astype(BF)

        @pl.when(col[0] == c)
        def _():
            output[...] = (pre * half).astype(BF)

    grad_agg = dot(weight[pl.ds(mine, FEAT), :], grad[...]).astype(BF)
    weight_grad = dot(agg[pl.ds(mine, FEAT), :], grad[...], NT)
    for b in range(BLOCKS):
        cols = slice(b * BLK, (b + 1) * BLK)
        pick[b] = grad_agg[:, cols]
        own_grad[:, cols] = dot(grad_agg[:, cols], local[b], NT)
    pick[BLOCKS] = jnp.zeros((FEAT, BLK), BF)
    hub = dot(adj[...], grad_agg, NT)
    hub = jnp.concatenate([hub[:PEERS], hub[PEERS:]], axis=1)
    for n in range(NEAR):
        m = ORDER[n]
        i, j = n // 2, n % 2
        tile = weight_grad[i * 8 : (i + 1) * 8, j * 128 : (j + 1) * 128]
        back[n, FAR * HALF :, :] = jnp.concatenate([hub[m * 8 : (m + 1) * 8], tile], axis=0).astype(BF)

    for s in range(FAR):
        for n in range(NEAR):
            q = s * NEAR + ORDER[n]
            tile = dot(pick[target[q]], remote[q], NT)
            tile = jnp.concatenate([tile[:HALF], tile[HALF:]], axis=1)
            back[n, s * HALF : (s + 1) * HALF, :] = tile.astype(BF)


def gather_body(place, piece, came, out, total):
    slot = [slot_of(place[0], s) for s in range(FAR)]
    total[...] = jnp.zeros_like(total)
    extra = jnp.zeros((16, 128), F32)
    for n in range(NEAR):
        extra += came[n, FAR * HALF :, :].astype(F32)
    for s in range(FAR):
        hub = jnp.broadcast_to(extra[s : s + 1], (8, 128))
        out[slot[s], DENSE:, :] = jnp.concatenate([hub, extra[8:]], axis=0).astype(BF)

    for s in range(FAR):
        for n in range(NEAR):
            at = pl.multiple_of(piece[s, ORDER[n]] * HALF, HALF)
            total[s, pl.ds(at, HALF), :] += came[n, s * HALF : (s + 1) * HALF, :].astype(F32)
        out[slot[s], :DENSE, :] = total[s].astype(BF)


def chunk_body(came, chunk):
    tail = came[0, DENSE:, :].astype(F32)
    for s in range(1, FAR):
        tail += came[s, DENSE:, :].astype(F32)
    for n in range(NEAR):
        chunk[n] = tail[8:]


def final_body(hubs, came, own_grad, out):
    total = came[0].astype(F32)
    for s in range(1, FAR):
        total += came[s].astype(F32)
    node = lax.broadcasted_iota(jnp.int32, (8, ROWS), 1)
    which = lax.broadcasted_iota(jnp.int32, (8, ROWS), 0)
    hub = jnp.where(which == 0, hubs[0, 0], hubs[0, 1])
    pick = ((node == hub) & (which < 2)).astype(F32)
    row = total[DENSE : DENSE + 8]
    place = lax.broadcasted_iota(jnp.int32, (8, FEAT), 0)
    values = jnp.where(place == 0, row[:, :FEAT], row[:, FEAT:])
    hub_grad = lax.dot_general(
        values, pick, TN, preferred_element_type=F32, precision=lax.Precision.HIGHEST
    )
    for k in range(0, PIECES, 2):
        cols = slice(k * PIECE, (k + 2) * PIECE)
        a, b = total[k * HALF : (k + 1) * HALF], total[(k + 1) * HALF : (k + 2) * HALF]
        low = jnp.concatenate([a[:, :PIECE], b[:, :PIECE]], axis=1)
        high = jnp.concatenate([a[:, PIECE:], b[:, PIECE:]], axis=1)
        tiles = jnp.concatenate([low, high], axis=0)
        out[:, cols] = (own_grad[:, cols] + tiles + hub_grad[:, cols]).astype(BF)


def exchange(values, axis, groups=None):
    return lax.all_to_all(
        values,
        axis,
        split_axis=0,
        concat_axis=0,
        tiled=True,
        axis_index_groups=groups,
    )


def shards(
    features,
    send_pieces,
    remote_target,
    remote_count,
    local_values,
    remote_values,
    hub_rows,
    hub_adjacency,
    weight,
    cotangent,
):
    row = lax.axis_index("row").astype(jnp.int32)
    far, near = row // NEAR, row % NEAR
    place = place_of(near).reshape(1)
    col = lax.axis_index("col").astype(jnp.int32).reshape(1)
    target = jnp.where(
        jnp.arange(PEERS, dtype=jnp.int32) < remote_count[0], remote_target[0], BLOCKS
    )
    adj = (
        hub_adjacency.reshape(FAR, NEAR, 2, ROWS).transpose(2, 1, 0, 3).reshape(2 * PEERS, ROWS)
    )
    (packed,) = call(pack_body, [smem(), vmem(), vmem()], [((OUT_ROWS, 128), BF, vmem())])(
        stay(hub_rows), stay(features), stay(send_pieces)
    )
    gathered = lax.all_gather(packed, "row", axis=0, axis_index_groups=FAR_IDS)
    piece = lax.dynamic_slice(
        gathered[:, DENSE, :], (jnp.int32(0), far * NEAR), (FAR, NEAR)
    ).astype(jnp.int32)
    near_all = (NEAR, NEAR_ROWS, 128)
    (picked,) = call(
        pick_body,
        [smem(), vmem()],
        [(near_all, BF, away())],
        [pltpu.VMEM(near_all, BF), pltpu.SemaphoreType.DMA((NEAR,))],
    )(piece, gathered)
    picked, cotangent = lax.optimization_barrier((picked, cotangent))
    came = exchange(picked, "row", NEAR_GROUPS)
    cots = [cotangent]
    for hop in range(1, COLS):
        turn = [(c, (c + hop) % COLS) for c in range(COLS)]
        cots.append(lax.ppermute(cotangent, "col", turn))
    came, cots, col, place = lax.optimization_barrier((came, cots, col, place))
    wide = (COLS * FEAT, ROWS)
    agg, cot = call(
        forward_body,
        [smem(), smem()] + [vmem()] * 4 + [away()] * 5,
        [((COLS, FEAT, ROWS), BF, vmem()), (wide, BF, vmem())],
        [
            pltpu.VMEM((BLOCKS, BLK, BLK), BF),
            pltpu.VMEM((BLOCKS + 1, HALF, 2 * BLK), F32),
            pltpu.SemaphoreType.DMA((1 + COLS,)),
        ],
    )(col, target, came, remote_values, features, adj, *map(stay, (local_values, *cots)))
    agg = exchange(agg, "col").reshape(wide)
    output, back, own_grad = call(
        middle_body,
        [smem(), smem()] + [vmem()] * 6,
        [((FEAT, ROWS), BF, vmem()), (near_all, BF, vmem()), ((FEAT, ROWS), F32, vmem())],
        [pltpu.VMEM(wide, BF), pltpu.VMEM((BLOCKS + 1, FEAT, BLK), BF)],
    )(col, target, agg, remote_values, weight, local_values, adj, cot)
    back = exchange(back, "row", NEAR_GROUPS)
    far_all = (FAR, BACK_ROWS, 128)
    (sums,) = call(
        gather_body,
        [smem(), smem(), vmem()],
        [(far_all, BF, vmem())],
        [pltpu.VMEM((FAR, DENSE, 128), F32)],
    )(place, piece, back)
    sums = exchange(sums, "row", FAR_GROUPS)
    (chunk,) = call(chunk_body, [vmem()], [((NEAR, 8, 128), F32, vmem())])(sums)
    tiles = exchange(chunk, "row", NEAR_GROUPS)
    (grad_input,) = call(
        final_body, [smem(), vmem(), vmem()], [((FEAT, ROWS), BF, vmem())]
    )(stay(hub_rows), sums, own_grad)
    weight_grad = tiles.reshape(8, 2, 8, 128).transpose(0, 2, 1, 3).reshape(FEAT, 256)
    return (output, grad_input, weight_grad)


def solution(mesh):
    row = "row"
    placed = (
        P("col", row),
        P(row, None),
        P(row, None),
        P(row),
        P(row, None, None),
        P(row, None, None),
        P(row, None),
        P(None, row),
        P(),
        P("col", row),
    )
    return jax.shard_map(
        shards,
        mesh=mesh,
        in_specs=placed,
        out_specs=(P("col", row), P("col", row), P("col", None)),
        check_vma=False,
    )
```

```python
import jax
import jax.numpy as jnp
from jax import lax
from jax.experimental import pallas as pl
from jax.experimental.pallas import tpu as pltpu
from jax.sharding import PartitionSpec as P

BF = jnp.bfloat16
F32 = jnp.float32

FAR = 8
NEAR = 16
COLS = 4
PEERS = FAR * NEAR
FEAT = 64
HALF = FEAT // 2
ROWS = 512
BLK = 128
BLOCKS = ROWS // BLK
PIECE = 64
PIECES = ROWS // PIECE
DENSE = PIECES * HALF
OUT_ROWS = DENSE + 16
NEAR_ROWS = FAR * HALF + 16
BACK_ROWS = NEAR_ROWS
VMEM_BYTES = 30 * 1024 * 1024
ORDER = (1, 5, 4, 2, 8, 13, 14, 9, 0, 15, 11, 3, 6, 7, 10, 12)
FAR_ORDERS = (
    (6, 2, 7, 0, 5, 3, 1, 4),
    (6, 1, 3, 0, 5, 4, 2, 7),
    (0, 7, 6, 2, 1, 5, 3, 4),
    (5, 6, 3, 2, 0, 7, 4, 1),
)
FAR_SLOTS = tuple(tuple(order.index(s) for s in range(FAR)) for order in FAR_ORDERS)
NEAR_IDS = tuple(tuple(f * NEAR + n for n in range(NEAR)) for f in range(FAR))
FAR_IDS = tuple(tuple(f * NEAR + n for f in range(FAR)) for n in range(NEAR))
NEAR_GROUPS = tuple(tuple(ids[n] for n in ORDER) for ids in NEAR_IDS)


def place_of(near):
    return 2 * (near // 8) + near % 2


def slot_of(place, s):
    chosen = jnp.int32(FAR_SLOTS[0][s])
    for other in range(1, len(FAR_SLOTS)):
        chosen = jnp.where(place == other, FAR_SLOTS[other][s], chosen)
    return chosen


FAR_GROUPS = tuple(
    tuple(FAR_IDS[n][f] for f in FAR_ORDERS[place_of(n)]) for n in range(NEAR)
)
SLOT = tuple(ORDER.index(n) for n in range(NEAR))

NT = (((1,), (1,)), ((), ()))
TN = (((0,), (0,)), ((), ()))
NN = (((1,), (0,)), ((), ()))


def dot(left, right, dims=NN):
    return lax.dot_general(left, right, dims, preferred_element_type=F32)


def vmem():
    return pl.BlockSpec(memory_space=pltpu.VMEM)


def smem():
    return pl.BlockSpec(memory_space=pltpu.SMEM)


def away():
    return pl.BlockSpec(memory_space=pl.ANY)


def call(body, ins, outs, scratch=(), flops=1_000_000, size=1_000_000):
    return pl.pallas_call(
        body,
        in_specs=ins,
        out_specs=[spec for _, _, spec in outs],
        out_shape=[
            pltpu.HBM(shape, kind)
            if spec.memory_space is pl.ANY
            else jax.ShapeDtypeStruct(shape, kind)
            for shape, kind, spec in outs
        ],
        scratch_shapes=list(scratch),
        compiler_params=pltpu.CompilerParams(vmem_limit_bytes=VMEM_BYTES),
        cost_estimate=pl.CostEstimate(flops=flops, bytes_accessed=size, transcendentals=0),
    )


def start_all(pairs, sems):
    copies = [pltpu.make_async_copy(src, dst, sems.at[i]) for i, (src, dst) in enumerate(pairs)]
    for copy in copies:
        copy.start()
    return copies


def stay(value):
    return pltpu.with_memory_space_constraint(value, pltpu.HBM)


def pack_body(hubs, feats, wanted, out):
    for k in range(PIECES):
        low = feats[:HALF, k * PIECE : (k + 1) * PIECE]
        high = feats[HALF:, k * PIECE : (k + 1) * PIECE]
        out[k * HALF : (k + 1) * HALF, :] = jnp.concatenate([low, high], axis=1)
    node = lax.broadcasted_iota(jnp.int32, (8, ROWS), 1)
    which = lax.broadcasted_iota(jnp.int32, (8, ROWS), 0)
    hub = jnp.where(which == 0, hubs[0, 0], hubs[0, 1])
    pick = ((node == hub) & (which < 2)).astype(BF)
    rows = dot(pick, feats[...], NT)
    hub_row = jnp.concatenate([rows[0:1], rows[1:2]], axis=1)
    place = lax.broadcasted_iota(jnp.int32, (16, 128), 0)
    extra = jnp.where(
        place == 0,
        jnp.broadcast_to(wanted[...].astype(F32), (16, 128)),
        jnp.where(place == 1, jnp.broadcast_to(hub_row, (16, 128)), 0.0),
    )
    out[DENSE:, :] = extra.astype(BF)


def pick_body(piece, gathered, out, held, sems):
    place = lax.broadcasted_iota(jnp.int32, (16, 128), 0)
    extra = jnp.zeros((16, 128), F32)
    for s in range(FAR):
        tail = gathered[s, DENSE:, :].astype(F32)
        extra = jnp.where(place == s, jnp.broadcast_to(tail[1:2], (16, 128)), extra)
    extra = extra.astype(BF)
    copies = []
    for n in range(NEAR):
        for s in range(FAR):
            start = pl.multiple_of(piece[s, ORDER[n]] * HALF, HALF)
            held[n, s * HALF : (s + 1) * HALF, :] = gathered[s, pl.ds(start, HALF), :]
        held[n, FAR * HALF :, :] = extra
        copies.append(pltpu.make_async_copy(held.at[n], out.at[n], sems.at[n]))
        copies[-1].start()
    for copy in copies:
        copy.wait()


def twice(tile):
    zero = jnp.zeros_like(tile)
    return jnp.concatenate(
        [jnp.concatenate([tile, zero], axis=1), jnp.concatenate([zero, tile], axis=1)], axis=0
    )


def forward_body(
    col,
    target,
    came,
    remote,
    feats,
    adj,
    local_far,
    cot_0,
    cot_1,
    cot_2,
    cot_3,
    out,
    cot,
    local,
    total,
    sems,
):
    pairs = [(local_far, local)]
    for hop, value in enumerate((cot_0, cot_1, cot_2, cot_3)):
        source = lax.rem(col[0] + COLS - hop, COLS)
        pairs.append((value, cot.at[pl.ds(pl.multiple_of(source * FEAT, FEAT), FEAT)]))
    copies = start_all(pairs, sems)
    total[...] = jnp.zeros_like(total)

    def step(i, carry):
        for s in (4 * i + k for k in range(4)):
            start = pl.multiple_of(s * HALF, HALF)
            for first in range(0, NEAR, 8):
                parts = []
                for n in range(first, first + 8):
                    q = s * NEAR + ORDER[n]
                    parts.append(dot(came[n, pl.ds(start, HALF), :], twice(remote[q])))
                for n in range(first, first + 8):
                    total[target[s * NEAR + ORDER[n]]] += parts[n - first]
        return carry

    lax.fori_loop(0, FAR // 4, step, 0)
    for copy in copies:
        copy.wait()
    hub_rows = jnp.concatenate([came[SLOT[n], FAR * HALF :, :][:8] for n in range(NEAR)], axis=0)
    hub_rows = jnp.concatenate([hub_rows[:, :FEAT], hub_rows[:, FEAT:]], axis=0)
    hub = dot(hub_rows, adj[...], TN)
    for b in range(BLOCKS):
        cols = slice(b * BLK, (b + 1) * BLK)
        tiles = jnp.concatenate([total[b, :, :BLK], total[b, :, BLK:]], axis=0)
        own = dot(feats[:, cols], local[b])
        value = (own + tiles + hub[:, cols]).astype(BF)
        for c in range(COLS):
            out[c, :, cols] = value


def middle_body(
    col,
    target,
    agg,
    remote,
    weight,
    local,
    adj,
    cot,
    output,
    back,
    own_grad,
    grad,
    pick,
):
    scale = 0.7978845608028654
    mine = pl.multiple_of(col[0] * FEAT, FEAT)
    for c in range(COLS):
        pre = dot(weight[:, c * FEAT : (c + 1) * FEAT], agg[...], TN)
        square = pre * pre
        bend = jnp.tanh(scale * (pre + 0.044715 * (square * pre)))
        half = 0.5 * (1.0 + bend)
        slope = half + 0.5 * pre * (1.0 - bend * bend) * (
            scale * (1.0 + 3.0 * 0.044715 * square)
        )
        grad[c * FEAT : (c + 1) * FEAT, :] = (
            cot[c * FEAT : (c + 1) * FEAT, :].astype(F32) * slope
        ).astype(BF)

        @pl.when(col[0] == c)
        def _():
            output[...] = (pre * half).astype(BF)

    grad_agg = dot(weight[pl.ds(mine, FEAT), :], grad[...]).astype(BF)
    weight_grad = dot(agg[pl.ds(mine, FEAT), :], grad[...], NT)
    for b in range(BLOCKS):
        cols = slice(b * BLK, (b + 1) * BLK)
        pick[b] = grad_agg[:, cols]
        own_grad[:, cols] = dot(grad_agg[:, cols], local[b], NT)
    pick[BLOCKS] = jnp.zeros((FEAT, BLK), BF)
    hub = dot(adj[...], grad_agg, NT)
    hub = jnp.concatenate([hub[:PEERS], hub[PEERS:]], axis=1)
    for n in range(NEAR):
        m = ORDER[n]
        i, j = n // 2, n % 2
        tile = weight_grad[i * 8 : (i + 1) * 8, j * 128 : (j + 1) * 128]
        back[n, FAR * HALF :, :] = jnp.concatenate([hub[m * 8 : (m + 1) * 8], tile], axis=0).astype(BF)

    for s in range(FAR):
        for n in range(NEAR):
            q = s * NEAR + ORDER[n]
            tile = dot(pick[target[q]], remote[q], NT)
            tile = jnp.concatenate([tile[:HALF], tile[HALF:]], axis=1)
            back[n, s * HALF : (s + 1) * HALF, :] = tile.astype(BF)


def gather_body(place, piece, came, out, total):
    slot = [slot_of(place[0], s) for s in range(FAR)]
    total[...] = jnp.zeros_like(total)
    extra = jnp.zeros((16, 128), F32)
    for n in range(NEAR):
        extra += came[n, FAR * HALF :, :].astype(F32)
    for s in range(FAR):
        hub = jnp.broadcast_to(extra[s : s + 1], (8, 128))
        out[slot[s], DENSE:, :] = jnp.concatenate([hub, extra[8:]], axis=0).astype(BF)

    for s in range(FAR):
        for n in range(NEAR):
            at = pl.multiple_of(piece[s, ORDER[n]] * HALF, HALF)
            total[s, pl.ds(at, HALF), :] += came[n, s * HALF : (s + 1) * HALF, :].astype(F32)
        out[slot[s], :DENSE, :] = total[s].astype(BF)


def chunk_body(came, chunk):
    tail = came[0, DENSE:, :].astype(F32)
    for s in range(1, FAR):
        tail += came[s, DENSE:, :].astype(F32)
    for n in range(NEAR):
        chunk[n] = tail[8:]


def final_body(hubs, came, own_grad, out):
    total = came[0].astype(F32)
    for s in range(1, FAR):
        total += came[s].astype(F32)
    node = lax.broadcasted_iota(jnp.int32, (8, ROWS), 1)
    which = lax.broadcasted_iota(jnp.int32, (8, ROWS), 0)
    hub = jnp.where(which == 0, hubs[0, 0], hubs[0, 1])
    pick = ((node == hub) & (which < 2)).astype(F32)
    row = total[DENSE : DENSE + 8]
    place = lax.broadcasted_iota(jnp.int32, (8, FEAT), 0)
    values = jnp.where(place == 0, row[:, :FEAT], row[:, FEAT:])
    hub_grad = lax.dot_general(
        values, pick, TN, preferred_element_type=F32, precision=lax.Precision.HIGHEST
    )
    for k in range(0, PIECES, 2):
        cols = slice(k * PIECE, (k + 2) * PIECE)
        a, b = total[k * HALF : (k + 1) * HALF], total[(k + 1) * HALF : (k + 2) * HALF]
        low = jnp.concatenate([a[:, :PIECE], b[:, :PIECE]], axis=1)
        high = jnp.concatenate([a[:, PIECE:], b[:, PIECE:]], axis=1)
        tiles = jnp.concatenate([low, high], axis=0)
        out[:, cols] = (own_grad[:, cols] + tiles + hub_grad[:, cols]).astype(BF)


def exchange(values, axis, groups=None):
    return lax.all_to_all(
        values,
        axis,
        split_axis=0,
        concat_axis=0,
        tiled=True,
        axis_index_groups=groups,
    )


def shards(
    features,
    send_pieces,
    remote_target,
    remote_count,
    local_values,
    remote_values,
    hub_rows,
    hub_adjacency,
    weight,
    cotangent,
):
    row = lax.axis_index("row").astype(jnp.int32)
    far, near = row // NEAR, row % NEAR
    place = place_of(near).reshape(1)
    col = lax.axis_index("col").astype(jnp.int32).reshape(1)
    target = jnp.where(
        jnp.arange(PEERS, dtype=jnp.int32) < remote_count[0], remote_target[0], BLOCKS
    )
    adj = (
        hub_adjacency.reshape(FAR, NEAR, 2, ROWS).transpose(2, 1, 0, 3).reshape(2 * PEERS, ROWS)
    )
    (packed,) = call(pack_body, [smem(), vmem(), vmem()], [((OUT_ROWS, 128), BF, vmem())])(
        stay(hub_rows), stay(features), stay(send_pieces)
    )
    gathered = lax.all_gather(packed, "row", axis=0, axis_index_groups=FAR_IDS)
    piece = lax.dynamic_slice(
        gathered[:, DENSE, :], (jnp.int32(0), far * NEAR), (FAR, NEAR)
    ).astype(jnp.int32)
    near_all = (NEAR, NEAR_ROWS, 128)
    (picked,) = call(
        pick_body,
        [smem(), vmem()],
        [(near_all, BF, away())],
        [pltpu.VMEM(near_all, BF), pltpu.SemaphoreType.DMA((NEAR,))],
    )(piece, gathered)
    picked, cotangent = lax.optimization_barrier((picked, cotangent))
    came = exchange(picked, "row", NEAR_GROUPS)
    cots = [cotangent]
    for hop in range(1, COLS):
        turn = [(c, (c + hop) % COLS) for c in range(COLS)]
        cots.append(lax.ppermute(cotangent, "col", turn))
    came, cots, col, place = lax.optimization_barrier((came, cots, col, place))
    wide = (COLS * FEAT, ROWS)
    agg, cot = call(
        forward_body,
        [smem(), smem()] + [vmem()] * 4 + [away()] * 5,
        [((COLS, FEAT, ROWS), BF, vmem()), (wide, BF, vmem())],
        [
            pltpu.VMEM((BLOCKS, BLK, BLK), BF),
            pltpu.VMEM((BLOCKS + 1, HALF, 2 * BLK), F32),
            pltpu.SemaphoreType.DMA((1 + COLS,)),
        ],
    )(col, target, came, remote_values, features, adj, *map(stay, (local_values, *cots)))
    agg = exchange(agg, "col").reshape(wide)
    output, back, own_grad = call(
        middle_body,
        [smem(), smem()] + [vmem()] * 6,
        [((FEAT, ROWS), BF, vmem()), (near_all, BF, vmem()), ((FEAT, ROWS), F32, vmem())],
        [pltpu.VMEM(wide, BF), pltpu.VMEM((BLOCKS + 1, FEAT, BLK), BF)],
    )(col, target, agg, remote_values, weight, local_values, adj, cot)
    back = exchange(back, "row", NEAR_GROUPS)
    far_all = (FAR, BACK_ROWS, 128)
    (sums,) = call(
        gather_body,
        [smem(), smem(), vmem()],
        [(far_all, BF, vmem())],
        [pltpu.VMEM((FAR, DENSE, 128), F32)],
    )(place, piece, back)
    sums = exchange(sums, "row", FAR_GROUPS)
    (chunk,) = call(chunk_body, [vmem()], [((NEAR, 8, 128), F32, vmem())])(sums)
    tiles = exchange(chunk, "row", NEAR_GROUPS)
    (grad_input,) = call(
        final_body, [smem(), vmem(), vmem()], [((FEAT, ROWS), BF, vmem())]
    )(stay(hub_rows), sums, own_grad)
    weight_grad = tiles.reshape(8, 2, 8, 128).transpose(0, 2, 1, 3).reshape(FEAT, 256)
    return (output, grad_input, weight_grad)


def solution(mesh):
    row = "row"
    placed = (
        P("col", row),
        P(row, None),
        P(row, None),
        P(row),
        P(row, None, None),
        P(row, None, None),
        P(row, None),
        P(None, row),
        P(),
        P("col", row),
    )
    return jax.shard_map(
        shards,
        mesh=mesh,
        in_specs=placed,
        out_specs=(P("col", row), P("col", row), P("col", None)),
        check_vma=False,
    )
```

```python
import jax
import jax.numpy as jnp
from jax import lax
from jax.experimental import pallas as pl
from jax.experimental.pallas import tpu as pltpu
from jax.sharding import PartitionSpec as P

BF = jnp.bfloat16
F32 = jnp.float32

FAR = 8
NEAR = 16
COLS = 4
PEERS = FAR * NEAR
FEAT = 64
HALF = FEAT // 2
ROWS = 512
BLK = 128
BLOCKS = ROWS // BLK
PIECE = 64
PIECES = ROWS // PIECE
DENSE = PIECES * HALF
OUT_ROWS = DENSE + 16
NEAR_ROWS = FAR * HALF + 16
BACK_ROWS = NEAR_ROWS
VMEM_BYTES = 30 * 1024 * 1024
ORDER = (1, 5, 4, 2, 8, 13, 14, 9, 0, 15, 11, 3, 6, 7, 10, 12)
FAR_ORDERS = (
    (6, 2, 7, 0, 5, 3, 1, 4),
    (6, 1, 3, 0, 5, 4, 2, 7),
    (0, 7, 6, 2, 1, 5, 3, 4),
    (5, 6, 3, 2, 0, 7, 4, 1),
)
FAR_SLOTS = tuple(tuple(order.index(s) for s in range(FAR)) for order in FAR_ORDERS)
NEAR_IDS = tuple(tuple(f * NEAR + n for n in range(NEAR)) for f in range(FAR))
FAR_IDS = tuple(tuple(f * NEAR + n for f in range(FAR)) for n in range(NEAR))
NEAR_GROUPS = tuple(tuple(ids[n] for n in ORDER) for ids in NEAR_IDS)


def place_of(near):
    return 2 * (near // 8) + near % 2


def slot_of(place, s):
    chosen = jnp.int32(FAR_SLOTS[0][s])
    for other in range(1, len(FAR_SLOTS)):
        chosen = jnp.where(place == other, FAR_SLOTS[other][s], chosen)
    return chosen


FAR_GROUPS = tuple(
    tuple(FAR_IDS[n][f] for f in FAR_ORDERS[place_of(n)]) for n in range(NEAR)
)
SLOT = tuple(ORDER.index(n) for n in range(NEAR))

NT = (((1,), (1,)), ((), ()))
TN = (((0,), (0,)), ((), ()))
NN = (((1,), (0,)), ((), ()))


def dot(left, right, dims=NN):
    return lax.dot_general(left, right, dims, preferred_element_type=F32)


def vmem():
    return pl.BlockSpec(memory_space=pltpu.VMEM)


def smem():
    return pl.BlockSpec(memory_space=pltpu.SMEM)


def away():
    return pl.BlockSpec(memory_space=pl.ANY)


def call(body, ins, outs, scratch=(), flops=1_000_000, size=1_000_000):
    return pl.pallas_call(
        body,
        in_specs=ins,
        out_specs=[spec for _, _, spec in outs],
        out_shape=[
            pltpu.HBM(shape, kind)
            if spec.memory_space is pl.ANY
            else jax.ShapeDtypeStruct(shape, kind)
            for shape, kind, spec in outs
        ],
        scratch_shapes=list(scratch),
        compiler_params=pltpu.CompilerParams(vmem_limit_bytes=VMEM_BYTES),
        cost_estimate=pl.CostEstimate(flops=flops, bytes_accessed=size, transcendentals=0),
    )


def start_all(pairs, sems):
    copies = [pltpu.make_async_copy(src, dst, sems.at[i]) for i, (src, dst) in enumerate(pairs)]
    for copy in copies:
        copy.start()
    return copies


def stay(value):
    return pltpu.with_memory_space_constraint(value, pltpu.HBM)


def pack_body(hubs, feats, wanted, out):
    for k in range(PIECES):
        low = feats[:HALF, k * PIECE : (k + 1) * PIECE]
        high = feats[HALF:, k * PIECE : (k + 1) * PIECE]
        out[k * HALF : (k + 1) * HALF, :] = jnp.concatenate([low, high], axis=1)
    node = lax.broadcasted_iota(jnp.int32, (8, ROWS), 1)
    which = lax.broadcasted_iota(jnp.int32, (8, ROWS), 0)
    hub = jnp.where(which == 0, hubs[0, 0], hubs[0, 1])
    pick = ((node == hub) & (which < 2)).astype(BF)
    rows = dot(pick, feats[...], NT)
    hub_row = jnp.concatenate([rows[0:1], rows[1:2]], axis=1)
    place = lax.broadcasted_iota(jnp.int32, (16, 128), 0)
    extra = jnp.where(
        place == 0,
        jnp.broadcast_to(wanted[...].astype(F32), (16, 128)),
        jnp.where(place == 1, jnp.broadcast_to(hub_row, (16, 128)), 0.0),
    )
    out[DENSE:, :] = extra.astype(BF)


def pick_body(piece, gathered, out, held, sems):
    place = lax.broadcasted_iota(jnp.int32, (16, 128), 0)
    extra = jnp.zeros((16, 128), F32)
    for s in range(FAR):
        tail = gathered[s, DENSE:, :].astype(F32)
        extra = jnp.where(place == s, jnp.broadcast_to(tail[1:2], (16, 128)), extra)
    extra = extra.astype(BF)
    copies = []
    for n in range(NEAR):
        for s in range(FAR):
            start = pl.multiple_of(piece[s, ORDER[n]] * HALF, HALF)
            held[n, s * HALF : (s + 1) * HALF, :] = gathered[s, pl.ds(start, HALF), :]
        held[n, FAR * HALF :, :] = extra
        copies.append(pltpu.make_async_copy(held.at[n], out.at[n], sems.at[n]))
        copies[-1].start()
    for copy in copies:
        copy.wait()


def twice(tile):
    zero = jnp.zeros_like(tile)
    return jnp.concatenate(
        [jnp.concatenate([tile, zero], axis=1), jnp.concatenate([zero, tile], axis=1)], axis=0
    )


def forward_body(
    col,
    target,
    came,
    remote,
    feats,
    adj,
    local_far,
    cot_0,
    cot_1,
    cot_2,
    cot_3,
    out,
    cot,
    local,
    total,
    sems,
):
    pairs = [(local_far, local)]
    for hop, value in enumerate((cot_0, cot_1, cot_2, cot_3)):
        source = lax.rem(col[0] + COLS - hop, COLS)
        pairs.append((value, cot.at[pl.ds(pl.multiple_of(source * FEAT, FEAT), FEAT)]))
    copies = start_all(pairs, sems)
    total[...] = jnp.zeros_like(total)

    def step(i, carry):
        for s in (4 * i + k for k in range(4)):
            start = pl.multiple_of(s * HALF, HALF)
            for first in range(0, NEAR, 8):
                parts = []
                for n in range(first, first + 8):
                    q = s * NEAR + ORDER[n]
                    parts.append(dot(came[n, pl.ds(start, HALF), :], twice(remote[q])))
                for n in range(first, first + 8):
                    total[target[s * NEAR + ORDER[n]]] += parts[n - first]
        return carry

    lax.fori_loop(0, FAR // 4, step, 0)
    for copy in copies:
        copy.wait()
    hub_rows = jnp.concatenate([came[SLOT[n], FAR * HALF :, :][:8] for n in range(NEAR)], axis=0)
    hub_rows = jnp.concatenate([hub_rows[:, :FEAT], hub_rows[:, FEAT:]], axis=0)
    hub = dot(hub_rows, adj[...], TN)
    for b in range(BLOCKS):
        cols = slice(b * BLK, (b + 1) * BLK)
        tiles = jnp.concatenate([total[b, :, :BLK], total[b, :, BLK:]], axis=0)
        own = dot(feats[:, cols], local[b])
        value = (own + tiles + hub[:, cols]).astype(BF)
        for c in range(COLS):
            out[c, :, cols] = value


def middle_body(
    col,
    target,
    agg,
    remote,
    weight,
    local,
    adj,
    cot,
    output,
    back,
    own_grad,
    grad,
    pick,
):
    scale = 0.7978845608028654
    mine = pl.multiple_of(col[0] * FEAT, FEAT)
    for c in range(COLS):
        pre = dot(weight[:, c * FEAT : (c + 1) * FEAT], agg[...], TN)
        square = pre * pre
        bend = jnp.tanh(scale * (pre + 0.044715 * (square * pre)))
        half = 0.5 * (1.0 + bend)
        slope = half + 0.5 * pre * (1.0 - bend * bend) * (
            scale * (1.0 + 3.0 * 0.044715 * square)
        )
        grad[c * FEAT : (c + 1) * FEAT, :] = (
            cot[c * FEAT : (c + 1) * FEAT, :].astype(F32) * slope
        ).astype(BF)

        @pl.when(col[0] == c)
        def _():
            output[...] = (pre * half).astype(BF)

    grad_agg = dot(weight[pl.ds(mine, FEAT), :], grad[...]).astype(BF)
    weight_grad = dot(agg[pl.ds(mine, FEAT), :], grad[...], NT)
    for b in range(BLOCKS):
        cols = slice(b * BLK, (b + 1) * BLK)
        pick[b] = grad_agg[:, cols]
        own_grad[:, cols] = dot(grad_agg[:, cols], local[b], NT)
    pick[BLOCKS] = jnp.zeros((FEAT, BLK), BF)
    hub = dot(adj[...], grad_agg, NT)
    hub = jnp.concatenate([hub[:PEERS], hub[PEERS:]], axis=1)
    for n in range(NEAR):
        m = ORDER[n]
        i, j = n // 2, n % 2
        tile = weight_grad[i * 8 : (i + 1) * 8, j * 128 : (j + 1) * 128]
        back[n, FAR * HALF :, :] = jnp.concatenate([hub[m * 8 : (m + 1) * 8], tile], axis=0).astype(BF)

    def step(i, carry):
        for s in (4 * i + k for k in range(4)):
            start = pl.multiple_of(s * HALF, HALF)
            for n in range(NEAR):
                q = s * NEAR + ORDER[n]
                tile = dot(pick[target[q]], remote[q], NT)
                tile = jnp.concatenate([tile[:HALF], tile[HALF:]], axis=1)
                back[n, pl.ds(start, HALF), :] = tile.astype(BF)
        return carry

    lax.fori_loop(0, FAR // 4, step, 0)


def gather_body(place, piece, came, out, total):
    slot = [slot_of(place[0], s) for s in range(FAR)]
    total[...] = jnp.zeros_like(total)
    extra = jnp.zeros((16, 128), F32)
    for n in range(NEAR):
        extra += came[n, FAR * HALF :, :].astype(F32)
    for s in range(FAR):
        hub = jnp.broadcast_to(extra[s : s + 1], (8, 128))
        out[slot[s], DENSE:, :] = jnp.concatenate([hub, extra[8:]], axis=0).astype(BF)

    for s in range(FAR):
        for n in range(NEAR):
            at = pl.multiple_of(piece[s, ORDER[n]] * HALF, HALF)
            total[s, pl.ds(at, HALF), :] += came[n, s * HALF : (s + 1) * HALF, :].astype(F32)
        out[slot[s], :DENSE, :] = total[s].astype(BF)


def chunk_body(came, chunk):
    tail = came[0, DENSE:, :].astype(F32)
    for s in range(1, FAR):
        tail += came[s, DENSE:, :].astype(F32)
    for n in range(NEAR):
        chunk[n] = tail[8:]


def final_body(hubs, came, own_grad, out):
    total = came[0].astype(F32)
    for s in range(1, FAR):
        total += came[s].astype(F32)
    node = lax.broadcasted_iota(jnp.int32, (8, ROWS), 1)
    which = lax.broadcasted_iota(jnp.int32, (8, ROWS), 0)
    hub = jnp.where(which == 0, hubs[0, 0], hubs[0, 1])
    pick = ((node == hub) & (which < 2)).astype(F32)
    row = total[DENSE : DENSE + 8]
    place = lax.broadcasted_iota(jnp.int32, (8, FEAT), 0)
    values = jnp.where(place == 0, row[:, :FEAT], row[:, FEAT:])
    hub_grad = lax.dot_general(
        values, pick, TN, preferred_element_type=F32, precision=lax.Precision.HIGHEST
    )
    for k in range(0, PIECES, 2):
        cols = slice(k * PIECE, (k + 2) * PIECE)
        a, b = total[k * HALF : (k + 1) * HALF], total[(k + 1) * HALF : (k + 2) * HALF]
        low = jnp.concatenate([a[:, :PIECE], b[:, :PIECE]], axis=1)
        high = jnp.concatenate([a[:, PIECE:], b[:, PIECE:]], axis=1)
        tiles = jnp.concatenate([low, high], axis=0)
        out[:, cols] = (own_grad[:, cols] + tiles + hub_grad[:, cols]).astype(BF)


def exchange(values, axis, groups=None):
    return lax.all_to_all(
        values,
        axis,
        split_axis=0,
        concat_axis=0,
        tiled=True,
        axis_index_groups=groups,
    )


def shards(
    features,
    send_pieces,
    remote_target,
    remote_count,
    local_values,
    remote_values,
    hub_rows,
    hub_adjacency,
    weight,
    cotangent,
):
    row = lax.axis_index("row").astype(jnp.int32)
    far, near = row // NEAR, row % NEAR
    place = place_of(near).reshape(1)
    col = lax.axis_index("col").astype(jnp.int32).reshape(1)
    target = jnp.where(
        jnp.arange(PEERS, dtype=jnp.int32) < remote_count[0], remote_target[0], BLOCKS
    )
    adj = (
        hub_adjacency.reshape(FAR, NEAR, 2, ROWS).transpose(2, 1, 0, 3).reshape(2 * PEERS, ROWS)
    )
    (packed,) = call(pack_body, [smem(), vmem(), vmem()], [((OUT_ROWS, 128), BF, vmem())])(
        stay(hub_rows), stay(features), stay(send_pieces)
    )
    gathered = lax.all_gather(packed, "row", axis=0, axis_index_groups=FAR_IDS)
    piece = lax.dynamic_slice(
        gathered[:, DENSE, :], (jnp.int32(0), far * NEAR), (FAR, NEAR)
    ).astype(jnp.int32)
    near_all = (NEAR, NEAR_ROWS, 128)
    (picked,) = call(
        pick_body,
        [smem(), vmem()],
        [(near_all, BF, away())],
        [pltpu.VMEM(near_all, BF), pltpu.SemaphoreType.DMA((NEAR,))],
    )(piece, gathered)
    picked, cotangent = lax.optimization_barrier((picked, cotangent))
    came = exchange(picked, "row", NEAR_GROUPS)
    cots = [cotangent]
    for hop in range(1, COLS):
        turn = [(c, (c + hop) % COLS) for c in range(COLS)]
        cots.append(lax.ppermute(cotangent, "col", turn))
    came, cots, col, place = lax.optimization_barrier((came, cots, col, place))
    wide = (COLS * FEAT, ROWS)
    agg, cot = call(
        forward_body,
        [smem(), smem()] + [vmem()] * 4 + [away()] * 5,
        [((COLS, FEAT, ROWS), BF, vmem()), (wide, BF, vmem())],
        [
            pltpu.VMEM((BLOCKS, BLK, BLK), BF),
            pltpu.VMEM((BLOCKS + 1, HALF, 2 * BLK), F32),
            pltpu.SemaphoreType.DMA((1 + COLS,)),
        ],
    )(col, target, came, remote_values, features, adj, *map(stay, (local_values, *cots)))
    agg = exchange(agg, "col").reshape(wide)
    output, back, own_grad = call(
        middle_body,
        [smem(), smem()] + [vmem()] * 6,
        [((FEAT, ROWS), BF, vmem()), (near_all, BF, vmem()), ((FEAT, ROWS), F32, vmem())],
        [pltpu.VMEM(wide, BF), pltpu.VMEM((BLOCKS + 1, FEAT, BLK), BF)],
    )(col, target, agg, remote_values, weight, local_values, adj, cot)
    back = exchange(back, "row", NEAR_GROUPS)
    far_all = (FAR, BACK_ROWS, 128)
    (sums,) = call(
        gather_body,
        [smem(), smem(), vmem()],
        [(far_all, BF, vmem())],
        [pltpu.VMEM((FAR, DENSE, 128), F32)],
    )(place, piece, back)
    sums = exchange(sums, "row", FAR_GROUPS)
    (chunk,) = call(chunk_body, [vmem()], [((NEAR, 8, 128), F32, vmem())])(sums)
    tiles = exchange(chunk, "row", NEAR_GROUPS)
    (grad_input,) = call(
        final_body, [smem(), vmem(), vmem()], [((FEAT, ROWS), BF, vmem())]
    )(stay(hub_rows), sums, own_grad)
    weight_grad = tiles.reshape(8, 2, 8, 128).transpose(0, 2, 1, 3).reshape(FEAT, 256)
    return (output, grad_input, weight_grad)


def solution(mesh):
    row = "row"
    placed = (
        P("col", row),
        P(row, None),
        P(row, None),
        P(row),
        P(row, None, None),
        P(row, None, None),
        P(row, None),
        P(None, row),
        P(),
        P("col", row),
    )
    return jax.shard_map(
        shards,
        mesh=mesh,
        in_specs=placed,
        out_specs=(P("col", row), P("col", row), P("col", None)),
        check_vma=False,
    )
```

```python
import jax
import jax.numpy as jnp
from jax import lax
from jax.experimental import pallas as pl
from jax.experimental.pallas import tpu as pltpu
from jax.sharding import PartitionSpec as P

BF = jnp.bfloat16
F32 = jnp.float32

FAR = 8
NEAR = 16
COLS = 4
PEERS = FAR * NEAR
FEAT = 64
HALF = FEAT // 2
ROWS = 512
BLK = 128
BLOCKS = ROWS // BLK
PIECE = 64
PIECES = ROWS // PIECE
DENSE = PIECES * HALF
OUT_ROWS = DENSE + 16
NEAR_ROWS = FAR * HALF + 16
BACK_ROWS = NEAR_ROWS
VMEM_BYTES = 30 * 1024 * 1024
ORDER = (1, 5, 4, 2, 8, 13, 14, 9, 0, 15, 11, 3, 6, 7, 10, 12)
FAR_ORDERS = (
    (6, 2, 7, 0, 5, 3, 1, 4),
    (6, 1, 3, 0, 5, 4, 2, 7),
    (0, 7, 6, 2, 1, 5, 3, 4),
    (5, 6, 3, 2, 0, 7, 4, 1),
)
FAR_SLOTS = tuple(tuple(order.index(s) for s in range(FAR)) for order in FAR_ORDERS)
NEAR_IDS = tuple(tuple(f * NEAR + n for n in range(NEAR)) for f in range(FAR))
FAR_IDS = tuple(tuple(f * NEAR + n for f in range(FAR)) for n in range(NEAR))
NEAR_GROUPS = tuple(tuple(ids[n] for n in ORDER) for ids in NEAR_IDS)


def place_of(near):
    return 2 * (near // 8) + near % 2


def slot_of(place, s):
    chosen = jnp.int32(FAR_SLOTS[0][s])
    for other in range(1, len(FAR_SLOTS)):
        chosen = jnp.where(place == other, FAR_SLOTS[other][s], chosen)
    return chosen


FAR_GROUPS = tuple(
    tuple(FAR_IDS[n][f] for f in FAR_ORDERS[place_of(n)]) for n in range(NEAR)
)
SLOT = tuple(ORDER.index(n) for n in range(NEAR))

NT = (((1,), (1,)), ((), ()))
TN = (((0,), (0,)), ((), ()))
NN = (((1,), (0,)), ((), ()))


def dot(left, right, dims=NN):
    return lax.dot_general(left, right, dims, preferred_element_type=F32)


def vmem():
    return pl.BlockSpec(memory_space=pltpu.VMEM)


def smem():
    return pl.BlockSpec(memory_space=pltpu.SMEM)


def away():
    return pl.BlockSpec(memory_space=pl.ANY)


def call(body, ins, outs, scratch=(), flops=1_000_000, size=1_000_000):
    return pl.pallas_call(
        body,
        in_specs=ins,
        out_specs=[spec for _, _, spec in outs],
        out_shape=[
            pltpu.HBM(shape, kind)
            if spec.memory_space is pl.ANY
            else jax.ShapeDtypeStruct(shape, kind)
            for shape, kind, spec in outs
        ],
        scratch_shapes=list(scratch),
        compiler_params=pltpu.CompilerParams(vmem_limit_bytes=VMEM_BYTES),
        cost_estimate=pl.CostEstimate(flops=flops, bytes_accessed=size, transcendentals=0),
    )


def start_all(pairs, sems):
    copies = [pltpu.make_async_copy(src, dst, sems.at[i]) for i, (src, dst) in enumerate(pairs)]
    for copy in copies:
        copy.start()
    return copies


def stay(value):
    return pltpu.with_memory_space_constraint(value, pltpu.HBM)


def pack_body(hubs, feats, wanted, out):
    for k in range(PIECES):
        low = feats[:HALF, k * PIECE : (k + 1) * PIECE]
        high = feats[HALF:, k * PIECE : (k + 1) * PIECE]
        out[k * HALF : (k + 1) * HALF, :] = jnp.concatenate([low, high], axis=1)
    node = lax.broadcasted_iota(jnp.int32, (8, ROWS), 1)
    which = lax.broadcasted_iota(jnp.int32, (8, ROWS), 0)
    hub = jnp.where(which == 0, hubs[0, 0], hubs[0, 1])
    pick = ((node == hub) & (which < 2)).astype(BF)
    rows = dot(pick, feats[...], NT)
    hub_row = jnp.concatenate([rows[0:1], rows[1:2]], axis=1)
    place = lax.broadcasted_iota(jnp.int32, (16, 128), 0)
    extra = jnp.where(
        place == 0,
        jnp.broadcast_to(wanted[...].astype(F32), (16, 128)),
        jnp.where(place == 1, jnp.broadcast_to(hub_row, (16, 128)), 0.0),
    )
    out[DENSE:, :] = extra.astype(BF)


def pick_body(piece, gathered, out, held, sems):
    place = lax.broadcasted_iota(jnp.int32, (16, 128), 0)
    extra = jnp.zeros((16, 128), F32)
    for s in range(FAR):
        tail = gathered[s, DENSE:, :].astype(F32)
        extra = jnp.where(place == s, jnp.broadcast_to(tail[1:2], (16, 128)), extra)
    extra = extra.astype(BF)
    for n in range(NEAR):
        held[n, FAR * HALF :, :] = extra
    ends = slice(FAR * HALF, NEAR_ROWS)
    copies = [pltpu.make_async_copy(held.at[:, ends, :], out.at[:, ends, :], sems.at[2])]
    copies[0].start()
    rows = FAR * HALF // 2
    halves = [slice(i * rows, (i + 1) * rows) for i in range(2)]
    for i, half in enumerate(halves):
        copies.append(pltpu.make_async_copy(held.at[:, half, :], out.at[:, half, :], sems.at[i]))

    def step(i, carry):
        for s in (4 * i + k for k in range(4)):
            to = pl.multiple_of(s * HALF, HALF)
            for n in range(NEAR):
                start = pl.multiple_of(piece[s, ORDER[n]] * HALF, HALF)
                held[n, pl.ds(to, HALF), :] = gathered[s, pl.ds(start, HALF), :]
        half = pl.ds(pl.multiple_of(i * rows, rows), rows)
        pltpu.make_async_copy(held.at[:, half, :], out.at[:, half, :], sems.at[i]).start()
        return carry

    lax.fori_loop(0, 2, step, 0)
    for copy in copies:
        copy.wait()


def twice(tile):
    zero = jnp.zeros_like(tile)
    return jnp.concatenate(
        [jnp.concatenate([tile, zero], axis=1), jnp.concatenate([zero, tile], axis=1)], axis=0
    )


def forward_body(
    col,
    target,
    came,
    remote,
    feats,
    adj,
    local_far,
    cot_0,
    cot_1,
    cot_2,
    cot_3,
    out,
    cot,
    local,
    total,
    sems,
):
    pairs = [(local_far, local)]
    for hop, value in enumerate((cot_0, cot_1, cot_2, cot_3)):
        source = lax.rem(col[0] + COLS - hop, COLS)
        pairs.append((value, cot.at[pl.ds(pl.multiple_of(source * FEAT, FEAT), FEAT)]))
    copies = start_all(pairs, sems)
    total[...] = jnp.zeros_like(total)

    def step(i, carry):
        for s in (4 * i + k for k in range(4)):
            start = pl.multiple_of(s * HALF, HALF)
            for first in range(0, NEAR, 8):
                parts = []
                for n in range(first, first + 8):
                    q = s * NEAR + ORDER[n]
                    parts.append(dot(came[n, pl.ds(start, HALF), :], twice(remote[q])))
                for n in range(first, first + 8):
                    total[target[s * NEAR + ORDER[n]]] += parts[n - first]
        return carry

    lax.fori_loop(0, FAR // 4, step, 0)
    for copy in copies:
        copy.wait()
    hub_rows = jnp.concatenate([came[SLOT[n], FAR * HALF :, :][:8] for n in range(NEAR)], axis=0)
    hub_rows = jnp.concatenate([hub_rows[:, :FEAT], hub_rows[:, FEAT:]], axis=0)
    hub = dot(hub_rows, adj[...], TN)
    for b in range(BLOCKS):
        cols = slice(b * BLK, (b + 1) * BLK)
        tiles = jnp.concatenate([total[b, :, :BLK], total[b, :, BLK:]], axis=0)
        own = dot(feats[:, cols], local[b])
        value = (own + tiles + hub[:, cols]).astype(BF)
        for c in range(COLS):
            out[c, :, cols] = value


def middle_body(
    col,
    target,
    agg,
    remote,
    weight,
    local,
    adj,
    cot,
    output,
    back,
    own_grad,
    grad,
    pick,
):
    scale = 0.7978845608028654
    mine = pl.multiple_of(col[0] * FEAT, FEAT)
    for c in range(COLS):
        pre = dot(weight[:, c * FEAT : (c + 1) * FEAT], agg[...], TN)
        square = pre * pre
        bend = jnp.tanh(scale * (pre + 0.044715 * (square * pre)))
        half = 0.5 * (1.0 + bend)
        slope = half + 0.5 * pre * (1.0 - bend * bend) * (
            scale * (1.0 + 3.0 * 0.044715 * square)
        )
        grad[c * FEAT : (c + 1) * FEAT, :] = (
            cot[c * FEAT : (c + 1) * FEAT, :].astype(F32) * slope
        ).astype(BF)

        @pl.when(col[0] == c)
        def _():
            output[...] = (pre * half).astype(BF)

    grad_agg = dot(weight[pl.ds(mine, FEAT), :], grad[...]).astype(BF)
    weight_grad = dot(agg[pl.ds(mine, FEAT), :], grad[...], NT)
    for b in range(BLOCKS):
        cols = slice(b * BLK, (b + 1) * BLK)
        pick[b] = grad_agg[:, cols]
        own_grad[:, cols] = dot(grad_agg[:, cols], local[b], NT)
    pick[BLOCKS] = jnp.zeros((FEAT, BLK), BF)
    hub = dot(adj[...], grad_agg, NT)
    hub = jnp.concatenate([hub[:PEERS], hub[PEERS:]], axis=1)
    for n in range(NEAR):
        m = ORDER[n]
        i, j = n // 2, n % 2
        tile = weight_grad[i * 8 : (i + 1) * 8, j * 128 : (j + 1) * 128]
        back[n, FAR * HALF :, :] = jnp.concatenate([hub[m * 8 : (m + 1) * 8], tile], axis=0).astype(BF)

    for s in range(FAR):
        for n in range(NEAR):
            q = s * NEAR + ORDER[n]
            tile = dot(pick[target[q]], remote[q], NT)
            tile = jnp.concatenate([tile[:HALF], tile[HALF:]], axis=1)
            back[n, s * HALF : (s + 1) * HALF, :] = tile.astype(BF)


def gather_body(place, piece, came, out, total):
    slot = [slot_of(place[0], s) for s in range(FAR)]
    total[...] = jnp.zeros_like(total)
    extra = jnp.zeros((16, 128), F32)
    for n in range(NEAR):
        extra += came[n, FAR * HALF :, :].astype(F32)
    for s in range(FAR):
        hub = jnp.broadcast_to(extra[s : s + 1], (8, 128))
        out[slot[s], DENSE:, :] = jnp.concatenate([hub, extra[8:]], axis=0).astype(BF)

    for s in range(FAR):
        for n in range(NEAR):
            at = pl.multiple_of(piece[s, ORDER[n]] * HALF, HALF)
            total[s, pl.ds(at, HALF), :] += came[n, s * HALF : (s + 1) * HALF, :].astype(F32)
        out[slot[s], :DENSE, :] = total[s].astype(BF)


def chunk_body(came, chunk):
    tail = came[0, DENSE:, :].astype(F32)
    for s in range(1, FAR):
        tail += came[s, DENSE:, :].astype(F32)
    for n in range(NEAR):
        chunk[n] = tail[8:]


def final_body(hubs, came, own_grad, out):
    total = came[0].astype(F32)
    for s in range(1, FAR):
        total += came[s].astype(F32)
    node = lax.broadcasted_iota(jnp.int32, (8, ROWS), 1)
    which = lax.broadcasted_iota(jnp.int32, (8, ROWS), 0)
    hub = jnp.where(which == 0, hubs[0, 0], hubs[0, 1])
    pick = ((node == hub) & (which < 2)).astype(F32)
    row = total[DENSE : DENSE + 8]
    place = lax.broadcasted_iota(jnp.int32, (8, FEAT), 0)
    values = jnp.where(place == 0, row[:, :FEAT], row[:, FEAT:])
    hub_grad = lax.dot_general(
        values, pick, TN, preferred_element_type=F32, precision=lax.Precision.HIGHEST
    )
    for k in range(0, PIECES, 2):
        cols = slice(k * PIECE, (k + 2) * PIECE)
        a, b = total[k * HALF : (k + 1) * HALF], total[(k + 1) * HALF : (k + 2) * HALF]
        low = jnp.concatenate([a[:, :PIECE], b[:, :PIECE]], axis=1)
        high = jnp.concatenate([a[:, PIECE:], b[:, PIECE:]], axis=1)
        tiles = jnp.concatenate([low, high], axis=0)
        out[:, cols] = (own_grad[:, cols] + tiles + hub_grad[:, cols]).astype(BF)


def exchange(values, axis, groups=None):
    return lax.all_to_all(
        values,
        axis,
        split_axis=0,
        concat_axis=0,
        tiled=True,
        axis_index_groups=groups,
    )


def shards(
    features,
    send_pieces,
    remote_target,
    remote_count,
    local_values,
    remote_values,
    hub_rows,
    hub_adjacency,
    weight,
    cotangent,
):
    row = lax.axis_index("row").astype(jnp.int32)
    far, near = row // NEAR, row % NEAR
    place = place_of(near).reshape(1)
    col = lax.axis_index("col").astype(jnp.int32).reshape(1)
    target = jnp.where(
        jnp.arange(PEERS, dtype=jnp.int32) < remote_count[0], remote_target[0], BLOCKS
    )
    adj = (
        hub_adjacency.reshape(FAR, NEAR, 2, ROWS).transpose(2, 1, 0, 3).reshape(2 * PEERS, ROWS)
    )
    (packed,) = call(pack_body, [smem(), vmem(), vmem()], [((OUT_ROWS, 128), BF, vmem())])(
        stay(hub_rows), stay(features), stay(send_pieces)
    )
    gathered = lax.all_gather(packed, "row", axis=0, axis_index_groups=FAR_IDS)
    piece = lax.dynamic_slice(
        gathered[:, DENSE, :], (jnp.int32(0), far * NEAR), (FAR, NEAR)
    ).astype(jnp.int32)
    near_all = (NEAR, NEAR_ROWS, 128)
    (picked,) = call(
        pick_body,
        [smem(), vmem()],
        [(near_all, BF, away())],
        [pltpu.VMEM(near_all, BF), pltpu.SemaphoreType.DMA((3,))],
    )(piece, gathered)
    picked, cotangent = lax.optimization_barrier((picked, cotangent))
    came = exchange(picked, "row", NEAR_GROUPS)
    cots = [cotangent]
    for hop in range(1, COLS):
        turn = [(c, (c + hop) % COLS) for c in range(COLS)]
        cots.append(lax.ppermute(cotangent, "col", turn))
    came, cots, col, place = lax.optimization_barrier((came, cots, col, place))
    wide = (COLS * FEAT, ROWS)
    agg, cot = call(
        forward_body,
        [smem(), smem()] + [vmem()] * 4 + [away()] * 5,
        [((COLS, FEAT, ROWS), BF, vmem()), (wide, BF, vmem())],
        [
            pltpu.VMEM((BLOCKS, BLK, BLK), BF),
            pltpu.VMEM((BLOCKS + 1, HALF, 2 * BLK), F32),
            pltpu.SemaphoreType.DMA((1 + COLS,)),
        ],
    )(col, target, came, remote_values, features, adj, *map(stay, (local_values, *cots)))
    agg = exchange(agg, "col").reshape(wide)
    output, back, own_grad = call(
        middle_body,
        [smem(), smem()] + [vmem()] * 6,
        [((FEAT, ROWS), BF, vmem()), (near_all, BF, vmem()), ((FEAT, ROWS), F32, vmem())],
        [pltpu.VMEM(wide, BF), pltpu.VMEM((BLOCKS + 1, FEAT, BLK), BF)],
    )(col, target, agg, remote_values, weight, local_values, adj, cot)
    back = exchange(back, "row", NEAR_GROUPS)
    far_all = (FAR, BACK_ROWS, 128)
    (sums,) = call(
        gather_body,
        [smem(), smem(), vmem()],
        [(far_all, BF, vmem())],
        [pltpu.VMEM((FAR, DENSE, 128), F32)],
    )(place, piece, back)
    sums = exchange(sums, "row", FAR_GROUPS)
    (chunk,) = call(chunk_body, [vmem()], [((NEAR, 8, 128), F32, vmem())])(sums)
    tiles = exchange(chunk, "row", NEAR_GROUPS)
    (grad_input,) = call(
        final_body, [smem(), vmem(), vmem()], [((FEAT, ROWS), BF, vmem())]
    )(stay(hub_rows), sums, own_grad)
    weight_grad = tiles.reshape(8, 2, 8, 128).transpose(0, 2, 1, 3).reshape(FEAT, 256)
    return (output, grad_input, weight_grad)


def solution(mesh):
    row = "row"
    placed = (
        P("col", row),
        P(row, None),
        P(row, None),
        P(row),
        P(row, None, None),
        P(row, None, None),
        P(row, None),
        P(None, row),
        P(),
        P("col", row),
    )
    return jax.shard_map(
        shards,
        mesh=mesh,
        in_specs=placed,
        out_specs=(P("col", row), P("col", row), P("col", None)),
        check_vma=False,
    )
```

```python
import jax
import jax.numpy as jnp
from jax import lax
from jax.experimental import pallas as pl
from jax.experimental.pallas import tpu as pltpu
from jax.sharding import PartitionSpec as P

BF = jnp.bfloat16
F32 = jnp.float32

FAR = 8
NEAR = 16
COLS = 4
PEERS = FAR * NEAR
FEAT = 64
HALF = FEAT // 2
ROWS = 512
BLK = 128
BLOCKS = ROWS // BLK
PIECE = 64
PIECES = ROWS // PIECE
DENSE = PIECES * HALF
OUT_ROWS = DENSE + 16
NEAR_ROWS = FAR * HALF + 16
BACK_ROWS = NEAR_ROWS
VMEM_BYTES = 30 * 1024 * 1024
ORDER = (1, 5, 4, 2, 8, 13, 14, 9, 0, 15, 11, 3, 6, 7, 10, 12)
FAR_ORDERS = (
    (6, 2, 7, 0, 5, 3, 1, 4),
    (6, 1, 3, 0, 5, 4, 2, 7),
    (0, 7, 6, 2, 1, 5, 3, 4),
    (5, 6, 3, 2, 0, 7, 4, 1),
)
FAR_SLOTS = tuple(tuple(order.index(s) for s in range(FAR)) for order in FAR_ORDERS)
NEAR_IDS = tuple(tuple(f * NEAR + n for n in range(NEAR)) for f in range(FAR))
FAR_IDS = tuple(tuple(f * NEAR + n for f in range(FAR)) for n in range(NEAR))
NEAR_GROUPS = tuple(tuple(ids[n] for n in ORDER) for ids in NEAR_IDS)


def place_of(near):
    return 2 * (near // 8) + near % 2


def slot_of(place, s):
    chosen = jnp.int32(FAR_SLOTS[0][s])
    for other in range(1, len(FAR_SLOTS)):
        chosen = jnp.where(place == other, FAR_SLOTS[other][s], chosen)
    return chosen


FAR_GROUPS = tuple(
    tuple(FAR_IDS[n][f] for f in FAR_ORDERS[place_of(n)]) for n in range(NEAR)
)
SLOT = tuple(ORDER.index(n) for n in range(NEAR))

NT = (((1,), (1,)), ((), ()))
TN = (((0,), (0,)), ((), ()))
NN = (((1,), (0,)), ((), ()))


def dot(left, right, dims=NN):
    return lax.dot_general(left, right, dims, preferred_element_type=F32)


def vmem():
    return pl.BlockSpec(memory_space=pltpu.VMEM)


def smem():
    return pl.BlockSpec(memory_space=pltpu.SMEM)


def away():
    return pl.BlockSpec(memory_space=pl.ANY)


def call(body, ins, outs, scratch=(), flops=1_000_000, size=1_000_000):
    return pl.pallas_call(
        body,
        in_specs=ins,
        out_specs=[spec for _, _, spec in outs],
        out_shape=[
            pltpu.HBM(shape, kind)
            if spec.memory_space is pl.ANY
            else jax.ShapeDtypeStruct(shape, kind)
            for shape, kind, spec in outs
        ],
        scratch_shapes=list(scratch),
        compiler_params=pltpu.CompilerParams(vmem_limit_bytes=VMEM_BYTES),
        cost_estimate=pl.CostEstimate(flops=flops, bytes_accessed=size, transcendentals=0),
    )


def start_all(pairs, sems):
    copies = [pltpu.make_async_copy(src, dst, sems.at[i]) for i, (src, dst) in enumerate(pairs)]
    for copy in copies:
        copy.start()
    return copies


def stay(value):
    return pltpu.with_memory_space_constraint(value, pltpu.HBM)


def pack_body(hubs, feats, wanted, out):
    for k in range(PIECES):
        low = feats[:HALF, k * PIECE : (k + 1) * PIECE]
        high = feats[HALF:, k * PIECE : (k + 1) * PIECE]
        out[k * HALF : (k + 1) * HALF, :] = jnp.concatenate([low, high], axis=1)
    node = lax.broadcasted_iota(jnp.int32, (8, ROWS), 1)
    which = lax.broadcasted_iota(jnp.int32, (8, ROWS), 0)
    hub = jnp.where(which == 0, hubs[0, 0], hubs[0, 1])
    pick = ((node == hub) & (which < 2)).astype(BF)
    rows = dot(pick, feats[...], NT)
    hub_row = jnp.concatenate([rows[0:1], rows[1:2]], axis=1)
    place = lax.broadcasted_iota(jnp.int32, (16, 128), 0)
    extra = jnp.where(
        place == 0,
        jnp.broadcast_to(wanted[...].astype(F32), (16, 128)),
        jnp.where(place == 1, jnp.broadcast_to(hub_row, (16, 128)), 0.0),
    )
    out[DENSE:, :] = extra.astype(BF)


def pick_body(piece, gathered, out, held, sems):
    place = lax.broadcasted_iota(jnp.int32, (16, 128), 0)
    extra = jnp.zeros((16, 128), F32)
    for s in range(FAR):
        tail = gathered[s, DENSE:, :].astype(F32)
        extra = jnp.where(place == s, jnp.broadcast_to(tail[1:2], (16, 128)), extra)
    extra = extra.astype(BF)
    for n in range(NEAR):
        held[n, FAR * HALF :, :] = extra
    ends = slice(FAR * HALF, NEAR_ROWS)
    copies = [pltpu.make_async_copy(held.at[:, ends, :], out.at[:, ends, :], sems.at[2])]
    copies[0].start()
    rows = FAR * HALF // 2
    halves = [slice(i * rows, (i + 1) * rows) for i in range(2)]
    for i, half in enumerate(halves):
        copies.append(pltpu.make_async_copy(held.at[:, half, :], out.at[:, half, :], sems.at[i]))

    def step(i, carry):
        for s in (4 * i + k for k in range(4)):
            to = pl.multiple_of(s * HALF, HALF)
            for n in range(NEAR):
                start = pl.multiple_of(piece[s, ORDER[n]] * HALF, HALF)
                held[n, pl.ds(to, HALF), :] = gathered[s, pl.ds(start, HALF), :]
        half = pl.ds(pl.multiple_of(i * rows, rows), rows)
        pltpu.make_async_copy(held.at[:, half, :], out.at[:, half, :], sems.at[i]).start()
        return carry

    lax.fori_loop(0, 2, step, 0)
    for copy in copies:
        copy.wait()


def twice(tile):
    zero = jnp.zeros_like(tile)
    return jnp.concatenate(
        [jnp.concatenate([tile, zero], axis=1), jnp.concatenate([zero, tile], axis=1)], axis=0
    )


def forward_body(
    col,
    target,
    came,
    remote,
    feats,
    adj,
    local_far,
    cot_0,
    cot_1,
    cot_2,
    cot_3,
    out,
    cot,
    local,
    total,
    sems,
):
    pairs = [(local_far, local)]
    for hop, value in enumerate((cot_0, cot_1, cot_2, cot_3)):
        source = lax.rem(col[0] + COLS - hop, COLS)
        pairs.append((value, cot.at[pl.ds(pl.multiple_of(source * FEAT, FEAT), FEAT)]))
    copies = start_all(pairs, sems)
    total[...] = jnp.zeros_like(total)

    def step(i, carry):
        for s in (4 * i + k for k in range(4)):
            start = pl.multiple_of(s * HALF, HALF)
            for first in range(0, NEAR, 8):
                parts = []
                for n in range(first, first + 8):
                    q = s * NEAR + ORDER[n]
                    parts.append(dot(came[n, pl.ds(start, HALF), :], twice(remote[q])))
                for n in range(first, first + 8):
                    total[target[s * NEAR + ORDER[n]]] += parts[n - first]
        return carry

    lax.fori_loop(0, FAR // 4, step, 0)
    for copy in copies:
        copy.wait()
    hub_rows = jnp.concatenate([came[SLOT[n], FAR * HALF :, :][:8] for n in range(NEAR)], axis=0)
    hub_rows = jnp.concatenate([hub_rows[:, :FEAT], hub_rows[:, FEAT:]], axis=0)
    hub = dot(hub_rows, adj[...], TN)
    for b in range(BLOCKS):
        cols = slice(b * BLK, (b + 1) * BLK)
        tiles = jnp.concatenate([total[b, :, :BLK], total[b, :, BLK:]], axis=0)
        own = dot(feats[:, cols], local[b])
        value = (own + tiles + hub[:, cols]).astype(BF)
        for c in range(COLS):
            out[c, :, cols] = value


def middle_body(
    col,
    target,
    agg,
    remote,
    weight,
    local,
    adj,
    cot,
    output,
    back,
    own_grad,
    grad,
    pick,
):
    scale = 0.7978845608028654
    mine = pl.multiple_of(col[0] * FEAT, FEAT)
    for c in range(COLS):
        pre = dot(weight[:, c * FEAT : (c + 1) * FEAT], agg[...], TN)
        square = pre * pre
        bend = jnp.tanh(scale * (pre + 0.044715 * (square * pre)))
        half = 0.5 * (1.0 + bend)
        slope = half + 0.5 * pre * (1.0 - bend * bend) * (
            scale * (1.0 + 3.0 * 0.044715 * square)
        )
        grad[c * FEAT : (c + 1) * FEAT, :] = (
            cot[c * FEAT : (c + 1) * FEAT, :].astype(F32) * slope
        ).astype(BF)

        @pl.when(col[0] == c)
        def _():
            output[...] = (pre * half).astype(BF)

    grad_agg = dot(weight[pl.ds(mine, FEAT), :], grad[...]).astype(BF)
    weight_grad = dot(agg[pl.ds(mine, FEAT), :], grad[...], NT)
    for b in range(BLOCKS):
        cols = slice(b * BLK, (b + 1) * BLK)
        pick[b] = grad_agg[:, cols]
        own_grad[:, cols] = dot(grad_agg[:, cols], local[b], NT)
    pick[BLOCKS] = jnp.zeros((FEAT, BLK), BF)
    hub = dot(adj[...], grad_agg, NT)
    hub = jnp.concatenate([hub[:PEERS], hub[PEERS:]], axis=1)
    for n in range(NEAR):
        m = ORDER[n]
        i, j = n // 2, n % 2
        tile = weight_grad[i * 8 : (i + 1) * 8, j * 128 : (j + 1) * 128]
        back[n, FAR * HALF :, :] = jnp.concatenate([hub[m * 8 : (m + 1) * 8], tile], axis=0).astype(BF)

    for s in range(FAR):
        for n in range(NEAR):
            q = s * NEAR + ORDER[n]
            tile = dot(pick[target[q]], remote[q], NT)
            tile = jnp.concatenate([tile[:HALF], tile[HALF:]], axis=1)
            back[n, s * HALF : (s + 1) * HALF, :] = tile.astype(BF)


def gather_body(place, piece, came, out, total):
    slot = [slot_of(place[0], s) for s in range(FAR)]
    total[...] = jnp.zeros_like(total)
    extra = jnp.zeros((16, 128), F32)
    for n in range(NEAR):
        extra += came[n, FAR * HALF :, :].astype(F32)
    for s in range(FAR):
        hub = jnp.broadcast_to(extra[s : s + 1], (8, 128))
        out[slot[s], DENSE:, :] = jnp.concatenate([hub, extra[8:]], axis=0).astype(BF)

    def step(i, carry):
        for k in range(4):
            s = 4 * i + k
            start = pl.multiple_of(s * HALF, HALF)
            for n in range(NEAR):
                at = pl.multiple_of(piece[s, ORDER[n]] * HALF, HALF)
                total[s, pl.ds(at, HALF), :] += came[n, pl.ds(start, HALF), :].astype(F32)
            out[jnp.where(i == 0, slot[k], slot[4 + k]), :DENSE, :] = total[s].astype(BF)
        return carry

    lax.fori_loop(0, FAR // 4, step, 0)


def chunk_body(came, chunk):
    tail = came[0, DENSE:, :].astype(F32)
    for s in range(1, FAR):
        tail += came[s, DENSE:, :].astype(F32)
    for n in range(NEAR):
        chunk[n] = tail[8:]


def final_body(hubs, came, own_grad, out):
    total = came[0].astype(F32)
    for s in range(1, FAR):
        total += came[s].astype(F32)
    node = lax.broadcasted_iota(jnp.int32, (8, ROWS), 1)
    which = lax.broadcasted_iota(jnp.int32, (8, ROWS), 0)
    hub = jnp.where(which == 0, hubs[0, 0], hubs[0, 1])
    pick = ((node == hub) & (which < 2)).astype(F32)
    row = total[DENSE : DENSE + 8]
    place = lax.broadcasted_iota(jnp.int32, (8, FEAT), 0)
    values = jnp.where(place == 0, row[:, :FEAT], row[:, FEAT:])
    hub_grad = lax.dot_general(
        values, pick, TN, preferred_element_type=F32, precision=lax.Precision.HIGHEST
    )
    for k in range(0, PIECES, 2):
        cols = slice(k * PIECE, (k + 2) * PIECE)
        a, b = total[k * HALF : (k + 1) * HALF], total[(k + 1) * HALF : (k + 2) * HALF]
        low = jnp.concatenate([a[:, :PIECE], b[:, :PIECE]], axis=1)
        high = jnp.concatenate([a[:, PIECE:], b[:, PIECE:]], axis=1)
        tiles = jnp.concatenate([low, high], axis=0)
        out[:, cols] = (own_grad[:, cols] + tiles + hub_grad[:, cols]).astype(BF)


def exchange(values, axis, groups=None):
    return lax.all_to_all(
        values,
        axis,
        split_axis=0,
        concat_axis=0,
        tiled=True,
        axis_index_groups=groups,
    )


def shards(
    features,
    send_pieces,
    remote_target,
    remote_count,
    local_values,
    remote_values,
    hub_rows,
    hub_adjacency,
    weight,
    cotangent,
):
    row = lax.axis_index("row").astype(jnp.int32)
    far, near = row // NEAR, row % NEAR
    place = place_of(near).reshape(1)
    col = lax.axis_index("col").astype(jnp.int32).reshape(1)
    target = jnp.where(
        jnp.arange(PEERS, dtype=jnp.int32) < remote_count[0], remote_target[0], BLOCKS
    )
    adj = (
        hub_adjacency.reshape(FAR, NEAR, 2, ROWS).transpose(2, 1, 0, 3).reshape(2 * PEERS, ROWS)
    )
    (packed,) = call(pack_body, [smem(), vmem(), vmem()], [((OUT_ROWS, 128), BF, vmem())])(
        stay(hub_rows), stay(features), stay(send_pieces)
    )
    gathered = lax.all_gather(packed, "row", axis=0, axis_index_groups=FAR_IDS)
    piece = lax.dynamic_slice(
        gathered[:, DENSE, :], (jnp.int32(0), far * NEAR), (FAR, NEAR)
    ).astype(jnp.int32)
    near_all = (NEAR, NEAR_ROWS, 128)
    (picked,) = call(
        pick_body,
        [smem(), vmem()],
        [(near_all, BF, away())],
        [pltpu.VMEM(near_all, BF), pltpu.SemaphoreType.DMA((3,))],
    )(piece, gathered)
    picked, cotangent = lax.optimization_barrier((picked, cotangent))
    came = exchange(picked, "row", NEAR_GROUPS)
    cots = [cotangent]
    for hop in range(1, COLS):
        turn = [(c, (c + hop) % COLS) for c in range(COLS)]
        cots.append(lax.ppermute(cotangent, "col", turn))
    came, cots, col, place = lax.optimization_barrier((came, cots, col, place))
    wide = (COLS * FEAT, ROWS)
    agg, cot = call(
        forward_body,
        [smem(), smem()] + [vmem()] * 4 + [away()] * 5,
        [((COLS, FEAT, ROWS), BF, vmem()), (wide, BF, vmem())],
        [
            pltpu.VMEM((BLOCKS, BLK, BLK), BF),
            pltpu.VMEM((BLOCKS + 1, HALF, 2 * BLK), F32),
            pltpu.SemaphoreType.DMA((1 + COLS,)),
        ],
    )(col, target, came, remote_values, features, adj, *map(stay, (local_values, *cots)))
    agg = exchange(agg, "col").reshape(wide)
    output, back, own_grad = call(
        middle_body,
        [smem(), smem()] + [vmem()] * 6,
        [((FEAT, ROWS), BF, vmem()), (near_all, BF, vmem()), ((FEAT, ROWS), F32, vmem())],
        [pltpu.VMEM(wide, BF), pltpu.VMEM((BLOCKS + 1, FEAT, BLK), BF)],
    )(col, target, agg, remote_values, weight, local_values, adj, cot)
    back = exchange(back, "row", NEAR_GROUPS)
    far_all = (FAR, BACK_ROWS, 128)
    (sums,) = call(
        gather_body,
        [smem(), smem(), vmem()],
        [(far_all, BF, vmem())],
        [pltpu.VMEM((FAR, DENSE, 128), F32)],
    )(place, piece, back)
    sums = exchange(sums, "row", FAR_GROUPS)
    (chunk,) = call(chunk_body, [vmem()], [((NEAR, 8, 128), F32, vmem())])(sums)
    tiles = exchange(chunk, "row", NEAR_GROUPS)
    (grad_input,) = call(
        final_body, [smem(), vmem(), vmem()], [((FEAT, ROWS), BF, vmem())]
    )(stay(hub_rows), sums, own_grad)
    weight_grad = tiles.reshape(8, 2, 8, 128).transpose(0, 2, 1, 3).reshape(FEAT, 256)
    return (output, grad_input, weight_grad)


def solution(mesh):
    row = "row"
    placed = (
        P("col", row),
        P(row, None),
        P(row, None),
        P(row),
        P(row, None, None),
        P(row, None, None),
        P(row, None),
        P(None, row),
        P(),
        P("col", row),
    )
    return jax.shard_map(
        shards,
        mesh=mesh,
        in_specs=placed,
        out_specs=(P("col", row), P("col", row), P("col", None)),
        check_vma=False,
    )
```
